128 devices in a mesh: section: 4 (over y_hi, core), dp: 32 (over z, y_lo, x).
Axes of the slice: x: 4, y: 4 (y_hi: 2, y_lo: 2; y = y_hi * 2 + y_lo), z: 4, core: 2. Of those that a mesh axis runs over, the one named last changes fastest.
Arguments:
- frames_in: bfloat16 [4096, 4, 1024], P('dp', 'section'), may hold values from -6 to 6
- in_weights: bfloat16 [1024, 4, 2, 9728], P('dp', 'section'), may hold values from -0.1875 to 0.1875
- down_weights: bfloat16 [2816, 4, 2, 1024], P('dp', 'section'), may hold values from -0.109375 to 0.109375
- gains: bfloat16 [1024, 4, 2, 2], P(None, 'section'), may hold values from 0.099609375 to 1.8984375
- cotangent: bfloat16 [4096, 4, 1024], P('dp', 'section'), may hold values from -6 to 6
- segment_ids: int32 [4096], P('dp'), may hold values from 0 to 15, as said below
- valid: int32 [4096], P('dp'), may hold values 0 or 1
Outputs:
- output: bfloat16 [4096, 4, 1024], P('dp', 'section')
- input_grad: bfloat16 [4096, 4, 1024], P('dp', 'section')
- in_weights_grad: float32 [1024, 4, 2, 9728], P('dp', 'section')
- down_weights_grad: float32 [2816, 4, 2, 1024], P('dp', 'section')
- gains_grad: float32 [1024, 4, 2, 2], P('dp', 'section')
The draws below stay inside these ranges and needn't reach their ends.
Inputs may be any that keep to these rules, and one draw needn't show every extreme that they name: `segment_ids`: dialogue numbers never fall along the frames, and each of 0 to 15 occurs.
All inputs are finite; a program needn't handle non-finite values. No bound on the sum of `valid` on one device may be relied on, other than what follows from the above.
Results may differ from the reference program's by a relative error of at most 0.02.
Values may be sent and summed in bfloat16 or wider, within the bound.
No kernel may reach another device: no remote copies, remote signals or barrier semaphores. Data moves between devices by JAX's collectives and lax.ppermute only.
A program may use at most 320 MiB of HBM per device.

```python
import math
import jax
import jax.numpy as jnp
from jax import lax

D = 1024
HEADS = 16
HEAD = 64
FF = 2816
LAYERS = 2
NSEG = 16
F_DEV = 128
POS = 4
FRAMES = 4096


def draw_segment_ids(key, part):
    key = jax.random.fold_in(key, 11)
    half_dev = F_DEV // 2
    allowed = jnp.concatenate([jnp.arange(1, half_dev, dtype=jnp.int32), jnp.arange(FRAMES - half_dev, FRAMES, dtype=jnp.int32)])
    shuffled = jax.random.permutation(key, allowed.shape[0])
    starts = allowed[shuffled[:NSEG - 1]]
    boundary = jnp.zeros((FRAMES,), jnp.int32).at[starts].set(1)
    return jnp.cumsum(boundary).astype(jnp.int32)


def place_ends(values, key, least, largest):
    longest = values.shape.index(max(values.shape))
    spots = []
    for shift in (0, 1):
        where = [jax.random.randint(jax.random.fold_in(key, axis), (), 0, length) for axis, length in enumerate(values.shape)]
        where[longest] = (where[longest] + shift) % values.shape[longest]
        spots.append(tuple(where))
    return values.at[spots[0]].set(least).at[spots[1]].set(largest)


def block_scale(rng, extent, split, smallest, top_value):
    gain, own = 1.0, jax.random.fold_in(rng, 6)
    for position, blocks in split:
        steps = jnp.exp(jax.random.uniform(jax.random.fold_in(own, position), (blocks,), jnp.float32, smallest / len(split), top_value / len(split)))
        gain = gain * jnp.repeat(steps, extent[position] // blocks).reshape([-1 if axis == position else 1 for axis in range(len(extent))])
    return gain


def normal_values(stream_key, shape, deviation, reach, cuts=(), held_as=jnp.bfloat16):
    drawn = deviation * jax.random.normal(stream_key, shape, jnp.float32)
    if cuts:
        drawn = drawn * block_scale(stream_key, shape, cuts, -0.22, 0.18)
    return jnp.clip(drawn, -reach, reach).astype(held_as)


def setup_inputs(seed: int = 0) -> dict:
    key_list = jax.random.split(jax.random.key(seed), 8)
    frames_in = normal_values(key_list[0], (FRAMES, POS, D), 1.0, 6.0, ((0, 32), (1, 4)))
    in_weights = normal_values(key_list[1], (D, POS, LAYERS, 4 * D + 2 * FF), D ** -0.5, 0.1875, ((0, 32), (1, 4)))
    down_weights = normal_values(key_list[2], (FF, POS, LAYERS, D), FF ** -0.5, 0.109375, ((0, 32), (1, 4)))
    gains = jnp.clip(1.0 + 0.18 * jax.random.normal(key_list[3], (D, POS, LAYERS, 2), jnp.float32), 0.099609375, 1.8984375).astype(jnp.bfloat16)
    cotangent = normal_values(key_list[4], (FRAMES, POS, D), 1.0, 6.0, ((0, 32), (1, 4)))
    segment_ids = draw_segment_ids(jax.random.fold_in(key_list[7], 71), 0)
    valid = place_ends((jax.random.randint(key_list[6], (FRAMES,), 0, 8) < 7).astype(jnp.int32), jax.random.fold_in(key_list[6], 1), 0, 1)
    return dict(frames_in=frames_in, in_weights=in_weights, down_weights=down_weights, gains=gains, cotangent=cotangent, segment_ids=segment_ids, valid=valid)


EPS = 1e-05
NEG = -1e+30
HIGH = lax.Precision.HIGHEST
COUNT_BOOST = 4.0

@jax.custom_vjp
def low(v):
    return lax.optimization_barrier(v.astype(jnp.bfloat16)).astype(jnp.float32)

@jax.custom_vjp
def low_back(v):
    return v

def low_keep(v):
    return (low(v), None)

def low_pass(kept, grad):
    return (grad,)

def back_keep(v):
    return (v, None)

def back_low(kept, grad):
    return (low(grad),)
low.defvjp(low_keep, low_pass)
low_back.defvjp(back_keep, back_low)

def normalize(state):
    return state * lax.rsqrt(lax.optimization_barrier(jnp.mean(state * state, axis=-1, keepdims=True)) + EPS)

def project(left, weight):
    return jnp.einsum('fpd,dpe->fpe', left, weight, precision=HIGH)

def two_layers(state, in_weights, down_weights, gains):
    rows_here = state.shape[0]
    allowed = jnp.arange(POS)[None, :] <= jnp.arange(POS)[:, None]
    for layer in range(LAYERS):
        weight = in_weights[:, :, layer, :]
        normed = low(normalize(state) * gains[:, :, layer, 0].T[None])
        qkv = project(normed, weight[:, :, :3 * D])
        queries = low(low_back(qkv[:, :, :D])).reshape(rows_here, POS, HEADS, HEAD)
        keys = low(low_back(qkv[:, :, D:2 * D])).reshape(rows_here, POS, HEADS, HEAD)
        values = low(low_back(qkv[:, :, 2 * D:])).reshape(rows_here, POS, HEADS, HEAD)
        scores = jnp.einsum('fphe,fjhe->fhpj', queries, keys, precision=HIGH) / math.sqrt(HEAD)
        scores = jnp.where(allowed[None, None], scores, NEG)
        peak = lax.optimization_barrier(jnp.max(scores, axis=-1, keepdims=True))
        exponent_terms = jnp.exp(scores - peak)
        probs = low(exponent_terms / lax.optimization_barrier(jnp.sum(exponent_terms, axis=-1, keepdims=True)))
        mixed = jnp.einsum('fhpj,fjhe->fphe', probs, values, precision=HIGH).reshape(rows_here, POS, D)
        mixed = low(low_back(mixed))
        middle = state + low_back(project(mixed, weight[:, :, 3 * D:4 * D]))
        branch = low(normalize(middle) * gains[:, :, layer, 1].T[None])
        gate_up = project(branch, weight[:, :, 4 * D:])
        gate = low_back(gate_up[:, :, :FF])
        up_part = low_back(gate_up[:, :, FF:])
        activated = low(jax.nn.silu(gate) * up_part)
        ffn = jnp.einsum('fpk,kpd->fpd', activated, down_weights[:, :, layer, :], precision=HIGH)
        state = middle + low_back(ffn)
    return state

def reference(frames_in, in_weights, down_weights, gains, cotangent, segment_ids, valid):
    onehot = (segment_ids[:, None] == jnp.arange(NSEG, dtype=jnp.int32)[None, :]).astype(jnp.float32)
    valid_f = valid.astype(jnp.float32)
    counts = lax.optimization_barrier(jnp.sum(onehot * valid_f[:, None], axis=0))
    frame_count = lax.optimization_barrier(jnp.sum(onehot * counts[None, :], axis=1))
    weight = valid_f * (1.0 + COUNT_BOOST / jnp.maximum(frame_count, 1.0))
    rows_blk = math.gcd(FRAMES, max(1, 4096 // POS))
    blocks = FRAMES // rows_blk
    state = frames_in.astype(jnp.float32).reshape(blocks, rows_blk, POS, D)
    seed_grad = (cotangent.astype(jnp.float32) * weight[:, None, None]).reshape(blocks, rows_blk, POS, D)

    def forward(state_blocks, win, wdown, gain_all):
        stepper = jax.checkpoint(lambda part_rows: two_layers(part_rows, win, wdown, gain_all))
        return lax.map(stepper, state_blocks)
    result, pullback = jax.vjp(forward, state, in_weights.astype(jnp.float32), down_weights.astype(jnp.float32), gains.astype(jnp.float32))
    grad_state, grad_in, grad_down, grad_gain = pullback(seed_grad)
    output = result.reshape(FRAMES, POS, D).astype(jnp.bfloat16)
    input_grad = grad_state.reshape(FRAMES, POS, D).astype(jnp.bfloat16)
    return (output, input_grad, grad_in, grad_down, grad_gain)
```

```python
import math

import jax
import jax.numpy as jnp
from jax import lax
from jax.experimental import pallas as pl
from jax.experimental.pallas import tpu as pltpu
from jax.sharding import Mesh, PartitionSpec as P

D = 1024
HEAD = 64
FF = 2816
LAYERS = 2
POS = 4
NSEG = 16
EPS = 1e-05
NEG = -1e30
COUNT_BOOST = 4.0

HALF = D // 2
FFH = FF // 2
HEADS_HERE = HALF // HEAD
FRAMES_HERE = 256
LANES = 128

BF = jnp.bfloat16
F32 = jnp.float32

PLANE = ("c", "z", "x")
COLUMN = ("yh", "yl")
FIRST = ("x", "z")
SECOND = ("z", "x")
OFFSETS = (0, -1, 1, 2)


def ring_pairs(axis_of_core, step):
    pairs = []
    for c in range(2):
        for z in range(4):
            for x in range(4):
                if axis_of_core[c] == "x":
                    target = (c * 4 + z) * 4 + (x + step) % 4
                else:
                    target = (c * 4 + (z + step) % 4) * 4 + x
                pairs.append(((c * 4 + z) * 4 + x, target))
    return pairs


def shift(value, axis_of_core, step):
    return lax.ppermute(value, PLANE, ring_pairs(axis_of_core, step))


def gather_ring(piece, axis_of_core):
    half = piece.shape[1] // 2
    left = shift(piece, axis_of_core, 1)
    right = shift(piece, axis_of_core, -1)
    far_a = shift(left[:, :half], axis_of_core, 1)
    far_b = shift(right[:, half:], axis_of_core, -1)
    return jnp.concatenate([piece, left, right, jnp.concatenate([far_a, far_b], axis=1)], axis=0)


def gather_plane(piece):
    return gather_ring(gather_ring(piece, FIRST), SECOND)


def plus(one, two):
    return one.astype(F32) + two.astype(F32)


def scatter_ring(terms, axis_of_core, dtype):
    rows = terms.shape[0] // 4
    half = terms.shape[1] // 2
    own, left, right, far = [terms[k * rows : (k + 1) * rows] for k in range(4)]
    far_a = shift(far[:, :half], axis_of_core, 1)
    far_b = shift(far[:, half:], axis_of_core, -1)
    right = jnp.concatenate([plus(right[:, :half], far_a).astype(BF), right[:, half:]], axis=1)
    left = jnp.concatenate([left[:, :half], plus(left[:, half:], far_b).astype(BF)], axis=1)
    from_left = shift(right, axis_of_core, 1)
    from_right = shift(left, axis_of_core, -1)
    return (plus(own, from_left) + from_right.astype(F32)).astype(dtype)


def scatter_plane(terms):
    return scatter_ring(scatter_ring(terms, SECOND, BF), FIRST, BF)


def to_chip(value, place):
    pairs = [(c * 2 + yl, (yl ^ place) * 2 + c) for c in range(2) for yl in range(2)]
    return lax.ppermute(value, ("c", "yl"), pairs)


def to_owner(value, place):
    pairs = [(c * 2 + yl, yl * 2 + (c ^ place)) for c in range(2) for yl in range(2)]
    return lax.ppermute(value, ("c", "yl"), pairs)


def other_core(value):
    return lax.ppermute(value, "c", [(0, 1), (1, 0)])


def xor_order(blocks, y):
    swapped = jnp.where((y & 1) == 1, blocks[jnp.array([1, 0, 3, 2])], blocks)
    return jnp.where((y & 2) == 2, swapped[jnp.array([2, 3, 0, 1])], swapped)


def pick(flag, one, two):
    return jnp.where(flag, one, two), jnp.where(flag, two, one)


def exchange_column(blocks):
    got = [blocks[0]]
    for k in range(1, POS):
        got.append(lax.ppermute(blocks[k], COLUMN, [(y, y ^ k) for y in range(POS)]))
    return jnp.stack(got)


def matmul(one, two):
    return jnp.dot(one, two, preferred_element_type=F32)


def matmul_nt(one, two):
    return lax.dot_general(one, two, (((1,), (1,)), ((), ())), preferred_element_type=F32)


def matmul_tn(one, two):
    return lax.dot_general(one, two, (((0,), (0,)), ((), ())), preferred_element_type=F32)


def mover(source):
    size = source.shape[0]
    return (lax.broadcasted_iota(jnp.int32, (size, size), 0) == source[None, :]).astype(BF)


def normalize(state):
    return state * lax.rsqrt(jnp.mean(state * state, axis=-1, keepdims=True) + EPS)


def norm_backward(grad_out, state, gain_row):
    scale = lax.rsqrt(jnp.mean(state * state, axis=-1, keepdims=True) + EPS)
    normed = state * scale
    grad_norm = grad_out * gain_row[None]
    grad_state = scale * (grad_norm - normed * jnp.mean(grad_norm * normed, axis=-1, keepdims=True))
    return grad_state, jnp.sum(grad_out * normed, axis=0)


PAIRS = [(p, r) for p in range(POS) for r in range(p + 1)]


def head_matrix(shape, feature_dim):
    feature = lax.broadcasted_iota(jnp.int32, shape, feature_dim) // HEAD
    head = lax.broadcasted_iota(jnp.int32, shape, 1 - feature_dim)
    return (feature == head).astype(F32).astype(BF)


def head_sums(products):
    ones = head_matrix((HALF, LANES), 0)
    high = products.astype(BF)
    low = (products - high.astype(F32)).astype(BF)
    return matmul(high, ones) + matmul(low, ones)


def head_spread(values16):
    return matmul(values16, head_matrix((LANES, HALF), 1))


def pair_probs(queries, keys):
    rows = queries[0].shape[0]
    products = jnp.concatenate([queries[p] * keys[r] for p, r in PAIRS], axis=0)
    scores = head_sums(products) * (1.0 / math.sqrt(HEAD))
    probs = {}
    for p in range(POS):
        own = [scores[i * rows : (i + 1) * rows] for i, pair in enumerate(PAIRS) if pair[0] == p]
        peak = own[0]
        for term in own[1:]:
            peak = jnp.maximum(peak, term)
        terms = [jnp.exp(term - peak) for term in own]
        total = terms[0]
        for term in terms[1:]:
            total = total + term
        for r in range(p + 1):
            probs[p, r] = terms[r] / total
    return probs


def attend_kernel(y_ref, qkv_ref, out_ref):
    y = y_ref[0]
    rows = qkv_ref.shape[1]
    parts = [
        [qkv_ref[p ^ y, :, t * HALF : (t + 1) * HALF].astype(F32) for p in range(POS)]
        for t in range(3)
    ]
    queries, keys, values = parts
    probs = pair_probs(queries, keys)
    spread = head_spread(jnp.concatenate([probs[pair].astype(BF) for pair in PAIRS], axis=0))
    for p in range(POS):
        total = None
        for i, (pp, r) in enumerate(PAIRS):
            if pp == p:
                term = spread[i * rows : (i + 1) * rows] * values[r]
                total = term if total is None else total + term
        out_ref[p ^ y] = total.astype(BF)


def attend_backward_kernel(y_ref, qkv_ref, grad_ref, out_ref):
    y = y_ref[0]
    rows = qkv_ref.shape[1]
    parts = [
        [qkv_ref[p ^ y, :, t * HALF : (t + 1) * HALF].astype(F32) for p in range(POS)]
        for t in range(3)
    ]
    queries, keys, values = parts
    grads = [grad_ref[p ^ y].astype(F32) for p in range(POS)]
    probs = pair_probs(queries, keys)
    products = jnp.concatenate([grads[p] * values[r] for p, r in PAIRS], axis=0)
    grad_probs = head_sums(products)
    grad_probs = {pair: grad_probs[i * rows : (i + 1) * rows] for i, pair in enumerate(PAIRS)}
    grad_scores = []
    for p, r in PAIRS:
        mean = probs[p, 0] * grad_probs[p, 0]
        for other in range(1, p + 1):
            mean = mean + probs[p, other] * grad_probs[p, other]
        grad_scores.append(probs[p, r] * (grad_probs[p, r] - mean) * (1.0 / math.sqrt(HEAD)))
    stacked = jnp.concatenate(grad_scores, axis=0)
    high = stacked.astype(BF)
    low = (stacked - high.astype(F32)).astype(BF)
    spread_scores = head_spread(high) + head_spread(low)
    spread_probs = head_spread(jnp.concatenate([probs[pair].astype(BF) for pair in PAIRS], axis=0))
    grad_q = [None] * POS
    grad_k = [None] * POS
    grad_v = [None] * POS

    def put(totals, place, term):
        totals[place] = term if totals[place] is None else totals[place] + term

    for i, (p, r) in enumerate(PAIRS):
        score = spread_scores[i * rows : (i + 1) * rows]
        put(grad_q, p, score * keys[r])
        put(grad_k, r, score * queries[p])
        put(grad_v, r, spread_probs[i * rows : (i + 1) * rows] * grads[p])
    for p in range(POS):
        for t, totals in enumerate((grad_q, grad_k, grad_v)):
            out_ref[p ^ y, :, t * HALF : (t + 1) * HALF] = totals[p].astype(BF)


VMEM_LIMIT = 48 * 1024 * 1024


def call_kernel(kernel, y, operands, width, flops):
    rows = FRAMES_HERE // POS
    return pl.pallas_call(
        kernel,
        out_shape=jax.ShapeDtypeStruct((POS, rows, width), BF),
        in_specs=[pl.BlockSpec(memory_space=pltpu.SMEM)]
        + [pl.BlockSpec(memory_space=pltpu.VMEM)] * len(operands),
        out_specs=pl.BlockSpec(memory_space=pltpu.VMEM),
        compiler_params=pltpu.CompilerParams(vmem_limit_bytes=VMEM_LIMIT),
        cost_estimate=pl.CostEstimate(flops=flops, bytes_accessed=4 * 2**20, transcendentals=0),
    )(y.reshape(1), *operands)


def body(frames_in, in_weights, down_weights, gains, cotangent, segment_ids, valid):
    core = lax.axis_index("c")
    yl = lax.axis_index("yl")
    y = 2 * lax.axis_index("yh") + yl
    zi = lax.axis_index("z")
    xi = lax.axis_index("x")
    is_first = core == 0
    is_low = yl == 0

    def row_source(block, groups):
        index = jnp.arange(16 * block, dtype=jnp.int32)
        offsets = jnp.array(OFFSETS, dtype=jnp.int32)
        inner = offsets[(index // block) % 4]
        outer = offsets[index // (4 * block)]
        z_step = jnp.where(is_first, outer, inner)
        x_step = jnp.where(is_first, inner, outer)
        return (zi + z_step + 4) % 4, (xi + x_step + 4) % 4, index % block

    z_of, x_of, rest = row_source(64, 2)
    move_model = mover(32 * (8 * z_of + 4 * (core ^ (rest // 32)) + x_of) + rest % 32)
    z_of, x_of, rest = row_source(32, 1)
    move_heads = mover(128 * z_of + 32 * x_of + rest)
    z_of, x_of, rest = row_source(88, 1)
    move_units = mover(352 * z_of + 88 * x_of + rest)

    def frames_to_chip(value):
        one, two = pick(is_first, to_chip(value, 0), to_chip(value, 1))
        return jnp.concatenate([one, two], axis=0)

    def columns_to_chip(value):
        one, two = pick(is_low, value[:, :, 0], value[:, :, 1])
        rows = value.shape[0]
        return jnp.concatenate(
            [to_chip(one.reshape(rows, -1), 0), to_chip(two.reshape(rows, -1), 1)], axis=0
        )

    def columns_to_owner(value, groups, width):
        one = to_owner(value[:32], 0).reshape(32, groups, width)
        two = to_owner(value[32:], 1).reshape(32, groups, width)
        one, two = pick(is_low, one, two)
        return jnp.stack([one, two], axis=2).reshape(32, 2 * groups * width).astype(F32)

    gain_all = to_chip(gains[:, 0].reshape(32, LANES), 0).astype(F32).reshape(D, LAYERS, 2)

    weights = []
    for layer in range(LAYERS):
        shard = in_weights[:, 0, layer]
        qkv_part = columns_to_chip(shard[:, : 3 * D].reshape(32, 12, 2, 128))
        gate_up_part = columns_to_chip(shard[:, 4 * D :].reshape(32, 8, 2, 352))
        out_part = to_chip(shard[:, 3 * D : 4 * D], 0)
        down_part = to_chip(down_weights[:, 0, layer], 0)
        weights.append(
            (
                gather_plane(qkv_part),
                gather_plane(out_part),
                gather_plane(gate_up_part),
                gather_plane(down_part),
            )
        )

    state = frames_to_chip(frames_in[:, 0]).astype(F32)

    onehot = (segment_ids[:, None] == jnp.arange(NSEG, dtype=jnp.int32)[None, :]).astype(F32)
    valid_f = valid.astype(F32)
    counts = jnp.sum(onehot * valid_f[:, None], axis=0)[None]
    for axis, pairs in (
        ("yl", [(0, 1), (1, 0)]),
        ("x", [(0, 1), (1, 0), (2, 3), (3, 2)]),
        ("x", [(0, 3), (3, 0), (1, 2), (2, 1)]),
        ("z", [(0, 1), (1, 0), (2, 3), (3, 2)]),
        ("z", [(0, 3), (3, 0), (1, 2), (2, 1)]),
    ):
        counts = counts + lax.ppermute(counts, axis, pairs)
    own_count = jnp.sum(onehot * counts, axis=1)
    weight = valid_f * (1.0 + COUNT_BOOST / jnp.maximum(own_count, 1.0))
    weight = frames_to_chip(weight[:, None])

    def both_cores(partial):
        mine = partial.astype(BF)
        return plus(mine, other_core(mine))

    saved = []
    for layer in range(LAYERS):
        w_qkv, w_out, w_gate_up, w_down = weights[layer]
        normed = (normalize(state) * gain_all[None, :, layer, 0]).astype(BF)
        normed = matmul(normed, move_model).astype(BF)
        qkv = matmul(normed, w_qkv).astype(BF)
        qkv = exchange_column(xor_order(qkv.reshape(POS, 64, 3 * HALF), y))
        mixed = call_kernel(attend_kernel, y, (qkv,), HALF, 2 * 640 * 512 * 128 * 3)
        mixed = xor_order(exchange_column(mixed), y).reshape(FRAMES_HERE, HALF)
        mixed = matmul(mixed, move_heads).astype(BF)
        middle = state + both_cores(matmul(mixed, w_out))
        branch = (normalize(middle) * gain_all[None, :, layer, 1]).astype(BF)
        branch = matmul(branch, move_model).astype(BF)
        gate_up = matmul(branch, w_gate_up)
        gate = gate_up[:, :FFH]
        up_part = gate_up[:, FFH:]
        activated = (jax.nn.silu(gate) * up_part).astype(BF)
        activated = matmul(activated, move_units).astype(BF)
        saved.append((state, normed, qkv, mixed, middle, branch, gate, up_part, activated))
        state = middle + both_cores(matmul(activated, w_down))

    def frames_to_owner(value):
        value = value.astype(BF)
        return to_owner(jnp.where(is_first, value[:128], value[128:]), 0)[:, None]

    output = frames_to_owner(state)
    grad = frames_to_chip(cotangent[:, 0]).astype(F32) * weight

    in_list = [None] * LAYERS
    down_list = [None] * LAYERS
    gain_list = [None] * LAYERS
    for layer in reversed(range(LAYERS)):
        w_qkv, w_out, w_gate_up, w_down = weights[layer]
        state, normed, qkv, mixed, middle, branch, gate, up_part, activated = saved[layer]
        grad16 = grad.astype(BF)
        grad_down = scatter_plane(matmul_tn(activated, grad16).astype(BF))
        grad_act = matmul_nt(matmul_nt(grad16, w_down).astype(BF), move_units)
        sigma = jax.nn.sigmoid(gate)
        grad_gate = grad_act * up_part * sigma * (1.0 + gate * (1.0 - sigma))
        grad_up = grad_act * gate * sigma
        gate_up16 = jnp.concatenate([grad_gate, grad_up], axis=1).astype(BF)
        grad_gate_up = scatter_plane(matmul_tn(branch, gate_up16).astype(BF))
        grad_branch = both_cores(matmul_nt(matmul_nt(gate_up16, w_gate_up).astype(BF), move_model))
        grad_norm, gain_two = norm_backward(grad_branch, middle, gain_all[:, layer, 1])
        grad_middle = grad + grad_norm
        attn16 = grad_middle.astype(BF)
        grad_out = scatter_plane(matmul_tn(mixed, attn16).astype(BF))
        grad_mixed = matmul_nt(matmul_nt(attn16, w_out).astype(BF), move_heads).astype(BF)
        grad_mixed = exchange_column(xor_order(grad_mixed.reshape(POS, 64, HALF), y))
        grad_qkv = call_kernel(
            attend_backward_kernel, y, (qkv, grad_mixed), 3 * HALF, 2 * 640 * 512 * 128 * 7
        )
        grad_qkv = xor_order(exchange_column(grad_qkv), y).reshape(FRAMES_HERE, 3 * HALF)
        grad_in = scatter_plane(matmul_tn(normed, grad_qkv).astype(BF))
        grad_normed = both_cores(matmul_nt(matmul_nt(grad_qkv, w_qkv).astype(BF), move_model))
        grad_norm, gain_one = norm_backward(grad_normed, state, gain_all[:, layer, 0])
        grad = grad_middle + grad_norm
        in_list[layer] = jnp.concatenate(
            [
                columns_to_owner(grad_in, 12, 128),
                to_owner(grad_out, 0).astype(F32),
                columns_to_owner(grad_gate_up, 8, 352),
            ],
            axis=1,
        )
        down_list[layer] = to_owner(grad_down, 0).astype(F32)
        gain_list[layer] = jnp.stack([gain_one, gain_two], axis=-1)
    in_grads = jnp.stack(in_list, axis=1)[:, None]
    down_grads = jnp.stack(down_list, axis=1)[:, None]
    gain_grads = jnp.stack(gain_list, axis=1).reshape(32, LANES)
    for axis, pairs in (
        ("x", [(0, 1), (1, 0), (2, 3), (3, 2)]),
        ("x", [(0, 3), (3, 0), (1, 2), (2, 1)]),
        ("z", [(0, 1), (1, 0), (2, 3), (3, 2)]),
        ("z", [(0, 3), (3, 0), (1, 2), (2, 1)]),
    ):
        gain_grads = gain_grads + lax.ppermute(gain_grads, axis, pairs)
    gain_grads = gain_grads.reshape(4, 2, 4, LANES)
    gain_grads = lax.dynamic_index_in_dim(gain_grads, zi, 0, keepdims=False)
    gain_grads = lax.dynamic_index_in_dim(gain_grads, core, 0, keepdims=False)
    gain_grads = lax.dynamic_slice_in_dim(gain_grads, xi, 1, 0)
    gains_grad = to_owner(gain_grads, 0).reshape(32, 1, LAYERS, 2)
    return (output, frames_to_owner(grad), in_grads, down_grads, gains_grad)


def solution(mesh):
    parts = Mesh(mesh.devices.reshape(2, 2, 4, 2, 4), ("yh", "c", "z", "yl", "x"))
    dp = ("z", "yl", "x")
    section = ("yh", "c")
    return jax.shard_map(
        body,
        mesh=parts,
        in_specs=(
            P(dp, section, None),
            P(dp, section, None, None),
            P(dp, section, None, None),
            P(None, section, None, None),
            P(dp, section, None),
            P(dp),
            P(dp),
        ),
        out_specs=(
            P(dp, section, None),
            P(dp, section, None),
            P(dp, section, None, None),
            P(dp, section, None, None),
            P(dp, section, None, None),
        ),
        check_vma=False,
    )
```

```python
import math

import jax
import jax.numpy as jnp
import numpy as np
from jax import lax
from jax.experimental import pallas as pl
from jax.experimental.pallas import tpu as pltpu
from jax.sharding import Mesh, PartitionSpec as P

D = 1024
HEAD = 64
LAYERS = 2
POS = 4
NSEG = 16
EPS = 1e-05
COUNT_BOOST = 4.0

HALF = D // 2
UNITS = 1536
TOKENS = 256
ROWS = TOKENS // POS
LANES = 128
TILE = 256

BF = jnp.bfloat16
F32 = jnp.float32

PLANE = ("c", "z", "x")
COLUMN = ("yh", "yl")
FIRST = ("x", "z")
SECOND = ("z", "x")

QKV = 3 * HALF
ATTN = QKV + HALF
GATE_UP = 2 * UNITS
FFN = GATE_UP + D + HALF
ATTN_GAINS = ATTN + LANES
PAIR = 1408


def unit_picks():
    unit = np.arange(768)
    rest = unit - HALF
    source = np.where(
        unit < HALF,
        704 * (unit // 256) + 88 * (unit % 256 // 64) + unit % 64,
        704 * (rest // 128) + 88 * (rest % 128 // 32) + 64 + rest % 32,
    )
    source = np.where((unit >= HALF) & (rest % 32 >= 24), -PAIR, source)
    row = np.arange(PAIR)[:, None]
    return [jnp.asarray(row == (source + 352 * half)[None, :], BF) for half in range(2)]


def ring_pairs(axis_of_core, step):
    pairs = []
    for c in range(2):
        for z in range(4):
            for x in range(4):
                if axis_of_core[c] == "x":
                    target = (c * 4 + z) * 4 + (x + step) % 4
                else:
                    target = (c * 4 + (z + step) % 4) * 4 + x
                pairs.append(((c * 4 + z) * 4 + x, target))
    return pairs


def shift(value, axis_of_core, step):
    return lax.ppermute(value, PLANE, ring_pairs(axis_of_core, step))


def after(value, *others):
    return lax.optimization_barrier((value, others))[0]


class Gather:
    def __init__(self, piece):
        self.piece = piece

    def near(self, axis_of_core, *deps):
        self.piece = after(self.piece, *deps)
        self.left = shift(self.piece, axis_of_core, 1)
        self.right = shift(self.piece, axis_of_core, -1)
        return self.left, self.right

    def far(self, axis_of_core, *deps):
        half = self.piece.shape[1] // 2
        far_a = shift(after(self.left[:, :half], *deps), axis_of_core, 1)
        far_b = shift(after(self.right[:, half:], *deps), axis_of_core, -1)
        self.blocks = [(self.piece,), (self.left,), (self.right,), (far_a, far_b)]
        return far_a, far_b

    def one(self, *deps):
        return self.near(FIRST, *deps)

    def two(self, *deps):
        done = self.far(FIRST, *deps)
        rows, width = self.piece.shape
        half = width // 2
        whole, part = ((0, rows), (0, width)), ((0, rows), (0, half))
        blocks = [(self.piece, whole, 0, 0), (self.left, whole, rows, 0)]
        blocks += [(self.right, whole, 2 * rows, 0)]
        blocks += [(done[0], part, 3 * rows, 0), (done[1], part, 3 * rows, half)]
        self.piece = place_blocks(blocks, (4 * rows, width))
        return done

    def three(self, *deps):
        return self.near(SECOND, *deps)

    def four(self, *deps):
        return self.far(SECOND, *deps)


def plus(one, two):
    return one.astype(F32) + two.astype(F32)


class Scatter:
    def __init__(self, own, left, right, far_a, far_b):
        self.parts = own, left, right, far_a, far_b
        self.parts_half = far_a.shape[1]

    def far(self, axis_of_core, *deps):
        own, left, right, far_a, far_b = self.parts
        half = far_a.shape[1]
        far_a = shift(after(far_a, *deps), axis_of_core, 1)
        far_b = shift(after(far_b, *deps), axis_of_core, -1)
        right = jnp.concatenate([plus(right[:, :half], far_a).astype(BF), right[:, half:]], axis=1)
        left = jnp.concatenate([left[:, :half], plus(left[:, half:], far_b).astype(BF)], axis=1)
        self.parts = own, left, right
        return far_a, far_b

    def near(self, axis_of_core, *deps):
        own, left, right = self.parts
        from_left = shift(after(right, *deps), axis_of_core, 1)
        from_right = shift(after(left, *deps), axis_of_core, -1)
        self.block = (plus(own, from_left) + from_right.astype(F32)).astype(BF)
        return (self.block,)

    def one(self, *deps):
        return self.far(SECOND, *deps)

    def two(self, *deps):
        done = self.near(SECOND, *deps)
        own, left, right, far = [self.block[k * 64 : (k + 1) * 64] for k in range(4)]
        half = self.parts_half
        self.parts = own, left, right, far[:, :half], far[:, half:]
        return done

    def three(self, *deps):
        return self.far(FIRST, *deps)

    def four(self, *deps):
        return self.near(FIRST, *deps)


def to_chip(value, place):
    pairs = [(c * 2 + yl, (yl ^ place) * 2 + c) for c in range(2) for yl in range(2)]
    return lax.ppermute(value, ("c", "yl"), pairs)


def to_owner(value, place):
    pairs = [(c * 2 + yl, yl * 2 + (c ^ place)) for c in range(2) for yl in range(2)]
    return lax.ppermute(value, ("c", "yl"), pairs)


def other_core(value):
    return lax.ppermute(value, "c", [(0, 1), (1, 0)])


def pick(flag, one, two):
    return jnp.where(flag, one, two), jnp.where(flag, two, one)


def exchange_column(blocks):
    got = [blocks[0]]
    for k in range(1, POS):
        got.append(lax.ppermute(blocks[k], COLUMN, [(y, y ^ k) for y in range(POS)]))
    return got


def dot(one, two):
    return jnp.dot(one, two, preferred_element_type=F32)


def dot_nt(one, two):
    return lax.dot_general(one, two, (((1,), (1,)), ((), ())), preferred_element_type=F32)


Y, YL = 16, 17


def identity(size):
    row = lax.broadcasted_iota(jnp.int32, (size, size), 0)
    return (row == lax.broadcasted_iota(jnp.int32, (size, size), 1)).astype(F32).astype(BF)


def row_block(step):
    return pl.ds(pl.multiple_of(step * 32, 32), 32)


def lane_tile(step):
    return pl.ds(pl.multiple_of(step * TILE, TILE), TILE)


def chip_rows(meta, k):
    return pl.ds(pl.multiple_of((meta[Y] ^ k) * ROWS, ROWS), ROWS)


def rsqrt_mean(state):
    return lax.rsqrt(jnp.mean(state * state, axis=-1, keepdims=True) + EPS)


def norm_rows(step, state, gain_ref, out_ref):
    out_ref[row_block(step), :] = (state * rsqrt_mean(state) * gain_ref[...]).astype(BF)


def move_rows(a_s, mv_ref, mvt_ref, moved_s, moved_t_ref):
    for j in range(D // TILE):
        cols = slice(j * TILE, (j + 1) * TILE)
        moved_s[:, cols] = dot(a_s[...], mv_ref[:, cols]).astype(BF)
        moved_t_ref[cols, :] = dot_nt(mvt_ref[cols, :], a_s[...]).astype(BF)


def dot_pieces(left_s, pieces, cols):
    total = None
    for k, piece in enumerate(pieces):
        term = dot(left_s[:, k * TILE : (k + 1) * TILE], piece[:, cols])
        total = term if total is None else total + term
    return total


def qkv_kernel(first, meta, ready, *refs):
    if first:
        x_ref, gain_ref, mv_ref, mvt_ref, *refs = refs
    else:
        x_ref, own_ref, other_ref, gain_ref, mv_ref, mvt_ref, *refs = refs
    pieces, refs = refs[:4], refs[4:]
    h_ref, art_ref, *refs = refs
    outs, (a_s, ar_s, qkv_s) = refs[:4], refs[4:]

    @pl.loop(0, TOKENS // 32)
    def _(step):
        state = x_ref[row_block(step), :].astype(F32)
        if not first:
            state = state + own_ref[row_block(step), :].astype(F32)
            state = state + other_ref[row_block(step), :].astype(F32)
        h_ref[row_block(step), :] = state
        norm_rows(step, state, gain_ref, a_s)

    move_rows(a_s, mv_ref, mvt_ref, ar_s, art_ref)
    ready()

    @pl.loop(0, QKV // TILE)
    def _(step):
        qkv_s[:, lane_tile(step)] = dot_pieces(ar_s, pieces, lane_tile(step)).astype(BF)

    for k in range(POS):
        outs[k][...] = qkv_s[chip_rows(meta, k), :]


PAIRS = [(p, r) for p in range(POS) for r in range(p + 1)]


def head_matrix(shape, feature_dim):
    feature = lax.broadcasted_iota(jnp.int32, shape, feature_dim) // HEAD
    head = lax.broadcasted_iota(jnp.int32, shape, 1 - feature_dim)
    return (feature == head).astype(F32).astype(BF)


def head_sums(products):
    ones = head_matrix((HALF, LANES), 0)
    high = products.astype(BF)
    low = (products - high.astype(F32)).astype(BF)
    return dot(high, ones) + dot(low, ones)


def head_spread(values16):
    return dot(values16, head_matrix((LANES, HALF), 1))


def pair_probs(queries, keys):
    products = jnp.concatenate([queries[p] * keys[r] for p, r in PAIRS], axis=0)
    scores = head_sums(products) * (1.0 / math.sqrt(HEAD))
    probs = {}
    for p in range(POS):
        own = [scores[i * ROWS : (i + 1) * ROWS] for i, pair in enumerate(PAIRS) if pair[0] == p]
        peak = own[0]
        for term in own[1:]:
            peak = jnp.maximum(peak, term)
        terms = [jnp.exp(term - peak) for term in own]
        total = terms[0]
        for term in terms[1:]:
            total = total + term
        for r in range(p + 1):
            probs[p, r] = terms[r] / total
    return probs


def split_qkv(meta, blocks, qkv_s):
    for k in range(POS):
        qkv_s[k] = blocks[k][...]
    return [
        [qkv_s[p ^ meta[Y], :, t * HALF : (t + 1) * HALF].astype(F32) for p in range(POS)]
        for t in range(3)
    ]


def attend_kernel(meta, ready, *refs):
    blocks, outs, (qkv_s, out_s) = refs[:4], refs[4:8], refs[8:]
    queries, keys, values = split_qkv(meta, blocks, qkv_s)
    probs = pair_probs(queries, keys)
    spread = head_spread(jnp.concatenate([probs[pair].astype(BF) for pair in PAIRS], axis=0))
    for p in range(POS):
        total = None
        for i, (pp, r) in enumerate(PAIRS):
            if pp == p:
                term = spread[i * ROWS : (i + 1) * ROWS] * values[r]
                total = term if total is None else total + term
        out_s[p ^ meta[Y]] = total.astype(BF)
    for k in range(POS):
        outs[k][...] = out_s[k]


def attend_backward_kernel(meta, ready, *refs):
    blocks, grad_blocks, outs, (qkv_s, grad_s, out_s) = refs[:4], refs[4:8], refs[8:12], refs[12:]
    queries, keys, values = split_qkv(meta, blocks, qkv_s)
    for k in range(POS):
        grad_s[k] = grad_blocks[k][...]
    grads = [grad_s[p ^ meta[Y]].astype(F32) for p in range(POS)]
    probs = pair_probs(queries, keys)
    products = jnp.concatenate([grads[p] * values[r] for p, r in PAIRS], axis=0)
    grad_probs = head_sums(products)
    grad_probs = {pair: grad_probs[i * ROWS : (i + 1) * ROWS] for i, pair in enumerate(PAIRS)}
    grad_scores = []
    for p, r in PAIRS:
        mean = probs[p, 0] * grad_probs[p, 0]
        for other in range(1, p + 1):
            mean = mean + probs[p, other] * grad_probs[p, other]
        grad_scores.append(probs[p, r] * (grad_probs[p, r] - mean) * (1.0 / math.sqrt(HEAD)))
    stacked = jnp.concatenate(grad_scores, axis=0)
    high = stacked.astype(BF)
    low = (stacked - high.astype(F32)).astype(BF)
    spread_scores = head_spread(high) + head_spread(low)
    spread_probs = head_spread(jnp.concatenate([probs[pair].astype(BF) for pair in PAIRS], axis=0))
    grad_q = [None] * POS
    grad_k = [None] * POS
    grad_v = [None] * POS

    def put(totals, place, term):
        totals[place] = term if totals[place] is None else totals[place] + term

    for i, (p, r) in enumerate(PAIRS):
        score = spread_scores[i * ROWS : (i + 1) * ROWS]
        put(grad_q, p, score * keys[r])
        put(grad_k, r, score * queries[p])
        put(grad_v, r, spread_probs[i * ROWS : (i + 1) * ROWS] * grads[p])
    for p in range(POS):
        for t, totals in enumerate((grad_q, grad_k, grad_v)):
            out_s[p ^ meta[Y], :, t * HALF : (t + 1) * HALF] = totals[p].astype(BF)
    for k in range(POS):
        outs[k][...] = out_s[k]


def unpack_rows(meta, pieces, out_ref, start):
    for k in range(16):
        rows = pl.ds(pl.multiple_of(start + meta[k] * 32, 32), 32)
        piece, row = pieces[k // 4], (k % 4) * 64
        out_ref[rows, :HALF] = piece[row : row + 32, :]
        out_ref[rows, HALF:] = piece[row + 32 : row + 64, :]


def transpose_into(source_s, out_s):
    eye = identity(TILE)
    for j in range(source_s.shape[1] // TILE):
        cols = slice(j * TILE, (j + 1) * TILE)
        out_s[cols, :] = dot_nt(eye, source_s[:, cols]).astype(BF)


def out_kernel(meta, ready, *refs):
    blocks, pieces, refs = refs[:4], refs[4:8], refs[8:]
    ort_ref, wo_ref, partial_ref, o_s, ot_s = refs
    for k in range(POS):
        o_s[chip_rows(meta, k), :] = blocks[k][...]
    transpose_into(o_s, ot_s)
    ready()
    unpack_rows(meta, pieces, wo_ref, 0)
    for k in range(16):
        ort_ref[k * 32 : (k + 1) * 32, :] = ot_s[pl.ds(pl.multiple_of(meta[k] * 32, 32), 32), :]
    for j in range(D // TILE):
        cols = slice(j * TILE, (j + 1) * TILE)
        partial_ref[:, cols] = dot(o_s[...], wo_ref[:, cols]).astype(BF)


def ffn_kernel(counting, meta, ready, *refs):
    h_ref, own_ref, other_ref, gain_ref, mv_ref, mvt_ref, *refs = refs
    pieces, refs = refs[:4], refs[4:]
    m_ref, brt_ref, gate_ref, up_ref, actrt_ref, wd_ref, partial_ref, *refs = refs
    if counting:
        total_ref, *refs = refs
    b_s, br_s, act_s, actt_s = refs

    @pl.loop(0, TOKENS // 32)
    def _(step):
        state = h_ref[row_block(step), :] + own_ref[row_block(step), :].astype(F32)
        state = state + other_ref[row_block(step), :].astype(F32)
        m_ref[row_block(step), :] = state
        norm_rows(step, state, gain_ref, b_s)

    move_rows(b_s, mv_ref, mvt_ref, br_s, brt_ref)
    ready()

    @pl.loop(0, UNITS // TILE)
    def _(step):
        cols = lane_tile(step)
        gate = dot_pieces(br_s, pieces, cols)
        gate_ref[:, cols] = gate
        up = dot_pieces(br_s, pieces, lane_tile(step + UNITS // TILE))
        up_ref[:, cols] = up
        act_s[:, cols] = (gate * jax.nn.sigmoid(gate) * up).astype(BF)

    for k in range(16):
        rows = pl.ds(pl.multiple_of(meta[k] * 64, 64), 64)
        wd_ref[rows, :] = pieces[k // 4][
            (k % 4) * 64 : (k % 4 + 1) * 64, GATE_UP : GATE_UP + D
        ]
    unpack_rows(meta, [piece.at[:, pl.ds(GATE_UP + D, HALF)] for piece in pieces], wd_ref, D)
    if counting:
        total = jnp.zeros((1, LANES), F32)
        for k in range(16):
            rows = slice(D + k * 32, D + (k + 1) * 32)
            total = total + wd_ref[rows, :LANES].astype(F32)[24:25]
        total_ref[...] = total
    transpose_into(act_s, actt_s)
    for k in range(16):
        rows = pl.ds(pl.multiple_of(meta[k] * 64, 64), 64)
        actrt_ref[k * 64 : (k + 1) * 64, :] = actt_s[rows, :]
        rows = pl.ds(pl.multiple_of(D + meta[k] * 32, 32), 32)
        actrt_ref[D + k * 32 : D + (k + 1) * 32, :] = actt_s[rows, :]

    @pl.loop(0, D // TILE)
    def _(step):
        cols = lane_tile(step)
        partial_ref[:, cols] = dot(act_s[...], wd_ref[:, cols]).astype(BF)


def norm_backward(base_ref, own_ref, other_ref, state_ref, gain_ref, put):
    def one_block(step, total):
        rows = row_block(step)
        own = own_ref[rows, :].astype(F32)
        grad = own + other_ref[rows, :].astype(F32)
        state = state_ref[rows, :].astype(F32)
        scale = rsqrt_mean(state)
        normed = state * scale
        grad_norm = grad * gain_ref[...]
        mean = jnp.mean(grad_norm * normed, axis=-1, keepdims=True)
        put(rows, base_ref[rows, :] + scale * (grad_norm - normed * mean))
        return total + jnp.sum((own * normed).reshape(4, 8, D), axis=0)

    total = lax.fori_loop(0, TOKENS // 32, one_block, jnp.zeros((8, D), F32))
    return jnp.sum(total, axis=0, keepdims=True)


def put_piece(refs, k, rows, start, value):
    width = value.shape[1]
    if len(refs) == 1:
        refs[0][slice(k * TILE + rows.start, k * TILE + rows.stop), start : start + width] = value
    elif k < 3:
        refs[k][rows, start : start + width] = value
    else:
        half = refs[3].shape[1]
        if start < half:
            refs[3][rows, start : start + width] = value
        else:
            refs[4][rows, start - half : start - half + width] = value


def put_packed(refs, k, start, step, value):
    for i in range(4):
        row = i * 64 + (step // 2) * 32
        put_piece(
            refs, k, slice(row, row + 32), start + (step % 2) * TILE, value[i * 32 : (i + 1) * 32]
        )


def ffn_backward_kernel(last, meta, ready, *refs):
    if last:
        cot_ref, marks_ref, totals_ref, other_totals_ref, *refs = refs
    else:
        base_ref, own_ref, other_ref, state_ref, gain_ref, *refs = refs
    actrt_ref, brt_ref, gate_ref, up_ref, wd_ref, mv_ref, *refs = refs
    held = 4 if last else 8
    pieces, refs = refs[:held], refs[held:]
    g_ref, *refs = refs
    if not last:
        dgain_ref, *refs = refs
    partial_ref, *refs = refs
    outs, (gf_s, dgu_s, dbr_s) = refs[:-3], refs[-3:]
    pieces, above = pieces[:4], pieces[4:]

    def put(rows, value):
        g_ref[rows, :] = value
        gf_s[rows, :] = value.astype(BF)

    if last:

        @pl.loop(0, TOKENS // 32)
        def _(step):
            rows = row_block(step)
            marks = marks_ref[rows, :].astype(F32)
            totals = totals_ref[...] + other_totals_ref[...]
            place = lax.broadcasted_iota(jnp.int32, (32, LANES), 1).astype(F32)
            count = jnp.sum(jnp.where(place == marks[:, :1], totals, 0.0), axis=1, keepdims=True)
            weight = marks[:, 1:2] * (1.0 + COUNT_BOOST / jnp.maximum(count, 1.0))
            put(rows, cot_ref[rows, :].astype(F32) * weight)

    else:
        dgain_ref[...] = norm_backward(base_ref, own_ref, other_ref, state_ref, gain_ref, put)

    @pl.loop(0, UNITS // TILE)
    def _(step):
        cols = lane_tile(step)
        grad_act = dot_nt(gf_s[...], wd_ref[cols, :])
        gate = gate_ref[:, cols]
        sigma = jax.nn.sigmoid(gate)
        grad_up = grad_act * gate * sigma
        grad_gate = grad_act * up_ref[:, cols] * sigma * (1.0 + gate * (1.0 - sigma))
        dgu_s[:, cols] = grad_gate.astype(BF)
        dgu_s[:, lane_tile(step + UNITS // TILE)] = grad_up.astype(BF)

    everything = slice(0, TILE)
    for k in (3, 1, 2, 0):
        rows = slice(k * TILE, (k + 1) * TILE)
        for j in range(GATE_UP // TILE):
            value = dot(brt_ref[rows, :], dgu_s[:, j * TILE : (j + 1) * TILE]).astype(BF)
            put_piece(outs, k, everything, j * TILE, value)
        for j in range(D // TILE):
            value = dot(actrt_ref[rows, :], gf_s[:, j * TILE : (j + 1) * TILE]).astype(BF)
            put_piece(outs, k, everything, GATE_UP + j * TILE, value)
        tail = slice(D + k * 128, D + (k + 1) * 128)
        for j in range(D // TILE):
            value = dot(actrt_ref[tail, :], gf_s[:, j * TILE : (j + 1) * TILE]).astype(BF)
            put_packed(outs, k, GATE_UP + D, j, value)
    ready()
    for k, sums in enumerate(above):
        for j in range(ATTN // TILE):
            put_piece(outs, k, everything, FFN + j * TILE, sums[:, j * TILE : (j + 1) * TILE])
    for k in range(4):
        dbr_s[:, k * TILE : (k + 1) * TILE] = dot_nt(dgu_s[...], pieces[k][...]).astype(BF)
    for j in range(D // TILE):
        cols = slice(j * TILE, (j + 1) * TILE)
        partial_ref[:, cols] = dot_nt(dbr_s[...], mv_ref[cols, :]).astype(BF)


def out_backward_kernel(meta, ready, *refs):
    base_ref, own_ref, other_ref, state_ref, gain_ref, ort_ref, wo_ref, *refs = refs
    gm_ref, dgain_ref, dwo_ref, *refs = refs
    outs, (ga_s, do_s) = refs[:4], refs[4:]

    def put(rows, value):
        gm_ref[rows, :] = value
        ga_s[rows, :] = value.astype(BF)

    dgain_ref[...] = norm_backward(base_ref, own_ref, other_ref, state_ref, gain_ref, put)
    for j in range(HALF // TILE):
        cols = slice(j * TILE, (j + 1) * TILE)
        do_s[:, cols] = dot_nt(ga_s[...], wo_ref[cols, :]).astype(BF)
    for k in range(POS):
        outs[k][...] = do_s[chip_rows(meta, k), :]
    for k in range(4):
        for j in range(D // TILE):
            cols = slice(j * TILE, (j + 1) * TILE)
            value = dot(ort_ref[k * 128 : (k + 1) * 128, :], ga_s[:, cols]).astype(BF)
            for i in range(4):
                row = k * TILE + i * 64 + (j // 2) * 32
                part = slice((j % 2) * TILE, (j % 2 + 1) * TILE)
                dwo_ref[row : row + 32, part] = value[i * 32 : (i + 1) * 32]


def qkv_backward_kernel(first, meta, ready, *refs):
    blocks, refs = refs[:4], refs[4:]
    art_ref, dwo_ref, mv_ref, *refs = refs
    if first:
        mvt_ref, state_ref, *gain_refs = refs[:5]
        refs = refs[5:]
    pieces, refs = refs[:4], refs[4:]
    partial_ref, *refs = refs
    outs, (dqkv_s, dar_s) = refs[:-2], refs[-2:]
    for k in range(POS):
        dqkv_s[chip_rows(meta, k), :] = blocks[k][...]
    ready()
    for k in range(4):
        dar_s[:, k * TILE : (k + 1) * TILE] = dot_nt(dqkv_s[...], pieces[k][...]).astype(BF)
    for j in range(D // TILE):
        cols = slice(j * TILE, (j + 1) * TILE)
        partial_ref[:, cols] = dot_nt(dar_s[...], mv_ref[cols, :]).astype(BF)
    everything = slice(0, TILE)
    if first:
        def one_block(step, total):
            state = state_ref[row_block(step), :]
            term = partial_ref[row_block(step), :].astype(F32) * state * rsqrt_mean(state)
            return total + jnp.sum(term.reshape(4, 8, D), axis=0)

        total = lax.fori_loop(0, TOKENS // 32, one_block, jnp.zeros((8, D), F32))
        grads = [jnp.sum(total, axis=0, keepdims=True)] + [ref[...] for ref in gain_refs]
        grads = jnp.concatenate(grads + [jnp.zeros((LANES - 4, D), F32)], axis=0).astype(BF)
        for k in range(4):
            value = dot_nt(mvt_ref[k * TILE : (k + 1) * TILE, :], grads).astype(BF)
            put_piece(outs, k, everything, ATTN, value)
    for k in (3, 1, 2, 0):
        rows = slice(k * TILE, (k + 1) * TILE)
        for j in range(QKV // TILE):
            value = dot(art_ref[rows, :], dqkv_s[:, j * TILE : (j + 1) * TILE]).astype(BF)
            put_piece(outs, k, everything, j * TILE, value)
        put_piece(outs, k, everything, QKV, dwo_ref[rows, :])


def last_kernel(meta, ready, *refs):
    base_ref, own_ref, other_ref, state_ref, gain_ref, out_ref = refs

    def put(rows, value):
        out_ref[rows, :] = value.astype(BF)

    norm_backward(base_ref, own_ref, other_ref, state_ref, gain_ref, put)


def pack_attn_kernel(meta, ready, *refs):
    shard, one_ref, two_ref = refs
    low = meta[YL] == 0
    for k in range(QKV // LANES):
        first = shard[:, 2 * k * LANES : (2 * k + 1) * LANES]
        second = shard[:, (2 * k + 1) * LANES : (2 * k + 2) * LANES]
        cols = slice(k * LANES, (k + 1) * LANES)
        one_ref[:, cols] = jnp.where(low, first, second)
        two_ref[:, cols] = jnp.where(low, second, first)
    one_ref[:, QKV:] = shard[:, 3 * D :]


def pack_ffn_kernel(meta, ready, *refs):
    shard, down_ref, *picks = refs[:4]
    one_ref, two_ref = refs[4:]
    low = meta[YL] == 0
    parts = jnp.concatenate([shard[:, k * PAIR : (k + 1) * PAIR] for k in range(4)], axis=0)
    first, second = [dot(parts, pick_ref[...]).astype(BF) for pick_ref in picks]
    for ref, value in (
        (one_ref, jnp.where(low, first, second)),
        (two_ref, jnp.where(low, second, first)),
    ):
        for k in range(4):
            rows = slice(k * 32, (k + 1) * 32)
            start = (k // 2) * UNITS + (k % 2) * HALF
            ref[:, start : start + HALF] = value[rows, :HALF]
            start = (k // 2) * UNITS + D + (k % 2) * TILE
            ref[:, start : start + TILE] = value[rows, HALF:]
    for k in range(3):
        one_ref[:, GATE_UP + k * D : GATE_UP + (k + 1) * D] = down_ref[k * 32 : (k + 1) * 32, :]


def unpack_attn_kernel(meta, ready, *refs):
    one_ref, two_ref, out_ref = refs
    low = meta[YL] == 0
    for k in range(QKV // LANES):
        cols = slice(k * LANES, (k + 1) * LANES)
        first, second = one_ref[:, cols].astype(F32), two_ref[:, cols].astype(F32)
        out_ref[:, 2 * k * LANES : (2 * k + 1) * LANES] = jnp.where(low, first, second)
        out_ref[:, (2 * k + 1) * LANES : (2 * k + 2) * LANES] = jnp.where(low, second, first)
    out_ref[:, 3 * D :] = one_ref[:, QKV : QKV + D].astype(F32)


def unpack_ffn_kernel(meta, ready, *refs):
    one_ref, two_ref, *picks = refs[:4]
    out_ref, down_ref = refs[4:]
    low = meta[YL] == 0
    halves = []
    for ref in (one_ref, two_ref):
        parts = []
        for k in range(4):
            start = (k // 2) * UNITS + (k % 2) * HALF
            main = ref[:, start : start + HALF]
            start = (k // 2) * UNITS + D + (k % 2) * TILE
            parts.append(jnp.concatenate([main, ref[:, start : start + TILE]], axis=1))
        halves.append(jnp.concatenate(parts, axis=0))
    first = jnp.where(low, halves[0], halves[1])
    second = jnp.where(low, halves[1], halves[0])
    total = dot_nt(first, picks[0][...]) + dot_nt(second, picks[1][...])
    for k in range(4):
        out_ref[:, k * PAIR : (k + 1) * PAIR] = total[k * 32 : (k + 1) * 32]
    for k in range(3):
        part = one_ref[:, GATE_UP + k * D : GATE_UP + (k + 1) * D].astype(F32)
        down_ref[k * 32 : (k + 1) * 32, :] = part


RATE = 3.4e6
VMEM_LIMIT = 56 * 1024 * 1024


def run(kernel, meta, operands, outs, scratch, micros, early=()):
    arrays, specs, places, windows = [], [], [], []
    for operand in operands:
        places.append(len(arrays))
        if not isinstance(operand, tuple):
            arrays.append(operand)
            specs.append(pl.BlockSpec(memory_space=pltpu.VMEM))
            continue
        parts, first, (start, end) = operand
        moves, at = [], 0
        for part in parts:
            low, high = max(start, at), min(end, at + part.shape[1])
            if low < high:
                moves.append((len(arrays), low - at, low - start, high - low))
                arrays.append(part)
                specs.append(pl.BlockSpec(memory_space=pl.ANY))
            at += part.shape[1]
        windows.append((len(places) - 1, first, end - start, moves))
    n_in, n_out, n_early = len(arrays), len(outs), len(early)
    n_windows, n_copies = len(windows), sum(len(window[3]) for window in windows)
    arrays += early
    specs += [pl.BlockSpec(memory_space=pl.ANY)] * n_early
    held = [pltpu.VMEM((TILE, width), BF) for _, _, width, _ in windows]

    def whole(meta_ref, *refs):
        ins, rest = refs[:n_in], refs[n_in + n_early :]
        given = [ins[place] if place < n_in else None for place in places]
        if not windows:
            kernel(meta_ref, lambda: None, *given, *rest)
            return
        sems = rest[-1]
        slots = rest[-1 - n_windows : -1]
        copies = []
        for slot, (place, first, _, moves) in zip(slots, windows):
            for index, source, target, width in moves:
                source = ins[index].at[pl.ds(first, TILE), pl.ds(source, width)]
                target = slot.at[:, pl.ds(target, width)]
                copies.append(pltpu.make_async_copy(source, target, sems.at[len(copies)]))
                copies[-1].start()
            given[place] = slot

        def ready():
            for copy in copies:
                copy.wait()

        kernel(meta_ref, ready, *given, *rest[: -1 - n_windows])

    extra = held + [pltpu.SemaphoreType.DMA((n_copies,))] if windows else []
    return pl.pallas_call(
        whole,
        out_shape=[jax.ShapeDtypeStruct(shape, dtype) for shape, dtype in outs],
        in_specs=[pl.BlockSpec(memory_space=pltpu.SMEM)] + specs,
        out_specs=[pl.BlockSpec(memory_space=pltpu.VMEM)] * n_out,
        scratch_shapes=[pltpu.VMEM(shape, BF) for shape in scratch] + extra,
        compiler_params=pltpu.CompilerParams(vmem_limit_bytes=VMEM_LIMIT),
        cost_estimate=pl.CostEstimate(
            flops=int(micros * 2e9), bytes_accessed=int(micros * RATE), transcendentals=0
        ),
    )(meta, *arrays)


def place_blocks(blocks, shape):
    count = len(blocks)

    def kernel(*refs):
        out_ref, sems = refs[count], refs[count + 1]
        copies = []
        for i, (_, (rows, columns), row, column) in enumerate(blocks):
            source = refs[i].at[pl.ds(rows[0], rows[1]), pl.ds(columns[0], columns[1])]
            target = out_ref.at[pl.ds(row, rows[1]), pl.ds(column, columns[1])]
            copies.append(pltpu.make_async_copy(source, target, sems.at[i]))
            copies[-1].start()
        for copy in copies:
            copy.wait()

    return pl.pallas_call(
        kernel,
        out_shape=jax.ShapeDtypeStruct(shape, BF),
        in_specs=[pl.BlockSpec(memory_space=pl.ANY)] * count,
        out_specs=pl.BlockSpec(memory_space=pltpu.VMEM),
        scratch_shapes=[pltpu.SemaphoreType.DMA((count,))],
        compiler_params=pltpu.CompilerParams(vmem_limit_bytes=VMEM_LIMIT),
        cost_estimate=pl.CostEstimate(
            flops=0, bytes_accessed=4 * math.prod(shape), transcendentals=0
        ),
    )(*[block[0] for block in blocks])


def body(frames_in, in_weights, down_weights, gains, cotangent, segment_ids, valid):
    core = lax.axis_index("c")
    yl = lax.axis_index("yl")
    y = 2 * lax.axis_index("yh") + yl
    zi = lax.axis_index("z")
    xi = lax.axis_index("x")
    is_first = core == 0
    is_low = yl == 0

    block = jnp.arange(16, dtype=jnp.int32)

    def offset(k):
        return jnp.where(k == 1, 3, k - k // 2)

    inner, outer = offset(block % 4), offset(block // 4)
    z_of = (zi + jnp.where(is_first, outer, inner)) % 4
    x_of = (xi + jnp.where(is_first, inner, outer)) % 4
    arrived = 4 * z_of + x_of
    chip = jnp.stack([y, yl])

    meta = jnp.concatenate([arrived, chip]).astype(jnp.int32)
    source = 32 * (8 * z_of[:, None] + x_of[:, None])
    source = source + 128 * jnp.stack([core, 1 - core])[None, :]
    source = (source[:, :, None] + jnp.arange(32, dtype=jnp.int32)).reshape(D)
    move = (lax.broadcasted_iota(jnp.int32, (D, D), 0) == source[None, :]).astype(BF)
    move_t = (lax.broadcasted_iota(jnp.int32, (D, D), 1) == source[:, None]).astype(BF)
    picks = unit_picks()

    def frames_to_chip(value):
        one, two = pick(is_first, to_chip(value, 0), to_chip(value, 1))
        return jnp.concatenate([one, two], axis=0)

    def pack_attn(shard):
        return run(
            pack_attn_kernel,
            meta,
            [shard],
            [((32, QKV + D), BF), ((32, QKV), BF)],
            [],
            1.7,
        )

    def attn_blocks(one, two, column):
        one, two = to_chip(one, 0), to_chip(two, 1)
        rows = (0, 32)
        return [
            (one, (rows, (0, ATTN)), 0, column),
            (two, (rows, (0, QKV)), 32, column),
            (one, (rows, (ATTN, HALF)), 32, column + QKV),
        ]

    def pack_ffn(shard, down, marks):
        padding = jnp.zeros((8, D), BF)
        if marks is not None:
            padding = lax.dynamic_update_slice(padding, marks[None], (0, 0))
        down = jnp.concatenate([down, padding], axis=0)
        return run(
            pack_ffn_kernel,
            meta,
            [shard, down, *picks],
            [((32, GATE_UP + 3 * D), BF), ((32, GATE_UP), BF)],
            [],
            4.5,
        )

    def ffn_blocks(one, two):
        one, two = to_chip(one, 0), to_chip(two, 1)
        rows, down, tail = (0, 32), GATE_UP + D, GATE_UP + 2 * D
        return [
            (one, (rows, (0, down)), 0, 0),
            (one, (rows, (tail, HALF)), 0, down),
            (two, (rows, (0, GATE_UP)), 32, 0),
            (one, (rows, (down, D)), 32, GATE_UP),
            (one, (rows, (tail + HALF, HALF)), 32, down),
        ]

    def attn_to_owner(block, column, extra):
        low, high = (0, 32), (32, 32)
        one = [(block, (low, (column, ATTN)), 0, 0), (block, (high, (column + QKV, HALF)), 0, ATTN)]
        two = [(block, (high, (column, QKV)), 0, 0)]
        if extra:
            columns = (column + ATTN, extra)
            one.append((block, (low, columns), 0, ATTN + HALF))
            two.append((block, (high, columns), 0, QKV))
        one = to_owner(place_blocks(one, (32, ATTN + HALF + extra)), 0)
        two = to_owner(place_blocks(two, (32, QKV + extra)), 1)
        sums = plus(one[:, ATTN + HALF :], two[:, QKV:])[:, :4] if extra else None
        return run(unpack_attn_kernel, meta, [one, two], [((32, 4 * D), F32)], [], 1.8)[0], sums

    def ffn_to_owner(block):
        low, high, down = (0, 32), (32, 32), GATE_UP + D
        one = [
            (block, (low, (0, down)), 0, 0),
            (block, (high, (GATE_UP, D)), 0, down),
            (block, (low, (down, HALF)), 0, down + D),
            (block, (high, (down, HALF)), 0, down + D + HALF),
        ]
        one = to_owner(place_blocks(one, (32, GATE_UP + 3 * D)), 0)
        two = to_owner(place_blocks([(block, (high, (0, GATE_UP)), 0, 0)], (32, GATE_UP)), 1)
        units, down = run(
            unpack_ffn_kernel,
            meta,
            [one, two, *picks],
            [((32, 4 * PAIR), F32), ((96, D), F32)],
            [],
            4.5,
        )
        return units, down[:88]

    gain_rows = gains[:, 0].transpose(1, 2, 0).reshape(4, D)

    def gain_row(layer, which):
        place = 2 * layer + which
        return gain_all[place : place + 1]

    onehot = segment_ids[:, None] == jnp.arange(LANES, dtype=jnp.int32)[None, :]
    counts = jnp.sum(jnp.where(onehot, valid.astype(F32)[:, None], 0.0), axis=0).astype(BF)
    marks = jnp.stack([segment_ids, valid], axis=1).astype(BF)
    marked = jnp.concatenate([frames_in[:, 0], jnp.pad(marks, ((0, 0), (0, LANES - 2)))], axis=1)

    attn0 = pack_attn(in_weights[:, 0, 0, : 4 * D])
    attn0 = Gather(place_blocks(attn_blocks(*attn0, 0), (64, ATTN)))
    attn0.one()
    later = after(in_weights, attn0.piece)
    ffn0_parts = pack_ffn(later[:, 0, 0, 4 * D :], down_weights[:, 0, 0], None)
    attn0.two(*ffn0_parts)
    attn1_parts = pack_attn(after(later, *ffn0_parts)[:, 0, 1, : 4 * D])
    attn0_three = attn0.three()
    blocks = ffn_blocks(*ffn0_parts)
    blocks += attn_blocks(*after(tuple(attn1_parts), blocks[0][0]), FFN)
    middle0 = Gather(place_blocks(blocks, (64, FFN + ATTN)))
    later = after(in_weights, *attn1_parts)
    ffn1_parts = pack_ffn(later[:, 0, 1, 4 * D :], down_weights[:, 0, 1], counts)
    blocks = ffn_blocks(*after(tuple(ffn1_parts), blocks[-1][0]))
    ffn1 = Gather(place_blocks(blocks, (64, FFN)))
    marked = frames_to_chip(after(marked, blocks[0][0]))
    state = marked[:, :D]
    marks = marked[:, D:]
    gain_all = to_chip(after(gain_rows, blocks[0][0]), 0).astype(F32)
    attn0_four = attn0.four()
    middle0.one()
    middle0.two()
    ffn1.one()
    ffn1_two = ffn1.two()
    ffn1_joined = ffn1.piece
    middle0_three = middle0.three(attn0_four, ffn1_two)
    ffn1.three(middle0_three)
    ffn1.four()

    def windows(gathered, start, end):
        if isinstance(gathered, list):
            return [(parts, 0, (start, end)) for parts in gathered]
        return [((gathered,), k * TILE, (start, end)) for k in range(4)]

    near = [(0, 1), (1, 0), (2, 3), (3, 2)]
    across = [(0, 3), (3, 0), (1, 2), (2, 1)]

    wide = ((TOKENS, D), F32)
    wide16 = ((TOKENS, D), BF)
    turned = ((D, TOKENS), BF)
    row = ((1, D), F32)
    saved = []
    base = None
    for layer in range(LAYERS):
        first = layer == 0
        attn, at = (attn0.blocks, 0) if first else (middle0.blocks, FFN)
        carried = [state] if first else list(base)
        state, turned_a, *blocks = run(
            lambda *refs, first=first: qkv_kernel(first, *refs),
            meta,
            [*carried, gain_row(layer, 0), move, move_t] + windows(attn, at, at + QKV),
            [wide, turned] + [((ROWS, QKV), BF)] * 4,
            [(TOKENS, D), (TOKENS, D), (TOKENS, QKV)],
            7.7,
        )
        blocks = exchange_column(blocks)
        if not first:
            cot = frames_to_chip(after(cotangent[:, 0], blocks[1]))
        mixed = run(
            attend_kernel,
            meta,
            blocks,
            [((ROWS, HALF), BF)] * 4,
            [(POS, ROWS, QKV), (POS, ROWS, HALF)],
            3.0,
        )
        if first:
            middle0.four()
        mixed = exchange_column(mixed)
        turned_o, w_out, partial = run(
            out_kernel,
            meta,
            mixed + windows(attn, at + QKV, at + ATTN),
            [((HALF, TOKENS), BF), ((HALF, D), BF), wide16],
            [(TOKENS, HALF), (HALF, TOKENS)],
            3.6,
        )
        ffn = (middle0 if first else ffn1).blocks
        middle, turned_b, gate, up_part, turned_act, w_down, down_partial, *totals = run(
            lambda *refs, first=first: ffn_kernel(not first, *refs),
            meta,
            [state, partial, other_core(partial), gain_row(layer, 1), move, move_t]
            + windows(ffn, 0, FFN),
            [wide, turned, ((TOKENS, UNITS), F32), ((TOKENS, UNITS), F32)]
            + [((UNITS, TOKENS), BF), ((UNITS, D), BF), wide16]
            + ([] if first else [((1, LANES), F32)]),
            [(TOKENS, D), (TOKENS, D), (TOKENS, UNITS), (UNITS, TOKENS)],
            15.0,
            (ffn1_joined,) if first else (),
        )
        saved.append(
            (state, turned_a, blocks, turned_o, w_out, middle, turned_b, gate, up_part)
            + (turned_act, w_down, attn, at, ffn)
        )
        base = (middle, down_partial, other_core(down_partial))
    totals = totals[0]
    other_totals = other_core(totals)

    def frames_to_owner(value):
        return to_owner(jnp.where(is_first, value[:128], value[128:]), 0)[:, None]

    output = frames_to_owner((base[0] + plus(base[1], base[2])).astype(BF))

    gain_list = [[None, None] for _ in range(LAYERS)]

    down_list = [None] * LAYERS

    def gradient_blocks(width):
        half = width // TILE // 2 * TILE
        return [((TILE, width), BF)] * 3 + [((TILE, half), BF), ((TILE, width - half), BF)]

    for layer in reversed(range(LAYERS)):
        (state, turned_a, blocks, turned_o, w_out, middle, turned_b, gate, up_part) = saved[layer][:9]
        turned_act, w_down, attn, at, ffn = saved[layer][9:]
        last = layer == LAYERS - 1
        carried = [cot, marks, totals, other_totals] if last else list(base)
        results = run(
            lambda *refs, last=last: ffn_backward_kernel(last, *refs),
            meta,
            [*carried, turned_act, turned_b, gate, up_part, w_down, move]
            + windows(ffn, 0, GATE_UP)
            + ([] if last else windows(attn_above, 0, ATTN)),
            [wide]
            + ([] if last else [row])
            + [wide16]
            + gradient_blocks(FFN if last else FFN + ATTN),
            [(TOKENS, D), (TOKENS, GATE_UP), (TOKENS, D)],
            18.0,
            () if last else above_three,
        )
        grad, *results = results
        if not last:
            gain_list[layer + 1][0], *results = results
        partial, *pieces = results
        if last:
            ffn_above = Scatter(*pieces)
            above_one = ffn_above.one()
            above_two = ffn_above.two()
            above_three = ffn_above.three()
            above_four = ffn_above.four()
        else:
            ffn_sum = Scatter(*pieces)
            ffn_one = ffn_sum.one()
        other = other_core(partial)
        grad, gain_list[layer][1], out_terms, *mixed = run(
            out_backward_kernel,
            meta,
            [grad, partial, other, middle, gain_row(layer, 1), turned_o, w_out],
            [wide, row, ((D, HALF), BF)] + [((ROWS, HALF), BF)] * 4,
            [(TOKENS, D), (TOKENS, HALF)],
            5.8,
            () if last else above_four,
        )
        mixed = exchange_column(mixed)
        if not last:
            ffn_two = ffn_sum.two()
        grads = run(
            attend_backward_kernel,
            meta,
            [*blocks, *mixed],
            [((ROWS, QKV), BF)] * 4,
            [(POS, ROWS, QKV), (POS, ROWS, HALF), (POS, ROWS, QKV)],
            3.8,
            above_one if last else ffn_one,
        )
        own = grads[0]
        grads = exchange_column(grads)
        if last:
            grads[0] = after(own, output)
        partial, *pieces = run(
            lambda *refs, first=not last: qkv_backward_kernel(first, *refs),
            meta,
            [*grads, turned_a, out_terms, move]
            + ([] if last else [move_t, state, gain_list[0][1], *gain_list[1]])
            + windows(attn, at, at + QKV),
            [wide16] + ([((D, ATTN), BF)] if last else gradient_blocks(ATTN_GAINS)),
            [(TOKENS, QKV), (TOKENS, D)],
            10.0,
        )
        if last:
            attn_above = pieces[0]
        else:
            attn_sum = Scatter(*pieces)
            attn_sum.one()
        base = (grad, partial, other_core(partial), state, gain_row(layer, 0))
    input_grad = run(last_kernel, meta, list(base), [wide16], [], 4.3, ffn_two)[0]
    ffn_sum.three()
    attn_sum.two(ffn_two)
    ffn_sum.four()
    last_sums = attn_sum.three()
    units_above, down_list[1] = ffn_to_owner(ffn_above.block)
    attn_sum.four()
    both = after(ffn_sum.block, last_sums)
    attn_part, _ = attn_to_owner(both, FFN, 0)
    in_parts = [None, [attn_part, units_above]]
    units, down_list[0] = ffn_to_owner(both)
    attn_part, gain_sums = attn_to_owner(attn_sum.block, 0, LANES)
    in_parts[0] = [attn_part, units]
    in_list = [jnp.concatenate(parts, axis=1) for parts in in_parts]
    in_grads = jnp.stack(in_list, axis=1)[:, None]
    down_grads = jnp.stack(down_list, axis=1)[:, None]

    gains_grad = gain_sums.reshape(32, 1, LAYERS, 2)
    return (output, frames_to_owner(input_grad), in_grads, down_grads, gains_grad)


def solution(mesh):
    parts = Mesh(mesh.devices.reshape(2, 2, 4, 2, 4), ("yh", "c", "z", "yl", "x"))
    dp = ("z", "yl", "x")
    section = ("yh", "c")
    return jax.shard_map(
        body,
        mesh=parts,
        in_specs=(
            P(dp, section, None),
            P(dp, section, None, None),
            P(dp, section, None, None),
            P(None, section, None, None),
            P(dp, section, None),
            P(dp),
            P(dp),
        ),
        out_specs=(
            P(dp, section, None),
            P(dp, section, None),
            P(dp, section, None, None),
            P(dp, section, None, None),
            P(dp, section, None, None),
        ),
        check_vma=False,
    )
```

```python
import math

import jax
import jax.numpy as jnp
import numpy as np
from jax import lax
from jax.experimental import pallas as pl
from jax.experimental.pallas import tpu as pltpu
from jax.sharding import Mesh, PartitionSpec as P

D = 1024
HEAD = 64
LAYERS = 2
POS = 4
NSEG = 16
EPS = 1e-05
COUNT_BOOST = 4.0

HALF = D // 2
UNITS = 1536
TOKENS = 256
ROWS = TOKENS // POS
LANES = 128
TILE = 256

BF = jnp.bfloat16
F32 = jnp.float32

PLANE = ("c", "z", "x")
COLUMN = ("yh", "yl")
FIRST = ("x", "z")
SECOND = ("z", "x")

QKV = 3 * HALF
ATTN = QKV + HALF
GATE_UP = 2 * UNITS
FFN = GATE_UP + D + HALF
ATTN_GAINS = ATTN + LANES
PAIR = 1408


def unit_picks():
    unit = np.arange(768)
    rest = unit - HALF
    source = np.where(
        unit < HALF,
        704 * (unit // 256) + 88 * (unit % 256 // 64) + unit % 64,
        704 * (rest // 128) + 88 * (rest % 128 // 32) + 64 + rest % 32,
    )
    source = np.where((unit >= HALF) & (rest % 32 >= 24), -PAIR, source)
    row = np.arange(PAIR)[:, None]
    return [jnp.asarray(row == (source + 352 * half)[None, :], BF) for half in range(2)]


def ring_pairs(axis_of_core, step):
    pairs = []
    for c in range(2):
        for z in range(4):
            for x in range(4):
                if axis_of_core[c] == "x":
                    target = (c * 4 + z) * 4 + (x + step) % 4
                else:
                    target = (c * 4 + (z + step) % 4) * 4 + x
                pairs.append(((c * 4 + z) * 4 + x, target))
    return pairs


def shift(value, axis_of_core, step):
    return lax.ppermute(value, PLANE, ring_pairs(axis_of_core, step))


def after(value, *others):
    return lax.optimization_barrier((value, others))[0]


class Gather:
    def __init__(self, piece):
        self.piece = piece

    def near(self, axis_of_core, *deps):
        self.piece = after(self.piece, *deps)
        self.left = shift(self.piece, axis_of_core, 1)
        self.right = shift(self.piece, axis_of_core, -1)
        return self.left, self.right

    def far(self, axis_of_core, *deps):
        half = self.piece.shape[1] // 2
        far_a = shift(after(self.left[:, :half], *deps), axis_of_core, 1)
        far_b = shift(after(self.right[:, half:], *deps), axis_of_core, -1)
        self.blocks = [(self.piece,), (self.left,), (self.right,), (far_a, far_b)]
        return far_a, far_b

    def one(self, *deps):
        return self.near(FIRST, *deps)

    def two(self, *deps):
        done = self.far(FIRST, *deps)
        rows, width = self.piece.shape
        half = width // 2
        whole, part = ((0, rows), (0, width)), ((0, rows), (0, half))
        blocks = [(self.piece, whole, 0, 0), (self.left, whole, rows, 0)]
        blocks += [(self.right, whole, 2 * rows, 0)]
        blocks += [(done[0], part, 3 * rows, 0), (done[1], part, 3 * rows, half)]
        self.piece = place_blocks((blocks, (4 * rows, width)))[0]
        return done

    def three(self, *deps):
        return self.near(SECOND, *deps)

    def four(self, *deps):
        return self.far(SECOND, *deps)


def plus(one, two):
    return one.astype(F32) + two.astype(F32)


class Scatter:
    def __init__(self, own, left, right, far_a, far_b):
        self.parts = own, left, right, far_a, far_b
        self.half = far_a.shape[1]

    def far(self, axis_of_core, deps):
        far_a, far_b = self.parts[3:]
        far_a = shift(after(far_a, *deps), axis_of_core, 1)
        far_b = shift(after(far_b, *deps), axis_of_core, -1)
        self.got = far_a, far_b
        return self.got

    def far_sums(self, deps):
        own, left, right = self.parts[:3]
        far_a, far_b = after(self.got, *deps)
        half = self.half
        right = jnp.concatenate([plus(right[:, :half], far_a).astype(BF), right[:, half:]], axis=1)
        left = jnp.concatenate([left[:, :half], plus(left[:, half:], far_b).astype(BF)], axis=1)
        self.parts = own, left, right
        return left, right

    def near(self, axis_of_core, deps):
        own, left, right = self.parts
        from_left = shift(after(right, *deps), axis_of_core, 1)
        from_right = shift(after(left, *deps), axis_of_core, -1)
        self.got = from_left, from_right
        return self.got

    def near_sums(self, deps):
        from_left, from_right = after(self.got, *deps)
        self.block = (plus(self.parts[0], from_left) + from_right.astype(F32)).astype(BF)
        return self.block

    def one(self, *deps):
        return self.far(SECOND, deps)

    def one_sums(self, *deps):
        return self.far_sums(deps)

    def two(self, *deps):
        return self.near(SECOND, deps)

    def two_sums(self, *deps):
        block = self.near_sums(deps)
        own, left, right, far = [block[k * 64 : (k + 1) * 64] for k in range(4)]
        self.parts = own, left, right, far[:, : self.half], far[:, self.half :]
        return block

    def three(self, *deps):
        return self.far(FIRST, deps)

    def three_sums(self, *deps):
        return self.far_sums(deps)

    def four(self, *deps):
        return self.near(FIRST, deps)

    def four_sums(self, *deps):
        return self.near_sums(deps)


def to_chip(value, place):
    pairs = [(c * 2 + yl, (yl ^ place) * 2 + c) for c in range(2) for yl in range(2)]
    return lax.ppermute(value, ("c", "yl"), pairs)


def to_owner(value, place):
    pairs = [(c * 2 + yl, yl * 2 + (c ^ place)) for c in range(2) for yl in range(2)]
    return lax.ppermute(value, ("c", "yl"), pairs)


def other_core(value):
    return lax.ppermute(value, "c", [(0, 1), (1, 0)])


def pick(flag, one, two):
    return jnp.where(flag, one, two), jnp.where(flag, two, one)


def exchange_column(blocks):
    got = [blocks[0]]
    for k in range(1, POS):
        got.append(lax.ppermute(blocks[k], COLUMN, [(y, y ^ k) for y in range(POS)]))
    return got


def dot(one, two):
    return jnp.dot(one, two, preferred_element_type=F32)


def dot_nt(one, two):
    return lax.dot_general(one, two, (((1,), (1,)), ((), ())), preferred_element_type=F32)


Y, YL = 16, 17


def identity(size):
    row = lax.broadcasted_iota(jnp.int32, (size, size), 0)
    return (row == lax.broadcasted_iota(jnp.int32, (size, size), 1)).astype(F32).astype(BF)


def row_block(step):
    return pl.ds(pl.multiple_of(step * 32, 32), 32)


def lane_tile(step):
    return pl.ds(pl.multiple_of(step * TILE, TILE), TILE)


def chip_rows(meta, k):
    return pl.ds(pl.multiple_of((meta[Y] ^ k) * ROWS, ROWS), ROWS)


def rsqrt_mean(state):
    return lax.rsqrt(jnp.mean(state * state, axis=-1, keepdims=True) + EPS)


def norm_rows(step, state, gain_ref, out_ref):
    out_ref[row_block(step), :] = (state * rsqrt_mean(state) * gain_ref[...]).astype(BF)


def move_rows(a_s, mv_ref, moved_s):
    for j in range(D // TILE):
        cols = slice(j * TILE, (j + 1) * TILE)
        moved_s[:, cols] = dot(a_s[...], mv_ref[:, cols]).astype(BF)


def turn_rows(a_ref, mvt_ref, turned_s):
    for j in range(D // TILE):
        cols = slice(j * TILE, (j + 1) * TILE)
        turned_s[cols, :] = dot_nt(mvt_ref[cols, :], a_ref[...]).astype(BF)


def dot_pieces(left_s, pieces, cols):
    total = None
    for k, piece in enumerate(pieces):
        term = dot(left_s[:, k * TILE : (k + 1) * TILE], piece[:, cols])
        total = term if total is None else total + term
    return total


def qkv_kernel(first, meta, ready, *refs):
    if first:
        x_ref, gain_ref, mv_ref, *refs = refs
    else:
        x_ref, own_ref, other_ref, gain_ref, mv_ref, *refs = refs
    pieces, refs = refs[:4], refs[4:]
    h_ref, a_ref, *refs = refs
    outs, (ar_s, qkv_s) = refs[:4], refs[4:]

    @pl.loop(0, TOKENS // 32)
    def _(step):
        state = x_ref[row_block(step), :].astype(F32)
        if not first:
            state = state + own_ref[row_block(step), :].astype(F32)
            state = state + other_ref[row_block(step), :].astype(F32)
        h_ref[row_block(step), :] = state
        norm_rows(step, state, gain_ref, a_ref)

    move_rows(a_ref, mv_ref, ar_s)
    ready()

    @pl.loop(0, QKV // TILE)
    def _(step):
        qkv_s[:, lane_tile(step)] = dot_pieces(ar_s, pieces, lane_tile(step)).astype(BF)

    for k in range(POS):
        outs[k][...] = qkv_s[chip_rows(meta, k), :]


PAIRS = [(p, r) for p in range(POS) for r in range(p + 1)]


def head_matrix(shape, feature_dim):
    feature = lax.broadcasted_iota(jnp.int32, shape, feature_dim) // HEAD
    head = lax.broadcasted_iota(jnp.int32, shape, 1 - feature_dim)
    return (feature == head).astype(F32).astype(BF)


def head_sums(products):
    ones = head_matrix((HALF, LANES), 0)
    high = products.astype(BF)
    low = (products - high.astype(F32)).astype(BF)
    return dot(high, ones) + dot(low, ones)


def head_spread(values16):
    return dot(values16, head_matrix((LANES, HALF), 1))


def pair_probs(queries, keys):
    products = jnp.concatenate([queries[p] * keys[r] for p, r in PAIRS], axis=0)
    scores = head_sums(products) * (1.0 / math.sqrt(HEAD))
    probs = {}
    for p in range(POS):
        own = [scores[i * ROWS : (i + 1) * ROWS] for i, pair in enumerate(PAIRS) if pair[0] == p]
        peak = own[0]
        for term in own[1:]:
            peak = jnp.maximum(peak, term)
        terms = [jnp.exp(term - peak) for term in own]
        total = terms[0]
        for term in terms[1:]:
            total = total + term
        for r in range(p + 1):
            probs[p, r] = terms[r] / total
    return probs


def split_qkv(meta, blocks, qkv_s):
    for k in range(POS):
        qkv_s[k] = blocks[k][...]
    return [
        [qkv_s[p ^ meta[Y], :, t * HALF : (t + 1) * HALF].astype(F32) for p in range(POS)]
        for t in range(3)
    ]


def attend_kernel(meta, ready, *refs):
    blocks, outs, (qkv_s, out_s) = refs[:4], refs[4:8], refs[8:]
    queries, keys, values = split_qkv(meta, blocks, qkv_s)
    probs = pair_probs(queries, keys)
    spread = head_spread(jnp.concatenate([probs[pair].astype(BF) for pair in PAIRS], axis=0))
    for p in range(POS):
        total = None
        for i, (pp, r) in enumerate(PAIRS):
            if pp == p:
                term = spread[i * ROWS : (i + 1) * ROWS] * values[r]
                total = term if total is None else total + term
        out_s[p ^ meta[Y]] = total.astype(BF)
    for k in range(POS):
        outs[k][...] = out_s[k]


def attend_backward_kernel(meta, ready, *refs):
    blocks, grad_blocks, outs, (qkv_s, grad_s, out_s) = refs[:4], refs[4:8], refs[8:12], refs[12:]
    queries, keys, values = split_qkv(meta, blocks, qkv_s)
    for k in range(POS):
        grad_s[k] = grad_blocks[k][...]
    grads = [grad_s[p ^ meta[Y]].astype(F32) for p in range(POS)]
    probs = pair_probs(queries, keys)
    products = jnp.concatenate([grads[p] * values[r] for p, r in PAIRS], axis=0)
    grad_probs = head_sums(products)
    grad_probs = {pair: grad_probs[i * ROWS : (i + 1) * ROWS] for i, pair in enumerate(PAIRS)}
    grad_scores = []
    for p, r in PAIRS:
        mean = probs[p, 0] * grad_probs[p, 0]
        for other in range(1, p + 1):
            mean = mean + probs[p, other] * grad_probs[p, other]
        grad_scores.append(probs[p, r] * (grad_probs[p, r] - mean) * (1.0 / math.sqrt(HEAD)))
    stacked = jnp.concatenate(grad_scores, axis=0)
    high = stacked.astype(BF)
    low = (stacked - high.astype(F32)).astype(BF)
    spread_scores = head_spread(high) + head_spread(low)
    spread_probs = head_spread(jnp.concatenate([probs[pair].astype(BF) for pair in PAIRS], axis=0))
    grad_q = [None] * POS
    grad_k = [None] * POS
    grad_v = [None] * POS

    def put(totals, place, term):
        totals[place] = term if totals[place] is None else totals[place] + term

    for i, (p, r) in enumerate(PAIRS):
        score = spread_scores[i * ROWS : (i + 1) * ROWS]
        put(grad_q, p, score * keys[r])
        put(grad_k, r, score * queries[p])
        put(grad_v, r, spread_probs[i * ROWS : (i + 1) * ROWS] * grads[p])
    for p in range(POS):
        for t, totals in enumerate((grad_q, grad_k, grad_v)):
            out_s[p ^ meta[Y], :, t * HALF : (t + 1) * HALF] = totals[p].astype(BF)
    for k in range(POS):
        outs[k][...] = out_s[k]


def unpack_rows(meta, pieces, out_ref, start):
    for k in range(16):
        rows = pl.ds(pl.multiple_of(start + meta[k] * 32, 32), 32)
        piece, row = pieces[k // 4], (k % 4) * 64
        out_ref[rows, :HALF] = piece[row : row + 32, :]
        out_ref[rows, HALF:] = piece[row + 32 : row + 64, :]


def transpose_into(source_s, out_s):
    eye = identity(TILE)
    for j in range(source_s.shape[1] // TILE):
        cols = slice(j * TILE, (j + 1) * TILE)
        out_s[cols, :] = dot_nt(eye, source_s[:, cols]).astype(BF)


def out_kernel(meta, ready, *refs):
    blocks, pieces, refs = refs[:4], refs[4:8], refs[8:]
    o_ref, partial_ref, wo_s = refs
    for k in range(POS):
        o_ref[chip_rows(meta, k), :] = blocks[k][...]
    ready()
    unpack_rows(meta, pieces, wo_s, 0)
    for j in range(D // TILE):
        cols = slice(j * TILE, (j + 1) * TILE)
        partial_ref[:, cols] = dot(o_ref[...], wo_s[:, cols]).astype(BF)


def unpack_down(meta, pieces, wd_s):
    for k in range(16):
        rows = pl.ds(pl.multiple_of(meta[k] * 64, 64), 64)
        wd_s[rows, :] = pieces[k // 4][
            (k % 4) * 64 : (k % 4 + 1) * 64, GATE_UP : GATE_UP + D
        ]
    unpack_rows(meta, [piece.at[:, pl.ds(GATE_UP + D, HALF)] for piece in pieces], wd_s, D)


def ffn_kernel(counting, meta, ready, *refs):
    h_ref, own_ref, other_ref, gain_ref, mv_ref, *refs = refs
    pieces, refs = refs[:4], refs[4:]
    m_ref, b_ref, gate_ref, up_ref, act_ref, partial_ref, *refs = refs
    if counting:
        total_ref, *refs = refs
    br_s, wd_s = refs

    @pl.loop(0, TOKENS // 32)
    def _(step):
        state = h_ref[row_block(step), :] + own_ref[row_block(step), :].astype(F32)
        state = state + other_ref[row_block(step), :].astype(F32)
        m_ref[row_block(step), :] = state
        norm_rows(step, state, gain_ref, b_ref)

    move_rows(b_ref, mv_ref, br_s)
    ready()

    @pl.loop(0, UNITS // TILE)
    def _(step):
        cols = lane_tile(step)
        gate = dot_pieces(br_s, pieces, cols)
        gate_ref[:, cols] = gate
        up = dot_pieces(br_s, pieces, lane_tile(step + UNITS // TILE))
        up_ref[:, cols] = up
        act_ref[:, cols] = (gate * jax.nn.sigmoid(gate) * up).astype(BF)

    unpack_down(meta, pieces, wd_s)
    if counting:
        total = jnp.zeros((1, LANES), F32)
        for k in range(16):
            rows = slice(D + k * 32, D + (k + 1) * 32)
            total = total + wd_s[rows, :LANES].astype(F32)[24:25]
        total_ref[...] = total

    @pl.loop(0, D // TILE)
    def _(step):
        cols = lane_tile(step)
        partial_ref[:, cols] = dot(act_ref[...], wd_s[:, cols]).astype(BF)


def norm_backward(base_ref, own_ref, other_ref, state_ref, gain_ref, put):
    def one_block(step, total):
        rows = row_block(step)
        own = own_ref[rows, :].astype(F32)
        grad = own + other_ref[rows, :].astype(F32)
        state = state_ref[rows, :].astype(F32)
        scale = rsqrt_mean(state)
        normed = state * scale
        grad_norm = grad * gain_ref[...]
        mean = jnp.mean(grad_norm * normed, axis=-1, keepdims=True)
        put(rows, base_ref[rows, :] + scale * (grad_norm - normed * mean))
        return total + jnp.sum((own * normed).reshape(4, 8, D), axis=0)

    total = lax.fori_loop(0, TOKENS // 32, one_block, jnp.zeros((8, D), F32))
    return jnp.sum(total, axis=0, keepdims=True)


def put_piece(refs, k, rows, start, value):
    width = value.shape[1]
    if len(refs) == 1:
        refs[0][slice(k * TILE + rows.start, k * TILE + rows.stop), start : start + width] = value
    elif k < 3:
        refs[k][rows, start : start + width] = value
    else:
        half = refs[3].shape[1]
        if start < half:
            refs[3][rows, start : start + width] = value
        else:
            refs[4][rows, start - half : start - half + width] = value


def put_packed(refs, k, start, step, value):
    for i in range(4):
        row = i * 64 + (step // 2) * 32
        put_piece(
            refs, k, slice(row, row + 32), start + (step % 2) * TILE, value[i * 32 : (i + 1) * 32]
        )


def ffn_backward_kernel(last, meta, ready, *refs):
    if last:
        cot_ref, marks_ref, totals_ref, other_totals_ref, *refs = refs
    else:
        base_ref, own_ref, other_ref, state_ref, gain_ref, *refs = refs
    gate_ref, up_ref, mv_ref, *refs = refs
    pieces, refs = refs[:4], refs[4:]
    g_ref, gf_ref, dgu_ref, partial_ref, *refs = refs
    if not last:
        dgain_ref, *refs = refs
    dbr_s, wd_s = refs

    def put(rows, value):
        g_ref[rows, :] = value
        gf_ref[rows, :] = value.astype(BF)

    if last:

        @pl.loop(0, TOKENS // 32)
        def _(step):
            rows = row_block(step)
            marks = marks_ref[rows, :].astype(F32)
            totals = totals_ref[...] + other_totals_ref[...]
            place = lax.broadcasted_iota(jnp.int32, (32, LANES), 1).astype(F32)
            count = jnp.sum(jnp.where(place == marks[:, :1], totals, 0.0), axis=1, keepdims=True)
            weight = marks[:, 1:2] * (1.0 + COUNT_BOOST / jnp.maximum(count, 1.0))
            put(rows, cot_ref[rows, :].astype(F32) * weight)

    else:
        dgain_ref[...] = norm_backward(base_ref, own_ref, other_ref, state_ref, gain_ref, put)
    ready()
    unpack_down(meta, pieces, wd_s)

    @pl.loop(0, UNITS // TILE)
    def _(step):
        cols = lane_tile(step)
        grad_act = dot_nt(gf_ref[...], wd_s[cols, :])
        gate = gate_ref[:, cols]
        sigma = jax.nn.sigmoid(gate)
        grad_up = grad_act * gate * sigma
        grad_gate = grad_act * up_ref[:, cols] * sigma * (1.0 + gate * (1.0 - sigma))
        dgu_ref[:, cols] = grad_gate.astype(BF)
        dgu_ref[:, lane_tile(step + UNITS // TILE)] = grad_up.astype(BF)

    for k in range(4):
        value = dot_nt(dgu_ref[...], pieces[k][:, :GATE_UP])
        dbr_s[:, k * TILE : (k + 1) * TILE] = value.astype(BF)
    for j in range(D // TILE):
        cols = slice(j * TILE, (j + 1) * TILE)
        partial_ref[:, cols] = dot_nt(dbr_s[...], mv_ref[cols, :]).astype(BF)


def ffn_gradient_kernel(last, meta, ready, *refs):
    b_ref, act_ref, gf_ref, dgu_ref, mvt_ref, *refs = refs
    above, refs = ([], refs) if last else (refs[:4], refs[4:])
    outs, (brt_s, actt_s, actrt_s) = refs[:5], refs[5:]
    turn_rows(b_ref, mvt_ref, brt_s)
    transpose_into(act_ref, actt_s)
    for k in range(16):
        rows = pl.ds(pl.multiple_of(meta[k] * 64, 64), 64)
        actrt_s[k * 64 : (k + 1) * 64, :] = actt_s[rows, :]
        rows = pl.ds(pl.multiple_of(D + meta[k] * 32, 32), 32)
        actrt_s[D + k * 32 : D + (k + 1) * 32, :] = actt_s[rows, :]
    everything = slice(0, TILE)
    for k in (3, 1, 2, 0):
        rows = slice(k * TILE, (k + 1) * TILE)
        for j in range(GATE_UP // TILE):
            value = dot(brt_s[rows, :], dgu_ref[:, j * TILE : (j + 1) * TILE]).astype(BF)
            put_piece(outs, k, everything, j * TILE, value)
        for j in range(D // TILE):
            value = dot(actrt_s[rows, :], gf_ref[:, j * TILE : (j + 1) * TILE]).astype(BF)
            put_piece(outs, k, everything, GATE_UP + j * TILE, value)
        tail = slice(D + k * 128, D + (k + 1) * 128)
        for j in range(D // TILE):
            value = dot(actrt_s[tail, :], gf_ref[:, j * TILE : (j + 1) * TILE]).astype(BF)
            put_packed(outs, k, GATE_UP + D, j, value)
    ready()
    for k, sums in enumerate(above):
        for j in range(ATTN // TILE):
            put_piece(outs, k, everything, FFN + j * TILE, sums[:, j * TILE : (j + 1) * TILE])


def out_backward_kernel(meta, ready, *refs):
    base_ref, own_ref, other_ref, state_ref, gain_ref, *refs = refs
    pieces, refs = refs[:4], refs[4:]
    gm_ref, dgain_ref, ga_ref, *refs = refs
    outs, (do_s, wo_s) = refs[:4], refs[4:]

    def put(rows, value):
        gm_ref[rows, :] = value
        ga_ref[rows, :] = value.astype(BF)

    dgain_ref[...] = norm_backward(base_ref, own_ref, other_ref, state_ref, gain_ref, put)
    ready()
    unpack_rows(meta, pieces, wo_s, 0)
    for j in range(HALF // TILE):
        cols = slice(j * TILE, (j + 1) * TILE)
        do_s[:, cols] = dot_nt(ga_ref[...], wo_s[cols, :]).astype(BF)
    for k in range(POS):
        outs[k][...] = do_s[chip_rows(meta, k), :]


def qkv_backward_kernel(meta, ready, *refs):
    blocks, refs = refs[:4], refs[4:]
    mv_ref, *refs = refs
    pieces, refs = refs[:4], refs[4:]
    partial_ref, dqkv_ref, dar_s = refs
    for k in range(POS):
        dqkv_ref[chip_rows(meta, k), :] = blocks[k][...]
    ready()
    for k in range(4):
        dar_s[:, k * TILE : (k + 1) * TILE] = dot_nt(dqkv_ref[...], pieces[k][...]).astype(BF)
    for j in range(D // TILE):
        cols = slice(j * TILE, (j + 1) * TILE)
        partial_ref[:, cols] = dot_nt(dar_s[...], mv_ref[cols, :]).astype(BF)


def attn_gradient_kernel(first, meta, ready, *refs):
    a_ref, dqkv_ref, o_ref, ga_ref, mvt_ref, *refs = refs
    if first:
        partial_ref, state_ref, *gain_refs = refs[:5]
        refs = refs[5:]
    outs, (art_s, ot_s, ort_s) = refs[:-3], refs[-3:]
    turn_rows(a_ref, mvt_ref, art_s)
    transpose_into(o_ref, ot_s)
    for k in range(16):
        ort_s[k * 32 : (k + 1) * 32, :] = ot_s[pl.ds(pl.multiple_of(meta[k] * 32, 32), 32), :]
    everything = slice(0, TILE)
    if first:
        def one_block(step, total):
            state = state_ref[row_block(step), :]
            term = partial_ref[row_block(step), :].astype(F32) * state * rsqrt_mean(state)
            return total + jnp.sum(term.reshape(4, 8, D), axis=0)

        total = lax.fori_loop(0, TOKENS // 32, one_block, jnp.zeros((8, D), F32))
        grads = [jnp.sum(total, axis=0, keepdims=True)] + [ref[...] for ref in gain_refs]
        grads = jnp.concatenate(grads + [jnp.zeros((LANES - 4, D), F32)], axis=0).astype(BF)
        for k in range(4):
            value = dot_nt(mvt_ref[k * TILE : (k + 1) * TILE, :], grads).astype(BF)
            put_piece(outs, k, everything, ATTN, value)
    for k in (3, 1, 2, 0):
        rows = slice(k * TILE, (k + 1) * TILE)
        for j in range(QKV // TILE):
            value = dot(art_s[rows, :], dqkv_ref[:, j * TILE : (j + 1) * TILE]).astype(BF)
            put_piece(outs, k, everything, j * TILE, value)
        for j in range(D // TILE):
            cols = slice(j * TILE, (j + 1) * TILE)
            value = dot(ort_s[k * 128 : (k + 1) * 128, :], ga_ref[:, cols]).astype(BF)
            put_packed(outs, k, QKV, j, value)


def last_kernel(meta, ready, *refs):
    base_ref, own_ref, other_ref, state_ref, gain_ref, out_ref = refs

    def put(rows, value):
        out_ref[rows, :] = value.astype(BF)

    norm_backward(base_ref, own_ref, other_ref, state_ref, gain_ref, put)


def pack_attn_kernel(meta, ready, *refs):
    shard, one_ref, two_ref = refs
    low = meta[YL] == 0
    for k in range(QKV // LANES):
        first = shard[:, 2 * k * LANES : (2 * k + 1) * LANES]
        second = shard[:, (2 * k + 1) * LANES : (2 * k + 2) * LANES]
        cols = slice(k * LANES, (k + 1) * LANES)
        one_ref[:, cols] = jnp.where(low, first, second)
        two_ref[:, cols] = jnp.where(low, second, first)
    one_ref[:, QKV:] = shard[:, 3 * D :]


def pack_ffn_kernel(meta, ready, *refs):
    shard, down_ref, *picks = refs[:4]
    one_ref, two_ref = refs[4:]
    low = meta[YL] == 0
    parts = jnp.concatenate([shard[:, k * PAIR : (k + 1) * PAIR] for k in range(4)], axis=0)
    first, second = [dot(parts, pick_ref[...]).astype(BF) for pick_ref in picks]
    for ref, value in (
        (one_ref, jnp.where(low, first, second)),
        (two_ref, jnp.where(low, second, first)),
    ):
        for k in range(4):
            rows = slice(k * 32, (k + 1) * 32)
            start = (k // 2) * UNITS + (k % 2) * HALF
            ref[:, start : start + HALF] = value[rows, :HALF]
            start = (k // 2) * UNITS + D + (k % 2) * TILE
            ref[:, start : start + TILE] = value[rows, HALF:]
    for k in range(3):
        one_ref[:, GATE_UP + k * D : GATE_UP + (k + 1) * D] = down_ref[k * 32 : (k + 1) * 32, :]


def unpack_attn_kernel(meta, one_ref, two_ref, out_ref):
    low = meta[YL] == 0
    for k in range(QKV // LANES):
        cols = slice(k * LANES, (k + 1) * LANES)
        first, second = one_ref[:, cols].astype(F32), two_ref[:, cols].astype(F32)
        out_ref[:, 2 * k * LANES : (2 * k + 1) * LANES] = jnp.where(low, first, second)
        out_ref[:, (2 * k + 1) * LANES : (2 * k + 2) * LANES] = jnp.where(low, second, first)
    out_ref[:, 3 * D :] = one_ref[:, QKV : QKV + D].astype(F32)


def unpack_ffn_kernel(meta, one_ref, two_ref, picks, out_ref, down_ref):
    low = meta[YL] == 0
    halves = []
    for ref in (one_ref, two_ref):
        parts = []
        for k in range(4):
            start = (k // 2) * UNITS + (k % 2) * HALF
            main = ref[:, start : start + HALF]
            start = (k // 2) * UNITS + D + (k % 2) * TILE
            parts.append(jnp.concatenate([main, ref[:, start : start + TILE]], axis=1))
        halves.append(jnp.concatenate(parts, axis=0))
    first = jnp.where(low, halves[0], halves[1])
    second = jnp.where(low, halves[1], halves[0])
    total = dot_nt(first, picks[0][...]) + dot_nt(second, picks[1][...])
    for k in range(4):
        out_ref[:, k * PAIR : (k + 1) * PAIR] = total[k * 32 : (k + 1) * 32]
    for k in range(3):
        part = one_ref[:, GATE_UP + k * D : GATE_UP + (k + 1) * D].astype(F32)
        down_ref[k * 32 : (k + 1) * 32, :] = part


RATE = 3.4e6
VMEM_LIMIT = 56 * 1024 * 1024


def run(kernel, meta, operands, outs, scratch, micros, early=()):
    arrays, specs, places, windows = [], [], [], []
    for operand in operands:
        places.append(len(arrays))
        if not isinstance(operand, tuple):
            arrays.append(operand)
            specs.append(pl.BlockSpec(memory_space=pltpu.VMEM))
            continue
        parts, first, (start, end) = operand
        moves, at = [], 0
        for part in parts:
            low, high = max(start, at), min(end, at + part.shape[1])
            if low < high:
                moves.append((len(arrays), low - at, low - start, high - low))
                arrays.append(part)
                specs.append(pl.BlockSpec(memory_space=pl.ANY))
            at += part.shape[1]
        windows.append((len(places) - 1, first, end - start, moves))
    n_in, n_out, n_early = len(arrays), len(outs), len(early)
    n_windows, n_copies = len(windows), sum(len(window[3]) for window in windows)
    arrays += early
    specs += [pl.BlockSpec(memory_space=pl.ANY)] * n_early
    held = [pltpu.VMEM((TILE, width), BF) for _, _, width, _ in windows]

    def whole(meta_ref, *refs):
        ins, rest = refs[:n_in], refs[n_in + n_early :]
        given = [ins[place] if place < n_in else None for place in places]
        if not windows:
            kernel(meta_ref, lambda: None, *given, *rest)
            return
        sems = rest[-1]
        slots = rest[-1 - n_windows : -1]
        copies = []
        for slot, (place, first, _, moves) in zip(slots, windows):
            for index, source, target, width in moves:
                source = ins[index].at[pl.ds(first, TILE), pl.ds(source, width)]
                target = slot.at[:, pl.ds(target, width)]
                copies.append(pltpu.make_async_copy(source, target, sems.at[len(copies)]))
                copies[-1].start()
            given[place] = slot

        def ready():
            for copy in copies:
                copy.wait()

        kernel(meta_ref, ready, *given, *rest[: -1 - n_windows])

    extra = held + [pltpu.SemaphoreType.DMA((n_copies,))] if windows else []
    return pl.pallas_call(
        whole,
        out_shape=[jax.ShapeDtypeStruct(shape, dtype) for shape, dtype in outs],
        in_specs=[pl.BlockSpec(memory_space=pltpu.SMEM)] + specs,
        out_specs=[pl.BlockSpec(memory_space=pltpu.VMEM)] * n_out,
        scratch_shapes=[pltpu.VMEM(shape, BF) for shape in scratch] + extra,
        compiler_params=pltpu.CompilerParams(vmem_limit_bytes=VMEM_LIMIT),
        cost_estimate=pl.CostEstimate(
            flops=int(micros * 2e9), bytes_accessed=int(micros * RATE), transcendentals=0
        ),
    )(meta, *arrays)


def place_blocks(*targets):
    moves = [(i, *block) for i, (blocks, _) in enumerate(targets) for block in blocks]
    count = len(moves)

    def kernel(*refs):
        out_refs, sems = refs[count:-1], refs[-1]
        copies = []
        for k, (i, _, (rows, columns), row, column) in enumerate(moves):
            source = refs[k].at[pl.ds(rows[0], rows[1]), pl.ds(columns[0], columns[1])]
            target = out_refs[i].at[pl.ds(row, rows[1]), pl.ds(column, columns[1])]
            copies.append(pltpu.make_async_copy(source, target, sems.at[k]))
            copies[-1].start()
        for copy in copies:
            copy.wait()

    size = sum(math.prod(shape) for _, shape in targets)
    return pl.pallas_call(
        kernel,
        out_shape=[jax.ShapeDtypeStruct(shape, BF) for _, shape in targets],
        in_specs=[pl.BlockSpec(memory_space=pl.ANY)] * count,
        out_specs=[pl.BlockSpec(memory_space=pltpu.VMEM)] * len(targets),
        scratch_shapes=[pltpu.SemaphoreType.DMA((count,))],
        compiler_params=pltpu.CompilerParams(vmem_limit_bytes=VMEM_LIMIT),
        cost_estimate=pl.CostEstimate(flops=0, bytes_accessed=4 * size, transcendentals=0),
    )(*[move[1] for move in moves])


def body(frames_in, in_weights, down_weights, gains, cotangent, segment_ids, valid):
    core = lax.axis_index("c")
    yl = lax.axis_index("yl")
    y = 2 * lax.axis_index("yh") + yl
    zi = lax.axis_index("z")
    xi = lax.axis_index("x")
    is_first = core == 0
    is_low = yl == 0

    block = jnp.arange(16, dtype=jnp.int32)

    def offset(k):
        return jnp.where(k == 1, 3, k - k // 2)

    inner, outer = offset(block % 4), offset(block // 4)
    z_of = (zi + jnp.where(is_first, outer, inner)) % 4
    x_of = (xi + jnp.where(is_first, inner, outer)) % 4
    arrived = 4 * z_of + x_of
    chip = jnp.stack([y, yl])

    meta = jnp.concatenate([arrived, chip]).astype(jnp.int32)
    source = 32 * (8 * z_of[:, None] + x_of[:, None])
    source = source + 128 * jnp.stack([core, 1 - core])[None, :]
    source = (source[:, :, None] + jnp.arange(32, dtype=jnp.int32)).reshape(D)
    move = (lax.broadcasted_iota(jnp.int32, (D, D), 0) == source[None, :]).astype(BF)
    move_t = (lax.broadcasted_iota(jnp.int32, (D, D), 1) == source[:, None]).astype(BF)
    picks = unit_picks()

    def frames_to_chip(value):
        one, two = pick(is_first, to_chip(value, 0), to_chip(value, 1))
        return jnp.concatenate([one, two], axis=0)

    def pack_attn(shard):
        return run(
            pack_attn_kernel,
            meta,
            [shard],
            [((32, QKV + D), BF), ((32, QKV), BF)],
            [],
            1.7,
        )

    def attn_blocks(one, two, column):
        one, two = to_chip(one, 0), to_chip(two, 1)
        rows = (0, 32)
        return [
            (one, (rows, (0, ATTN)), 0, column),
            (two, (rows, (0, QKV)), 32, column),
            (one, (rows, (ATTN, HALF)), 32, column + QKV),
        ]

    def pack_ffn(shard, down, marks):
        padding = jnp.zeros((8, D), BF)
        if marks is not None:
            padding = lax.dynamic_update_slice(padding, marks[None], (0, 0))
        down = jnp.concatenate([down, padding], axis=0)
        return run(
            pack_ffn_kernel,
            meta,
            [shard, down, *picks],
            [((32, GATE_UP + 3 * D), BF), ((32, GATE_UP), BF)],
            [],
            4.5,
        )

    def ffn_blocks(one, two):
        one, two = to_chip(one, 0), to_chip(two, 1)
        rows, down, tail = (0, 32), GATE_UP + D, GATE_UP + 2 * D
        return [
            (one, (rows, (0, down)), 0, 0),
            (one, (rows, (tail, HALF)), 0, down),
            (two, (rows, (0, GATE_UP)), 32, 0),
            (one, (rows, (down, D)), 32, GATE_UP),
            (one, (rows, (tail + HALF, HALF)), 32, down),
        ]

    def to_owners(block, has_ffn, attn_at, extra):
        low, high, down = (0, 32), (32, 32), GATE_UP + D
        one, two, outs, kernels = [], [], [], []
        if has_ffn:
            one = [
                (block, (low, (0, down)), 0, 0),
                (block, (high, (GATE_UP, D)), 0, down),
                (block, (low, (down, HALF)), 0, down + D),
                (block, (high, (down, HALF)), 0, down + D + HALF),
            ]
            two = [(block, (high, (0, GATE_UP)), 0, 0)]
            outs += [((32, 4 * PAIR), F32), ((96, D), F32)]
        wide, narrow = (GATE_UP + 3 * D, GATE_UP) if has_ffn else (0, 0)
        first, second = wide, narrow
        if attn_at is not None:
            one += [(block, (low, (attn_at, ATTN)), 0, wide)]
            one += [(block, (high, (attn_at + QKV, HALF)), 0, wide + ATTN)]
            two += [(block, (high, (attn_at, QKV)), 0, narrow)]
            wide, narrow = wide + ATTN + HALF, narrow + QKV
            if extra:
                columns = (attn_at + ATTN, extra)
                one.append((block, (low, columns), 0, wide))
                two.append((block, (high, columns), 0, narrow))
                wide, narrow = wide + extra, narrow + extra
            outs += [((32, 4 * D), F32)]
        one, two = place_blocks((one, (32, wide)), (two, (32, narrow)))
        one, two = to_owner(one, 0), to_owner(two, 1)
        sums = plus(one[:, wide - extra :], two[:, narrow - extra :])[:, :4] if extra else None

        def kernel(meta_ref, ready, one_ref, two_ref, *refs):
            if has_ffn:
                pick_refs, refs = refs[:2], refs[2:]
                unpack_ffn_kernel(meta_ref, one_ref, two_ref, pick_refs, refs[0], refs[1])
                refs = refs[2:]
            if attn_at is not None:
                cols = pl.ds(first, ATTN + HALF), pl.ds(second, QKV)
                attn_refs = one_ref.at[:, cols[0]], two_ref.at[:, cols[1]]
                unpack_attn_kernel(meta_ref, *attn_refs, refs[0])

        operands = [one, two, *picks] if has_ffn else [one, two]
        results = list(run(kernel, meta, operands, outs, [], 5.0 if has_ffn else 1.8))
        if has_ffn:
            results[1] = results[1][:88]
        if attn_at is not None:
            results.append(sums)
        return results

    gain_rows = gains[:, 0].transpose(1, 2, 0).reshape(4, D)

    def gain_row(layer, which):
        place = 2 * layer + which
        return gain_all[place : place + 1]

    onehot = segment_ids[:, None] == jnp.arange(LANES, dtype=jnp.int32)[None, :]
    counts = jnp.sum(jnp.where(onehot, valid.astype(F32)[:, None], 0.0), axis=0).astype(BF)
    marks = jnp.stack([segment_ids, valid], axis=1).astype(BF)
    marked = jnp.concatenate([frames_in[:, 0], jnp.pad(marks, ((0, 0), (0, LANES - 2)))], axis=1)

    attn0 = pack_attn(in_weights[:, 0, 0, : 4 * D])
    attn0 = Gather(place_blocks((attn_blocks(*attn0, 0), (64, ATTN)))[0])
    attn0.one()
    later = after(in_weights, attn0.piece)
    ffn0_parts = pack_ffn(later[:, 0, 0, 4 * D :], down_weights[:, 0, 0], None)
    attn0.two(*ffn0_parts)
    attn1_parts = pack_attn(after(later, *ffn0_parts)[:, 0, 1, : 4 * D])
    attn0_three = attn0.three()
    blocks = ffn_blocks(*ffn0_parts)
    blocks += attn_blocks(*after(tuple(attn1_parts), blocks[0][0]), FFN)
    middle0 = Gather(place_blocks((blocks, (64, FFN + ATTN)))[0])
    later = after(in_weights, *attn1_parts)
    ffn1_parts = pack_ffn(later[:, 0, 1, 4 * D :], down_weights[:, 0, 1], counts)
    blocks = ffn_blocks(*after(tuple(ffn1_parts), blocks[-1][0]))
    ffn1 = Gather(place_blocks((blocks, (64, FFN)))[0])
    marked = frames_to_chip(after(marked, blocks[0][0]))
    state = marked[:, :D]
    marks = marked[:, D:]
    gain_all = to_chip(after(gain_rows, blocks[0][0]), 0).astype(F32)
    attn0_four = attn0.four()
    middle0.one()
    middle0.two()
    ffn1.one()
    ffn1_two = ffn1.two()
    ffn1_joined = ffn1.piece
    middle0_three = middle0.three(attn0_four, ffn1_two)
    ffn1.three(middle0_three)
    ffn1.four()

    def windows(gathered, start, end):
        if isinstance(gathered, list):
            return [(parts, 0, (start, end)) for parts in gathered]
        return [((gathered,), k * TILE, (start, end)) for k in range(4)]

    near = [(0, 1), (1, 0), (2, 3), (3, 2)]
    across = [(0, 3), (3, 0), (1, 2), (2, 1)]

    wide = ((TOKENS, D), F32)
    wide16 = ((TOKENS, D), BF)
    row = ((1, D), F32)
    saved = []
    base = None
    for layer in range(LAYERS):
        first = layer == 0
        attn, at = (attn0.blocks, 0) if first else (middle0.blocks, FFN)
        carried = [state] if first else list(base)
        state, normed, *blocks = run(
            lambda *refs, first=first: qkv_kernel(first, *refs),
            meta,
            [*carried, gain_row(layer, 0), move] + windows(attn, at, at + QKV),
            [wide, wide16] + [((ROWS, QKV), BF)] * 4,
            [(TOKENS, D), (TOKENS, QKV)],
            7.7,
        )
        blocks = exchange_column(blocks)
        if not first:
            cot = frames_to_chip(after(cotangent[:, 0], blocks[1]))
        mixed = run(
            attend_kernel,
            meta,
            blocks,
            [((ROWS, HALF), BF)] * 4,
            [(POS, ROWS, QKV), (POS, ROWS, HALF)],
            3.0,
        )
        if first:
            middle0.four()
        mixed = exchange_column(mixed)
        mixed16, partial = run(
            out_kernel,
            meta,
            mixed + windows(attn, at + QKV, at + ATTN),
            [((TOKENS, HALF), BF), wide16],
            [(HALF, D)],
            3.6,
        )
        ffn = (middle0 if first else ffn1).blocks
        middle, branch, gate, up_part, activated, down_partial, *totals = run(
            lambda *refs, first=first: ffn_kernel(not first, *refs),
            meta,
            [state, partial, other_core(partial), gain_row(layer, 1), move]
            + windows(ffn, 0, FFN),
            [wide, wide16, ((TOKENS, UNITS), F32), ((TOKENS, UNITS), F32)]
            + [((TOKENS, UNITS), BF), wide16]
            + ([] if first else [((1, LANES), F32)]),
            [(TOKENS, D), (UNITS, D)],
            11.0,
            (ffn1_joined,) if first else (),
        )
        saved.append(
            (state, normed, blocks, mixed16, middle, branch, gate, up_part, activated)
            + (attn, at, ffn)
        )
        base = (middle, down_partial, other_core(down_partial))
    totals = totals[0]
    other_totals = other_core(totals)

    def frames_to_owner(value):
        return to_owner(jnp.where(is_first, value[:128], value[128:]), 0)[:, None]

    output = frames_to_owner((base[0] + plus(base[1], base[2])).astype(BF))

    gain_list = [[None, None] for _ in range(LAYERS)]

    down_list = [None] * LAYERS

    def gradient_blocks(width):
        half = width // TILE // 2 * TILE
        return [((TILE, width), BF)] * 3 + [((TILE, half), BF), ((TILE, width - half), BF)]

    for layer in reversed(range(LAYERS)):
        state, normed, blocks, mixed16, middle, branch, gate, up_part, activated = saved[layer][:9]
        attn, at, ffn = saved[layer][9:]
        last = layer == LAYERS - 1
        carried = [cot, marks, totals, other_totals] if last else list(base)
        grad, grad16, gate_up16, partial, *results = run(
            lambda *refs, last=last: ffn_backward_kernel(last, *refs),
            meta,
            [*carried, gate, up_part, move] + windows(ffn, 0, FFN),
            [wide, wide16, ((TOKENS, GATE_UP), BF), wide16] + ([] if last else [row]),
            [(TOKENS, D), (UNITS, D)],
            9.0,
            () if last else above_two,
        )
        if not last:
            gain_list[layer + 1][0] = results[0]
        other = other_core(partial)
        base_grad = grad

        def ffn_gradient(grad16):
            return Scatter(
                *run(
                    lambda *refs, last=last: ffn_gradient_kernel(last, *refs),
                    meta,
                    [branch, activated, grad16, gate_up16, move_t]
                    + ([] if last else windows(attn_above, 0, ATTN)),
                    gradient_blocks(FFN if last else FFN + ATTN),
                    [(D, TOKENS), (UNITS, TOKENS), (UNITS, TOKENS)],
                    12.0,
                )
            )

        if not last:
            ffn_above.two_sums(partial)
            above_three = ffn_above.three()
            ffn_sum = ffn_gradient(grad16)
            ffn_sum.one()
        grad, gain_list[layer][1], attn16, *mixed = run(
            out_backward_kernel,
            meta,
            [base_grad, partial, other, middle, gain_row(layer, 1)]
            + windows(attn, at + QKV, at + ATTN),
            [wide, row, wide16] + [((ROWS, HALF), BF)] * 4,
            [(TOKENS, HALF), (HALF, D)],
            4.5,
            () if last else above_three,
        )
        own = mixed[0]
        mixed = exchange_column(mixed)
        if last:
            ffn_above = ffn_gradient(after(grad16, own))
            above_one = ffn_above.one()
            early = ()
        else:
            early = ffn_sum.one_sums(own)
            ffn_sum.two()
        grads = run(
            attend_backward_kernel,
            meta,
            [*blocks, *mixed],
            [((ROWS, QKV), BF)] * 4,
            [(POS, ROWS, QKV), (POS, ROWS, HALF), (POS, ROWS, QKV)],
            3.8 if last else 1.1,
            early,
        )
        own = grads[0]
        grads = exchange_column(grads)
        if last:
            ffn_above.one_sums(own)
            above_two = ffn_above.two()
            grads[0] = after(own, output)
        else:
            ffn_above.three_sums(own)
        partial, qkv16 = run(
            qkv_backward_kernel,
            meta,
            [*grads, move] + windows(attn, at, at + QKV),
            [wide16, ((TOKENS, QKV), BF)],
            [(TOKENS, D)],
            5.0 if last else 1.5,
            above_one if last else (),
        )
        pieces = run(
            lambda *refs, first=not last: attn_gradient_kernel(first, *refs),
            meta,
            [normed, qkv16, mixed16, attn16, move_t]
            + ([] if last else [partial, state, gain_list[0][1], *gain_list[1]]),
            [((D, ATTN), BF)] if last else gradient_blocks(ATTN_GAINS),
            [(D, TOKENS), (HALF, TOKENS), (HALF, TOKENS)],
            7.0 if last else 2.0,
        )
        if last:
            attn_above = pieces[0]
        else:
            attn_sum = Scatter(*pieces)
            attn_sum.one()
            ffn_above.four(pieces[0])
        base = (grad, partial, other_core(partial), state, gain_row(layer, 0))
    middle = ffn_sum.two_sums()
    ffn_sum.three()
    attn_sum.one_sums()
    attn_sum.two(middle)
    ffn_sum.three_sums()
    ffn_sum.four()
    middle = attn_sum.two_sums()
    attn_sum.three()
    input_grad = run(last_kernel, meta, list(base), [wide16], [], 4.3, (middle,))[0]
    units_above, down_list[1] = to_owners(
        after(ffn_above.four_sums(), pieces[0]), True, None, 0
    )
    last_sums = attn_sum.three_sums()
    attn_sum.four()
    both = after(ffn_sum.four_sums(), last_sums)
    units, down_list[0], attn_above, _ = to_owners(both, True, FFN, 0)
    attn, gain_sums = to_owners(attn_sum.four_sums(), False, 0, LANES)
    in_parts = [[attn, units], [attn_above, units_above]]
    in_list = [jnp.concatenate(parts, axis=1) for parts in in_parts]
    in_grads = jnp.stack(in_list, axis=1)[:, None]
    down_grads = jnp.stack(down_list, axis=1)[:, None]

    gains_grad = gain_sums.reshape(32, 1, LAYERS, 2)
    return (output, frames_to_owner(input_grad), in_grads, down_grads, gains_grad)


def solution(mesh):
    parts = Mesh(mesh.devices.reshape(2, 2, 4, 2, 4), ("yh", "c", "z", "yl", "x"))
    dp = ("z", "yl", "x")
    section = ("yh", "c")
    return jax.shard_map(
        body,
        mesh=parts,
        in_specs=(
            P(dp, section, None),
            P(dp, section, None, None),
            P(dp, section, None, None),
            P(None, section, None, None),
            P(dp, section, None),
            P(dp),
            P(dp),
        ),
        out_specs=(
            P(dp, section, None),
            P(dp, section, None),
            P(dp, section, None, None),
            P(dp, section, None, None),
            P(dp, section, None, None),
        ),
        check_vma=False,
    )
```

```python
import math

import jax
import jax.numpy as jnp
import numpy as np
from jax import lax
from jax.experimental import pallas as pl
from jax.experimental.pallas import tpu as pltpu
from jax.sharding import Mesh, PartitionSpec as P

D = 1024
HEAD = 64
LAYERS = 2
POS = 4
NSEG = 16
EPS = 1e-05
COUNT_BOOST = 4.0

HALF = D // 2
UNITS = 1536
TOKENS = 256
ROWS = TOKENS // POS
LANES = 128
TILE = 256

BF = jnp.bfloat16
F32 = jnp.float32

PLANE = ("c", "z", "x")
COLUMN = ("yh", "yl")
FIRST = ("x", "z")
SECOND = ("z", "x")

QKV = 3 * HALF
ATTN = QKV + HALF
GATE_UP = 2 * UNITS
FFN = GATE_UP + D + HALF
ATTN_GAINS = ATTN + LANES
PAIR = 1408


def unit_picks():
    unit = np.arange(768)
    rest = unit - HALF
    source = np.where(
        unit < HALF,
        704 * (unit // 256) + 88 * (unit % 256 // 64) + unit % 64,
        704 * (rest // 128) + 88 * (rest % 128 // 32) + 64 + rest % 32,
    )
    source = np.where((unit >= HALF) & (rest % 32 >= 24), -PAIR, source)
    row = np.arange(PAIR)[:, None]
    return [jnp.asarray(row == (source + 352 * half)[None, :], BF) for half in range(2)]


def ring_pairs(axis_of_core, step):
    pairs = []
    for c in range(2):
        for z in range(4):
            for x in range(4):
                if axis_of_core[c] == "x":
                    target = (c * 4 + z) * 4 + (x + step) % 4
                else:
                    target = (c * 4 + (z + step) % 4) * 4 + x
                pairs.append(((c * 4 + z) * 4 + x, target))
    return pairs


def shift(value, axis_of_core, step):
    return lax.ppermute(value, PLANE, ring_pairs(axis_of_core, step))


def after(value, *others):
    return lax.optimization_barrier((value, others))[0]


class Gather:
    def __init__(self, piece):
        self.piece = piece

    def near(self, axis_of_core, *deps):
        self.piece = after(self.piece, *deps)
        self.left = shift(self.piece, axis_of_core, 1)
        self.right = shift(self.piece, axis_of_core, -1)
        return self.left, self.right

    def far(self, axis_of_core, *deps):
        half = self.piece.shape[1] // 2
        far_a = shift(after(self.left[:, :half], *deps), axis_of_core, 1)
        far_b = shift(after(self.right[:, half:], *deps), axis_of_core, -1)
        self.blocks = [(self.piece,), (self.left,), (self.right,), (far_a, far_b)]
        return far_a, far_b

    def one(self, *deps):
        return self.near(FIRST, *deps)

    def two(self, *deps):
        done = self.far(FIRST, *deps)
        rows, width = self.piece.shape
        half = width // 2
        whole, part = ((0, rows), (0, width)), ((0, rows), (0, half))
        blocks = [(self.piece, whole, 0, 0), (self.left, whole, rows, 0)]
        blocks += [(self.right, whole, 2 * rows, 0)]
        blocks += [(done[0], part, 3 * rows, 0), (done[1], part, 3 * rows, half)]
        self.piece = place_blocks((blocks, (4 * rows, width)))[0]
        return done

    def three(self, *deps):
        return self.near(SECOND, *deps)

    def four(self, *deps):
        return self.far(SECOND, *deps)


def plus(one, two):
    return one.astype(F32) + two.astype(F32)


def add_halves(left, right, far_a, far_b):
    rows, width = right.shape
    half = far_a.shape[1]
    rest = width - half

    def kernel(left_ref, right_ref, a_ref, b_ref, left_out, right_out, held_a, held_b, a_s, b_s, sems):
        first, last = pl.ds(0, half), pl.ds(half, rest)
        loads = [
            pltpu.make_async_copy(right_ref.at[:, first], held_a, sems.at[0]),
            pltpu.make_async_copy(a_ref, a_s, sems.at[1]),
            pltpu.make_async_copy(left_ref.at[:, last], held_b, sems.at[2]),
            pltpu.make_async_copy(b_ref, b_s, sems.at[3]),
        ]
        for copy in loads:
            copy.start()
        stores = []
        for place, (held, other, target) in enumerate(
            ((held_a, a_s, right_out.at[:, first]), (held_b, b_s, left_out.at[:, last]))
        ):
            loads[2 * place].wait()
            loads[2 * place + 1].wait()

            @pl.loop(0, rows // 16)
            def _(step):
                part = pl.ds(pl.multiple_of(step * 16, 16), 16)
                held[part, :] = (held[part, :].astype(F32) + other[part, :].astype(F32)).astype(BF)

            stores.append(pltpu.make_async_copy(held, target, sems.at[4 + place]))
            stores[-1].start()
        for copy in stores:
            copy.wait()

    scratch = [(rows, half), (rows, rest), (rows, half), (rows, rest)]
    return pl.pallas_call(
        kernel,
        out_shape=[jax.ShapeDtypeStruct(left.shape, BF), jax.ShapeDtypeStruct(right.shape, BF)],
        in_specs=[pl.BlockSpec(memory_space=pl.ANY)] * 4,
        out_specs=[pl.BlockSpec(memory_space=pl.ANY)] * 2,
        scratch_shapes=[pltpu.VMEM(shape, BF) for shape in scratch]
        + [pltpu.SemaphoreType.DMA((6,))],
        input_output_aliases={0: 0, 1: 1},
        compiler_params=pltpu.CompilerParams(vmem_limit_bytes=VMEM_LIMIT),
        cost_estimate=pl.CostEstimate(
            flops=0, bytes_accessed=6 * rows * width, transcendentals=0
        ),
    )(left, right, far_a, far_b)


class Scatter:
    def __init__(self, own, left, right, far_a, far_b):
        self.parts = own, left, right, far_a, far_b
        self.half = far_a.shape[1]

    def far(self, axis_of_core, deps):
        far_a, far_b = self.parts[3:]
        far_a = shift(after(far_a, *deps), axis_of_core, 1)
        far_b = shift(after(far_b, *deps), axis_of_core, -1)
        self.got = far_a, far_b
        return self.got

    def far_sums(self, deps):
        own, left, right = self.parts[:3]
        far_a, far_b = after(self.got, *deps)
        left, right = add_halves(left, right, far_a, far_b)
        self.parts = own, left, right
        return left, right

    def near(self, axis_of_core, deps):
        own, left, right = self.parts
        from_left = shift(after(right, *deps), axis_of_core, 1)
        from_right = shift(after(left, *deps), axis_of_core, -1)
        self.got = from_left, from_right
        return self.got

    def near_sums(self, deps):
        from_left, from_right = after(self.got, *deps)
        self.block = (plus(self.parts[0], from_left) + from_right.astype(F32)).astype(BF)
        return self.block

    def one(self, *deps):
        return self.far(SECOND, deps)

    def one_sums(self, *deps):
        return self.far_sums(deps)

    def two(self, *deps):
        return self.near(SECOND, deps)

    def two_sums(self, *deps):
        block = self.near_sums(deps)
        own, left, right, far = [block[k * 64 : (k + 1) * 64] for k in range(4)]
        self.parts = own, left, right, far[:, : self.half], far[:, self.half :]
        return block

    def three(self, *deps):
        return self.far(FIRST, deps)

    def three_sums(self, *deps):
        return self.far_sums(deps)

    def four(self, *deps):
        return self.near(FIRST, deps)

    def four_sums(self, *deps):
        return self.near_sums(deps)


def to_chip(value, place):
    pairs = [(c * 2 + yl, (yl ^ place) * 2 + c) for c in range(2) for yl in range(2)]
    return lax.ppermute(value, ("c", "yl"), pairs)


def to_owner(value, place):
    pairs = [(c * 2 + yl, yl * 2 + (c ^ place)) for c in range(2) for yl in range(2)]
    return lax.ppermute(value, ("c", "yl"), pairs)


def other_core(value):
    return lax.ppermute(value, "c", [(0, 1), (1, 0)])


def pick(flag, one, two):
    return jnp.where(flag, one, two), jnp.where(flag, two, one)


def exchange_column(blocks):
    got = [blocks[0]]
    for k in range(1, POS):
        got.append(lax.ppermute(blocks[k], COLUMN, [(y, y ^ k) for y in range(POS)]))
    return got


def dot(one, two):
    return jnp.dot(one, two, preferred_element_type=F32)


def dot_nt(one, two):
    return lax.dot_general(one, two, (((1,), (1,)), ((), ())), preferred_element_type=F32)


Y, YL = 16, 17


def identity(size):
    row = lax.broadcasted_iota(jnp.int32, (size, size), 0)
    return (row == lax.broadcasted_iota(jnp.int32, (size, size), 1)).astype(F32).astype(BF)


def row_block(step):
    return pl.ds(pl.multiple_of(step * 32, 32), 32)


def lane_tile(step):
    return pl.ds(pl.multiple_of(step * TILE, TILE), TILE)


def chip_rows(meta, k):
    return pl.ds(pl.multiple_of((meta[Y] ^ k) * ROWS, ROWS), ROWS)


def rsqrt_mean(state):
    return lax.rsqrt(jnp.mean(state * state, axis=-1, keepdims=True) + EPS)


def norm_rows(step, state, gain_ref, out_ref):
    out_ref[row_block(step), :] = (state * rsqrt_mean(state) * gain_ref[...]).astype(BF)


def move_rows(a_s, mv_ref, mvt_ref, moved_s, moved_t_ref):
    for j in range(D // TILE):
        cols = slice(j * TILE, (j + 1) * TILE)
        moved_s[:, cols] = dot(a_s[...], mv_ref[:, cols]).astype(BF)
        moved_t_ref[cols, :] = dot_nt(mvt_ref[cols, :], a_s[...]).astype(BF)


def dot_pieces(left_s, pieces, cols):
    total = None
    for k, piece in enumerate(pieces):
        term = dot(left_s[:, k * TILE : (k + 1) * TILE], piece[:, cols])
        total = term if total is None else total + term
    return total


def qkv_kernel(first, meta, ready, *refs):
    if first:
        x_ref, gain_ref, mv_ref, mvt_ref, *refs = refs
    else:
        x_ref, own_ref, other_ref, gain_ref, mv_ref, mvt_ref, *refs = refs
    pieces, refs = refs[:4], refs[4:]
    h_ref, art_ref, *refs = refs
    outs, (a_s, ar_s, qkv_s) = refs[:4], refs[4:]

    @pl.loop(0, TOKENS // 32)
    def _(step):
        state = x_ref[row_block(step), :].astype(F32)
        if not first:
            state = state + own_ref[row_block(step), :].astype(F32)
            state = state + other_ref[row_block(step), :].astype(F32)
        h_ref[row_block(step), :] = state
        norm_rows(step, state, gain_ref, a_s)

    move_rows(a_s, mv_ref, mvt_ref, ar_s, art_ref)
    ready()

    @pl.loop(0, QKV // TILE)
    def _(step):
        qkv_s[:, lane_tile(step)] = dot_pieces(ar_s, pieces, lane_tile(step)).astype(BF)

    for k in range(POS):
        outs[k][...] = qkv_s[chip_rows(meta, k), :]


PAIRS = [(p, r) for p in range(POS) for r in range(p + 1)]


def head_matrix(shape, feature_dim):
    feature = lax.broadcasted_iota(jnp.int32, shape, feature_dim) // HEAD
    head = lax.broadcasted_iota(jnp.int32, shape, 1 - feature_dim)
    return (feature == head).astype(F32).astype(BF)


def head_sums(products):
    ones = head_matrix((HALF, LANES), 0)
    high = products.astype(BF)
    low = (products - high.astype(F32)).astype(BF)
    return dot(high, ones) + dot(low, ones)


def head_spread(values16):
    return dot(values16, head_matrix((LANES, HALF), 1))


def pair_probs(queries, keys):
    products = jnp.concatenate([queries[p] * keys[r] for p, r in PAIRS], axis=0)
    scores = head_sums(products) * (1.0 / math.sqrt(HEAD))
    probs = {}
    for p in range(POS):
        own = [scores[i * ROWS : (i + 1) * ROWS] for i, pair in enumerate(PAIRS) if pair[0] == p]
        peak = own[0]
        for term in own[1:]:
            peak = jnp.maximum(peak, term)
        terms = [jnp.exp(term - peak) for term in own]
        total = terms[0]
        for term in terms[1:]:
            total = total + term
        for r in range(p + 1):
            probs[p, r] = terms[r] / total
    return probs


def split_qkv(meta, blocks, qkv_s):
    for k in range(POS):
        qkv_s[k] = blocks[k][...]
    return [
        [qkv_s[p ^ meta[Y], :, t * HALF : (t + 1) * HALF].astype(F32) for p in range(POS)]
        for t in range(3)
    ]


def attend_kernel(meta, ready, *refs):
    blocks, outs, (qkv_s, out_s) = refs[:4], refs[4:8], refs[8:]
    queries, keys, values = split_qkv(meta, blocks, qkv_s)
    probs = pair_probs(queries, keys)
    spread = head_spread(jnp.concatenate([probs[pair].astype(BF) for pair in PAIRS], axis=0))
    for p in range(POS):
        total = None
        for i, (pp, r) in enumerate(PAIRS):
            if pp == p:
                term = spread[i * ROWS : (i + 1) * ROWS] * values[r]
                total = term if total is None else total + term
        out_s[p ^ meta[Y]] = total.astype(BF)
    for k in range(POS):
        outs[k][...] = out_s[k]


def attend_backward_kernel(meta, ready, *refs):
    blocks, grad_blocks, outs, (qkv_s, grad_s, out_s) = refs[:4], refs[4:8], refs[8:12], refs[12:]
    queries, keys, values = split_qkv(meta, blocks, qkv_s)
    for k in range(POS):
        grad_s[k] = grad_blocks[k][...]
    grads = [grad_s[p ^ meta[Y]].astype(F32) for p in range(POS)]
    probs = pair_probs(queries, keys)
    products = jnp.concatenate([grads[p] * values[r] for p, r in PAIRS], axis=0)
    grad_probs = head_sums(products)
    grad_probs = {pair: grad_probs[i * ROWS : (i + 1) * ROWS] for i, pair in enumerate(PAIRS)}
    grad_scores = []
    for p, r in PAIRS:
        mean = probs[p, 0] * grad_probs[p, 0]
        for other in range(1, p + 1):
            mean = mean + probs[p, other] * grad_probs[p, other]
        grad_scores.append(probs[p, r] * (grad_probs[p, r] - mean) * (1.0 / math.sqrt(HEAD)))
    stacked = jnp.concatenate(grad_scores, axis=0)
    high = stacked.astype(BF)
    low = (stacked - high.astype(F32)).astype(BF)
    spread_scores = head_spread(high) + head_spread(low)
    spread_probs = head_spread(jnp.concatenate([probs[pair].astype(BF) for pair in PAIRS], axis=0))
    grad_q = [None] * POS
    grad_k = [None] * POS
    grad_v = [None] * POS

    def put(totals, place, term):
        totals[place] = term if totals[place] is None else totals[place] + term

    for i, (p, r) in enumerate(PAIRS):
        score = spread_scores[i * ROWS : (i + 1) * ROWS]
        put(grad_q, p, score * keys[r])
        put(grad_k, r, score * queries[p])
        put(grad_v, r, spread_probs[i * ROWS : (i + 1) * ROWS] * grads[p])
    for p in range(POS):
        for t, totals in enumerate((grad_q, grad_k, grad_v)):
            out_s[p ^ meta[Y], :, t * HALF : (t + 1) * HALF] = totals[p].astype(BF)
    for k in range(POS):
        outs[k][...] = out_s[k]


def unpack_rows(meta, pieces, out_ref, start):
    for k in range(16):
        rows = pl.ds(pl.multiple_of(start + meta[k] * 32, 32), 32)
        piece, row = pieces[k // 4], (k % 4) * 64
        out_ref[rows, :HALF] = piece[row : row + 32, :]
        out_ref[rows, HALF:] = piece[row + 32 : row + 64, :]


def transpose_into(source_s, out_s):
    eye = identity(TILE)
    for j in range(source_s.shape[1] // TILE):
        cols = slice(j * TILE, (j + 1) * TILE)
        out_s[cols, :] = dot_nt(eye, source_s[:, cols]).astype(BF)


def out_kernel(meta, ready, *refs):
    blocks, pieces, refs = refs[:4], refs[4:8], refs[8:]
    ort_ref, wo_ref, partial_ref, o_s, ot_s = refs
    for k in range(POS):
        o_s[chip_rows(meta, k), :] = blocks[k][...]
    transpose_into(o_s, ot_s)
    ready()
    unpack_rows(meta, pieces, wo_ref, 0)
    for k in range(16):
        ort_ref[k * 32 : (k + 1) * 32, :] = ot_s[pl.ds(pl.multiple_of(meta[k] * 32, 32), 32), :]
    for j in range(D // TILE):
        cols = slice(j * TILE, (j + 1) * TILE)
        partial_ref[:, cols] = dot(o_s[...], wo_ref[:, cols]).astype(BF)


def ffn_kernel(counting, meta, ready, *refs):
    h_ref, own_ref, other_ref, gain_ref, mv_ref, mvt_ref, *refs = refs
    pieces, refs = refs[:4], refs[4:]
    m_ref, brt_ref, gate_ref, up_ref, actrt_ref, wd_ref, partial_ref, *refs = refs
    if counting:
        total_ref, *refs = refs
    b_s, br_s, act_s, actt_s = refs

    @pl.loop(0, TOKENS // 32)
    def _(step):
        state = h_ref[row_block(step), :] + own_ref[row_block(step), :].astype(F32)
        state = state + other_ref[row_block(step), :].astype(F32)
        m_ref[row_block(step), :] = state
        norm_rows(step, state, gain_ref, b_s)

    move_rows(b_s, mv_ref, mvt_ref, br_s, brt_ref)
    ready()

    @pl.loop(0, UNITS // TILE)
    def _(step):
        cols = lane_tile(step)
        gate = dot_pieces(br_s, pieces, cols)
        gate_ref[:, cols] = gate
        up = dot_pieces(br_s, pieces, lane_tile(step + UNITS // TILE))
        up_ref[:, cols] = up
        act_s[:, cols] = (gate * jax.nn.sigmoid(gate) * up).astype(BF)

    for k in range(16):
        rows = pl.ds(pl.multiple_of(meta[k] * 64, 64), 64)
        wd_ref[rows, :] = pieces[k // 4][
            (k % 4) * 64 : (k % 4 + 1) * 64, GATE_UP : GATE_UP + D
        ]
    unpack_rows(meta, [piece.at[:, pl.ds(GATE_UP + D, HALF)] for piece in pieces], wd_ref, D)
    if counting:
        total = jnp.zeros((1, LANES), F32)
        for k in range(16):
            rows = slice(D + k * 32, D + (k + 1) * 32)
            total = total + wd_ref[rows, :LANES].astype(F32)[24:25]
        total_ref[...] = total
    transpose_into(act_s, actt_s)
    for k in range(16):
        rows = pl.ds(pl.multiple_of(meta[k] * 64, 64), 64)
        actrt_ref[k * 64 : (k + 1) * 64, :] = actt_s[rows, :]
        rows = pl.ds(pl.multiple_of(D + meta[k] * 32, 32), 32)
        actrt_ref[D + k * 32 : D + (k + 1) * 32, :] = actt_s[rows, :]

    @pl.loop(0, D // TILE)
    def _(step):
        cols = lane_tile(step)
        partial_ref[:, cols] = dot(act_s[...], wd_ref[:, cols]).astype(BF)


def norm_backward(base_ref, own_ref, other_ref, state_ref, gain_ref, put):
    def one_block(step, total):
        rows = row_block(step)
        own = own_ref[rows, :].astype(F32)
        grad = own + other_ref[rows, :].astype(F32)
        state = state_ref[rows, :].astype(F32)
        scale = rsqrt_mean(state)
        normed = state * scale
        grad_norm = grad * gain_ref[...]
        mean = jnp.mean(grad_norm * normed, axis=-1, keepdims=True)
        put(rows, base_ref[rows, :] + scale * (grad_norm - normed * mean))
        return total + jnp.sum((own * normed).reshape(4, 8, D), axis=0)

    total = lax.fori_loop(0, TOKENS // 32, one_block, jnp.zeros((8, D), F32))
    return jnp.sum(total, axis=0, keepdims=True)


def put_piece(refs, k, rows, start, value):
    width = value.shape[1]
    if len(refs) == 1:
        refs[0][slice(k * TILE + rows.start, k * TILE + rows.stop), start : start + width] = value
    elif k < 3:
        refs[k][rows, start : start + width] = value
    else:
        half = refs[3].shape[1]
        if start < half:
            refs[3][rows, start : start + width] = value
        else:
            refs[4][rows, start - half : start - half + width] = value


def put_packed(refs, k, start, step, value):
    for i in range(4):
        row = i * 64 + (step // 2) * 32
        put_piece(
            refs, k, slice(row, row + 32), start + (step % 2) * TILE, value[i * 32 : (i + 1) * 32]
        )


def ffn_backward_kernel(last, meta, ready, *refs):
    if last:
        cot_ref, marks_ref, totals_ref, other_totals_ref, *refs = refs
    else:
        base_ref, own_ref, other_ref, state_ref, gain_ref, *refs = refs
    actrt_ref, brt_ref, gate_ref, up_ref, wd_ref, mv_ref, *refs = refs
    held = 4 if last else 8
    pieces, refs = refs[:held], refs[held:]
    g_ref, *refs = refs
    if not last:
        dgain_ref, *refs = refs
    partial_ref, *refs = refs
    outs, (gf_s, dgu_s, dbr_s) = refs[:-3], refs[-3:]
    pieces, above = pieces[:4], pieces[4:]

    def put(rows, value):
        g_ref[rows, :] = value
        gf_s[rows, :] = value.astype(BF)

    if last:

        @pl.loop(0, TOKENS // 32)
        def _(step):
            rows = row_block(step)
            marks = marks_ref[rows, :].astype(F32)
            totals = totals_ref[...] + other_totals_ref[...]
            place = lax.broadcasted_iota(jnp.int32, (32, LANES), 1).astype(F32)
            count = jnp.sum(jnp.where(place == marks[:, :1], totals, 0.0), axis=1, keepdims=True)
            weight = marks[:, 1:2] * (1.0 + COUNT_BOOST / jnp.maximum(count, 1.0))
            put(rows, cot_ref[rows, :].astype(F32) * weight)

    else:
        dgain_ref[...] = norm_backward(base_ref, own_ref, other_ref, state_ref, gain_ref, put)

    @pl.loop(0, UNITS // TILE)
    def _(step):
        cols = lane_tile(step)
        grad_act = dot_nt(gf_s[...], wd_ref[cols, :])
        gate = gate_ref[:, cols]
        sigma = jax.nn.sigmoid(gate)
        grad_up = grad_act * gate * sigma
        grad_gate = grad_act * up_ref[:, cols] * sigma * (1.0 + gate * (1.0 - sigma))
        dgu_s[:, cols] = grad_gate.astype(BF)
        dgu_s[:, lane_tile(step + UNITS // TILE)] = grad_up.astype(BF)

    everything = slice(0, TILE)
    for k in (3, 1, 2, 0):
        rows = slice(k * TILE, (k + 1) * TILE)
        for j in range(GATE_UP // TILE):
            value = dot(brt_ref[rows, :], dgu_s[:, j * TILE : (j + 1) * TILE]).astype(BF)
            put_piece(outs, k, everything, j * TILE, value)
        for j in range(D // TILE):
            value = dot(actrt_ref[rows, :], gf_s[:, j * TILE : (j + 1) * TILE]).astype(BF)
            put_piece(outs, k, everything, GATE_UP + j * TILE, value)
        tail = slice(D + k * 128, D + (k + 1) * 128)
        for j in range(D // TILE):
            value = dot(actrt_ref[tail, :], gf_s[:, j * TILE : (j + 1) * TILE]).astype(BF)
            put_packed(outs, k, GATE_UP + D, j, value)
    ready()
    for k, sums in enumerate(above):
        for j in range(ATTN // TILE):
            put_piece(outs, k, everything, FFN + j * TILE, sums[:, j * TILE : (j + 1) * TILE])
    for k in range(4):
        dbr_s[:, k * TILE : (k + 1) * TILE] = dot_nt(dgu_s[...], pieces[k][...]).astype(BF)
    for j in range(D // TILE):
        cols = slice(j * TILE, (j + 1) * TILE)
        partial_ref[:, cols] = dot_nt(dbr_s[...], mv_ref[cols, :]).astype(BF)


def out_backward_kernel(meta, ready, *refs):
    base_ref, own_ref, other_ref, state_ref, gain_ref, ort_ref, wo_ref, *refs = refs
    gm_ref, dgain_ref, dwo_ref, *refs = refs
    outs, (ga_s, do_s) = refs[:4], refs[4:]

    def put(rows, value):
        gm_ref[rows, :] = value
        ga_s[rows, :] = value.astype(BF)

    dgain_ref[...] = norm_backward(base_ref, own_ref, other_ref, state_ref, gain_ref, put)
    for j in range(HALF // TILE):
        cols = slice(j * TILE, (j + 1) * TILE)
        do_s[:, cols] = dot_nt(ga_s[...], wo_ref[cols, :]).astype(BF)
    for k in range(POS):
        outs[k][...] = do_s[chip_rows(meta, k), :]
    for k in range(4):
        for j in range(D // TILE):
            cols = slice(j * TILE, (j + 1) * TILE)
            value = dot(ort_ref[k * 128 : (k + 1) * 128, :], ga_s[:, cols]).astype(BF)
            for i in range(4):
                row = k * TILE + i * 64 + (j // 2) * 32
                part = slice((j % 2) * TILE, (j % 2 + 1) * TILE)
                dwo_ref[row : row + 32, part] = value[i * 32 : (i + 1) * 32]


def qkv_backward_kernel(first, meta, ready, *refs):
    blocks, refs = refs[:4], refs[4:]
    art_ref, dwo_ref, mv_ref, *refs = refs
    if first:
        mvt_ref, state_ref, *gain_refs = refs[:5]
        refs = refs[5:]
    pieces, refs = refs[:4], refs[4:]
    partial_ref, *refs = refs
    outs, (dqkv_s, dar_s) = refs[:-2], refs[-2:]
    for k in range(POS):
        dqkv_s[chip_rows(meta, k), :] = blocks[k][...]
    ready()
    for k in range(4):
        dar_s[:, k * TILE : (k + 1) * TILE] = dot_nt(dqkv_s[...], pieces[k][...]).astype(BF)
    for j in range(D // TILE):
        cols = slice(j * TILE, (j + 1) * TILE)
        partial_ref[:, cols] = dot_nt(dar_s[...], mv_ref[cols, :]).astype(BF)
    everything = slice(0, TILE)
    if first:
        def one_block(step, total):
            state = state_ref[row_block(step), :]
            term = partial_ref[row_block(step), :].astype(F32) * state * rsqrt_mean(state)
            return total + jnp.sum(term.reshape(4, 8, D), axis=0)

        total = lax.fori_loop(0, TOKENS // 32, one_block, jnp.zeros((8, D), F32))
        grads = [jnp.sum(total, axis=0, keepdims=True)] + [ref[...] for ref in gain_refs]
        grads = jnp.concatenate(grads + [jnp.zeros((LANES - 4, D), F32)], axis=0).astype(BF)
        for k in range(4):
            value = dot_nt(mvt_ref[k * TILE : (k + 1) * TILE, :], grads).astype(BF)
            put_piece(outs, k, everything, ATTN, value)
    for k in (3, 1, 2, 0):
        rows = slice(k * TILE, (k + 1) * TILE)
        for j in range(QKV // TILE):
            value = dot(art_ref[rows, :], dqkv_s[:, j * TILE : (j + 1) * TILE]).astype(BF)
            put_piece(outs, k, everything, j * TILE, value)
        put_piece(outs, k, everything, QKV, dwo_ref[rows, :])


def last_kernel(meta, ready, *refs):
    base_ref, own_ref, other_ref, state_ref, gain_ref, out_ref = refs

    def put(rows, value):
        out_ref[rows, :] = value.astype(BF)

    norm_backward(base_ref, own_ref, other_ref, state_ref, gain_ref, put)


def pack_attn_kernel(meta, ready, *refs):
    shard, one_ref, two_ref = refs
    low = meta[YL] == 0
    for k in range(QKV // LANES):
        first = shard[:, 2 * k * LANES : (2 * k + 1) * LANES]
        second = shard[:, (2 * k + 1) * LANES : (2 * k + 2) * LANES]
        cols = slice(k * LANES, (k + 1) * LANES)
        one_ref[:, cols] = jnp.where(low, first, second)
        two_ref[:, cols] = jnp.where(low, second, first)
    one_ref[:, QKV:] = shard[:, 3 * D :]


def pack_ffn_kernel(meta, ready, *refs):
    shard, down_ref, *picks = refs[:4]
    one_ref, two_ref = refs[4:]
    low = meta[YL] == 0
    parts = jnp.concatenate([shard[:, k * PAIR : (k + 1) * PAIR] for k in range(4)], axis=0)
    first, second = [dot(parts, pick_ref[...]).astype(BF) for pick_ref in picks]
    for ref, value in (
        (one_ref, jnp.where(low, first, second)),
        (two_ref, jnp.where(low, second, first)),
    ):
        for k in range(4):
            rows = slice(k * 32, (k + 1) * 32)
            start = (k // 2) * UNITS + (k % 2) * HALF
            ref[:, start : start + HALF] = value[rows, :HALF]
            start = (k // 2) * UNITS + D + (k % 2) * TILE
            ref[:, start : start + TILE] = value[rows, HALF:]
    for k in range(3):
        one_ref[:, GATE_UP + k * D : GATE_UP + (k + 1) * D] = down_ref[k * 32 : (k + 1) * 32, :]


def unpack_attn_kernel(meta, one_ref, two_ref, out_ref):
    low = meta[YL] == 0
    for k in range(QKV // LANES):
        cols = slice(k * LANES, (k + 1) * LANES)
        first, second = one_ref[:, cols].astype(F32), two_ref[:, cols].astype(F32)
        out_ref[:, 2 * k * LANES : (2 * k + 1) * LANES] = jnp.where(low, first, second)
        out_ref[:, (2 * k + 1) * LANES : (2 * k + 2) * LANES] = jnp.where(low, second, first)
    out_ref[:, 3 * D :] = one_ref[:, QKV : QKV + D].astype(F32)


def unpack_ffn_kernel(meta, one_ref, two_ref, picks, out_ref, down_ref):
    low = meta[YL] == 0
    halves = []
    for ref in (one_ref, two_ref):
        parts = []
        for k in range(4):
            start = (k // 2) * UNITS + (k % 2) * HALF
            main = ref[:, start : start + HALF]
            start = (k // 2) * UNITS + D + (k % 2) * TILE
            parts.append(jnp.concatenate([main, ref[:, start : start + TILE]], axis=1))
        halves.append(jnp.concatenate(parts, axis=0))
    first = jnp.where(low, halves[0], halves[1])
    second = jnp.where(low, halves[1], halves[0])
    total = dot_nt(first, picks[0][...]) + dot_nt(second, picks[1][...])
    for k in range(4):
        out_ref[:, k * PAIR : (k + 1) * PAIR] = total[k * 32 : (k + 1) * 32]
    for k in range(3):
        part = one_ref[:, GATE_UP + k * D : GATE_UP + (k + 1) * D].astype(F32)
        down_ref[k * 32 : (k + 1) * 32, :] = part


RATE = 3.4e6
VMEM_LIMIT = 56 * 1024 * 1024


def run(kernel, meta, operands, outs, scratch, micros, early=()):
    arrays, specs, places, windows = [], [], [], []
    for operand in operands:
        places.append(len(arrays))
        if not isinstance(operand, tuple):
            arrays.append(operand)
            specs.append(pl.BlockSpec(memory_space=pltpu.VMEM))
            continue
        parts, first, (start, end) = operand
        moves, at = [], 0
        for part in parts:
            low, high = max(start, at), min(end, at + part.shape[1])
            if low < high:
                moves.append((len(arrays), low - at, low - start, high - low))
                arrays.append(part)
                specs.append(pl.BlockSpec(memory_space=pl.ANY))
            at += part.shape[1]
        windows.append((len(places) - 1, first, end - start, moves))
    n_in, n_out, n_early = len(arrays), len(outs), len(early)
    n_windows, n_copies = len(windows), sum(len(window[3]) for window in windows)
    arrays += early
    specs += [pl.BlockSpec(memory_space=pl.ANY)] * n_early
    held = [pltpu.VMEM((TILE, width), BF) for _, _, width, _ in windows]

    def whole(meta_ref, *refs):
        ins, rest = refs[:n_in], refs[n_in + n_early :]
        given = [ins[place] if place < n_in else None for place in places]
        if not windows:
            kernel(meta_ref, lambda: None, *given, *rest)
            return
        sems = rest[-1]
        slots = rest[-1 - n_windows : -1]
        copies = []
        for slot, (place, first, _, moves) in zip(slots, windows):
            for index, source, target, width in moves:
                source = ins[index].at[pl.ds(first, TILE), pl.ds(source, width)]
                target = slot.at[:, pl.ds(target, width)]
                copies.append(pltpu.make_async_copy(source, target, sems.at[len(copies)]))
                copies[-1].start()
            given[place] = slot

        def ready():
            for copy in copies:
                copy.wait()

        kernel(meta_ref, ready, *given, *rest[: -1 - n_windows])

    extra = held + [pltpu.SemaphoreType.DMA((n_copies,))] if windows else []
    return pl.pallas_call(
        whole,
        out_shape=[jax.ShapeDtypeStruct(shape, dtype) for shape, dtype in outs],
        in_specs=[pl.BlockSpec(memory_space=pltpu.SMEM)] + specs,
        out_specs=[pl.BlockSpec(memory_space=pltpu.VMEM)] * n_out,
        scratch_shapes=[pltpu.VMEM(shape, BF) for shape in scratch] + extra,
        compiler_params=pltpu.CompilerParams(vmem_limit_bytes=VMEM_LIMIT),
        cost_estimate=pl.CostEstimate(
            flops=int(micros * 2e9), bytes_accessed=int(micros * RATE), transcendentals=0
        ),
    )(meta, *arrays)


def place_blocks(*targets):
    moves = [(i, *block) for i, (blocks, _) in enumerate(targets) for block in blocks]
    count = len(moves)

    def kernel(*refs):
        out_refs, sems = refs[count:-1], refs[-1]
        copies = []
        for k, (i, _, (rows, columns), row, column) in enumerate(moves):
            source = refs[k].at[pl.ds(rows[0], rows[1]), pl.ds(columns[0], columns[1])]
            target = out_refs[i].at[pl.ds(row, rows[1]), pl.ds(column, columns[1])]
            copies.append(pltpu.make_async_copy(source, target, sems.at[k]))
            copies[-1].start()
        for copy in copies:
            copy.wait()

    size = sum(math.prod(shape) for _, shape in targets)
    return pl.pallas_call(
        kernel,
        out_shape=[jax.ShapeDtypeStruct(shape, BF) for _, shape in targets],
        in_specs=[pl.BlockSpec(memory_space=pl.ANY)] * count,
        out_specs=[pl.BlockSpec(memory_space=pltpu.VMEM)] * len(targets),
        scratch_shapes=[pltpu.SemaphoreType.DMA((count,))],
        compiler_params=pltpu.CompilerParams(vmem_limit_bytes=VMEM_LIMIT),
        cost_estimate=pl.CostEstimate(flops=0, bytes_accessed=4 * size, transcendentals=0),
    )(*[move[1] for move in moves])


def body(frames_in, in_weights, down_weights, gains, cotangent, segment_ids, valid):
    core = lax.axis_index("c")
    yl = lax.axis_index("yl")
    y = 2 * lax.axis_index("yh") + yl
    zi = lax.axis_index("z")
    xi = lax.axis_index("x")
    is_first = core == 0
    is_low = yl == 0

    block = jnp.arange(16, dtype=jnp.int32)

    def offset(k):
        return jnp.where(k == 1, 3, k - k // 2)

    inner, outer = offset(block % 4), offset(block // 4)
    z_of = (zi + jnp.where(is_first, outer, inner)) % 4
    x_of = (xi + jnp.where(is_first, inner, outer)) % 4
    arrived = 4 * z_of + x_of
    chip = jnp.stack([y, yl])

    meta = jnp.concatenate([arrived, chip]).astype(jnp.int32)
    source = 32 * (8 * z_of[:, None] + x_of[:, None])
    source = source + 128 * jnp.stack([core, 1 - core])[None, :]
    source = (source[:, :, None] + jnp.arange(32, dtype=jnp.int32)).reshape(D)
    move = (lax.broadcasted_iota(jnp.int32, (D, D), 0) == source[None, :]).astype(BF)
    move_t = (lax.broadcasted_iota(jnp.int32, (D, D), 1) == source[:, None]).astype(BF)
    picks = unit_picks()

    def frames_to_chip(value):
        one, two = pick(is_first, to_chip(value, 0), to_chip(value, 1))
        return jnp.concatenate([one, two], axis=0)

    def pack_attn(shard):
        return run(
            pack_attn_kernel,
            meta,
            [shard],
            [((32, QKV + D), BF), ((32, QKV), BF)],
            [],
            1.7,
        )

    def attn_blocks(one, two, column):
        one, two = to_chip(one, 0), to_chip(two, 1)
        rows = (0, 32)
        return [
            (one, (rows, (0, ATTN)), 0, column),
            (two, (rows, (0, QKV)), 32, column),
            (one, (rows, (ATTN, HALF)), 32, column + QKV),
        ]

    def pack_ffn(shard, down, marks):
        padding = jnp.zeros((8, D), BF)
        if marks is not None:
            padding = lax.dynamic_update_slice(padding, marks[None], (0, 0))
        down = jnp.concatenate([down, padding], axis=0)
        return run(
            pack_ffn_kernel,
            meta,
            [shard, down, *picks],
            [((32, GATE_UP + 3 * D), BF), ((32, GATE_UP), BF)],
            [],
            4.5,
        )

    def ffn_blocks(one, two):
        one, two = to_chip(one, 0), to_chip(two, 1)
        rows, down, tail = (0, 32), GATE_UP + D, GATE_UP + 2 * D
        return [
            (one, (rows, (0, down)), 0, 0),
            (one, (rows, (tail, HALF)), 0, down),
            (two, (rows, (0, GATE_UP)), 32, 0),
            (one, (rows, (down, D)), 32, GATE_UP),
            (one, (rows, (tail + HALF, HALF)), 32, down),
        ]

    def to_owners(block, has_ffn, attn_at, extra):
        low, high, down = (0, 32), (32, 32), GATE_UP + D
        one, two, outs, kernels = [], [], [], []
        if has_ffn:
            one = [
                (block, (low, (0, down)), 0, 0),
                (block, (high, (GATE_UP, D)), 0, down),
                (block, (low, (down, HALF)), 0, down + D),
                (block, (high, (down, HALF)), 0, down + D + HALF),
            ]
            two = [(block, (high, (0, GATE_UP)), 0, 0)]
            outs += [((32, 4 * PAIR), F32), ((96, D), F32)]
        wide, narrow = (GATE_UP + 3 * D, GATE_UP) if has_ffn else (0, 0)
        first, second = wide, narrow
        if attn_at is not None:
            one += [(block, (low, (attn_at, ATTN)), 0, wide)]
            one += [(block, (high, (attn_at + QKV, HALF)), 0, wide + ATTN)]
            two += [(block, (high, (attn_at, QKV)), 0, narrow)]
            wide, narrow = wide + ATTN + HALF, narrow + QKV
            if extra:
                columns = (attn_at + ATTN, extra)
                one.append((block, (low, columns), 0, wide))
                two.append((block, (high, columns), 0, narrow))
                wide, narrow = wide + extra, narrow + extra
            outs += [((32, 4 * D), F32)]
        one, two = place_blocks((one, (32, wide)), (two, (32, narrow)))
        one, two = to_owner(one, 0), to_owner(two, 1)
        sums = plus(one[:, wide - extra :], two[:, narrow - extra :])[:, :4] if extra else None

        def kernel(meta_ref, ready, one_ref, two_ref, *refs):
            if has_ffn:
                pick_refs, refs = refs[:2], refs[2:]
                unpack_ffn_kernel(meta_ref, one_ref, two_ref, pick_refs, refs[0], refs[1])
                refs = refs[2:]
            if attn_at is not None:
                cols = pl.ds(first, ATTN + HALF), pl.ds(second, QKV)
                attn_refs = one_ref.at[:, cols[0]], two_ref.at[:, cols[1]]
                unpack_attn_kernel(meta_ref, *attn_refs, refs[0])

        operands = [one, two, *picks] if has_ffn else [one, two]
        results = list(run(kernel, meta, operands, outs, [], 5.0 if has_ffn else 1.8))
        if has_ffn:
            results[1] = results[1][:88]
        if attn_at is not None:
            results.append(sums)
        return results

    gain_rows = gains[:, 0].transpose(1, 2, 0).reshape(4, D)

    def gain_row(layer, which):
        place = 2 * layer + which
        return gain_all[place : place + 1]

    onehot = segment_ids[:, None] == jnp.arange(LANES, dtype=jnp.int32)[None, :]
    counts = jnp.sum(jnp.where(onehot, valid.astype(F32)[:, None], 0.0), axis=0).astype(BF)
    marks = jnp.stack([segment_ids, valid], axis=1).astype(BF)
    marked = jnp.concatenate([frames_in[:, 0], jnp.pad(marks, ((0, 0), (0, LANES - 2)))], axis=1)

    attn0 = pack_attn(in_weights[:, 0, 0, : 4 * D])
    attn0 = Gather(place_blocks((attn_blocks(*attn0, 0), (64, ATTN)))[0])
    attn0.one()
    later = after(in_weights, attn0.piece)
    ffn0_parts = pack_ffn(later[:, 0, 0, 4 * D :], down_weights[:, 0, 0], None)
    attn0.two(*ffn0_parts)
    attn1_parts = pack_attn(after(later, *ffn0_parts)[:, 0, 1, : 4 * D])
    attn0_three = attn0.three()
    blocks = ffn_blocks(*ffn0_parts)
    blocks += attn_blocks(*after(tuple(attn1_parts), blocks[0][0]), FFN)
    middle0 = Gather(place_blocks((blocks, (64, FFN + ATTN)))[0])
    later = after(in_weights, *attn1_parts)
    ffn1_parts = pack_ffn(later[:, 0, 1, 4 * D :], down_weights[:, 0, 1], counts)
    blocks = ffn_blocks(*after(tuple(ffn1_parts), blocks[-1][0]))
    ffn1 = Gather(place_blocks((blocks, (64, FFN)))[0])
    marked = frames_to_chip(after(marked, blocks[0][0]))
    state = marked[:, :D]
    marks = marked[:, D:]
    gain_all = to_chip(after(gain_rows, blocks[0][0]), 0).astype(F32)
    attn0_four = attn0.four()
    middle0.one()
    middle0.two()
    ffn1.one()
    ffn1_two = ffn1.two()
    ffn1_joined = ffn1.piece
    middle0_three = middle0.three(attn0_four, ffn1_two)
    ffn1.three(middle0_three)
    ffn1.four()

    def windows(gathered, start, end):
        if isinstance(gathered, list):
            return [(parts, 0, (start, end)) for parts in gathered]
        return [((gathered,), k * TILE, (start, end)) for k in range(4)]

    near = [(0, 1), (1, 0), (2, 3), (3, 2)]
    across = [(0, 3), (3, 0), (1, 2), (2, 1)]

    wide = ((TOKENS, D), F32)
    wide16 = ((TOKENS, D), BF)
    turned = ((D, TOKENS), BF)
    row = ((1, D), F32)
    saved = []
    base = None
    for layer in range(LAYERS):
        first = layer == 0
        attn, at = (attn0.blocks, 0) if first else (middle0.blocks, FFN)
        carried = [state] if first else list(base)
        state, turned_a, *blocks = run(
            lambda *refs, first=first: qkv_kernel(first, *refs),
            meta,
            [*carried, gain_row(layer, 0), move, move_t] + windows(attn, at, at + QKV),
            [wide, turned] + [((ROWS, QKV), BF)] * 4,
            [(TOKENS, D), (TOKENS, D), (TOKENS, QKV)],
            7.7,
        )
        blocks = exchange_column(blocks)
        if not first:
            cot = frames_to_chip(after(cotangent[:, 0], blocks[1]))
        mixed = run(
            attend_kernel,
            meta,
            blocks,
            [((ROWS, HALF), BF)] * 4,
            [(POS, ROWS, QKV), (POS, ROWS, HALF)],
            3.0,
        )
        if first:
            middle0.four()
        mixed = exchange_column(mixed)
        turned_o, w_out, partial = run(
            out_kernel,
            meta,
            mixed + windows(attn, at + QKV, at + ATTN),
            [((HALF, TOKENS), BF), ((HALF, D), BF), wide16],
            [(TOKENS, HALF), (HALF, TOKENS)],
            3.6,
        )
        ffn = (middle0 if first else ffn1).blocks
        middle, turned_b, gate, up_part, turned_act, w_down, down_partial, *totals = run(
            lambda *refs, first=first: ffn_kernel(not first, *refs),
            meta,
            [state, partial, other_core(partial), gain_row(layer, 1), move, move_t]
            + windows(ffn, 0, FFN),
            [wide, turned, ((TOKENS, UNITS), F32), ((TOKENS, UNITS), F32)]
            + [((UNITS, TOKENS), BF), ((UNITS, D), BF), wide16]
            + ([] if first else [((1, LANES), F32)]),
            [(TOKENS, D), (TOKENS, D), (TOKENS, UNITS), (UNITS, TOKENS)],
            15.0,
            (ffn1_joined,) if first else (),
        )
        saved.append(
            (state, turned_a, blocks, turned_o, w_out, middle, turned_b, gate, up_part)
            + (turned_act, w_down, attn, at, ffn)
        )
        base = (middle, down_partial, other_core(down_partial))
    totals = totals[0]
    other_totals = other_core(totals)

    def frames_to_owner(value):
        return to_owner(jnp.where(is_first, value[:128], value[128:]), 0)[:, None]

    output = frames_to_owner((base[0] + plus(base[1], base[2])).astype(BF))

    gain_list = [[None, None] for _ in range(LAYERS)]

    down_list = [None] * LAYERS

    def gradient_blocks(width):
        half = width // TILE // 2 * TILE
        return [((TILE, width), BF)] * 3 + [((TILE, half), BF), ((TILE, width - half), BF)]

    for layer in reversed(range(LAYERS)):
        (state, turned_a, blocks, turned_o, w_out, middle, turned_b, gate, up_part) = saved[layer][:9]
        turned_act, w_down, attn, at, ffn = saved[layer][9:]
        last = layer == LAYERS - 1
        carried = [cot, marks, totals, other_totals] if last else list(base)
        results = run(
            lambda *refs, last=last: ffn_backward_kernel(last, *refs),
            meta,
            [*carried, turned_act, turned_b, gate, up_part, w_down, move]
            + windows(ffn, 0, GATE_UP)
            + ([] if last else windows(attn_above, 0, ATTN)),
            [wide]
            + ([] if last else [row])
            + [wide16]
            + gradient_blocks(FFN if last else FFN + ATTN),
            [(TOKENS, D), (TOKENS, GATE_UP), (TOKENS, D)],
            18.0,
            () if last else (middle_above,),
        )
        grad, *results = results
        if not last:
            gain_list[layer + 1][0], *results = results
        partial, *pieces = results
        if last:
            ffn_above = Scatter(*pieces)
            ffn_above.one()
        else:
            ffn_sum = Scatter(*pieces)
            ffn_sum.one()
            ffn_above.three_sums(partial)
            ffn_above.four()
        other = other_core(partial)
        grad, gain_list[layer][1], out_terms, *mixed = run(
            out_backward_kernel,
            meta,
            [grad, partial, other, middle, gain_row(layer, 1), turned_o, w_out],
            [wide, row, ((D, HALF), BF)] + [((ROWS, HALF), BF)] * 4,
            [(TOKENS, D), (TOKENS, HALF)],
            5.8,
        )
        sums = (ffn_above if last else ffn_sum).one_sums(mixed[0])
        mixed = exchange_column(mixed)
        (ffn_above if last else ffn_sum).two()
        grads = run(
            attend_backward_kernel,
            meta,
            [*blocks, *mixed],
            [((ROWS, QKV), BF)] * 4,
            [(POS, ROWS, QKV), (POS, ROWS, HALF), (POS, ROWS, QKV)],
            3.8 if last else 1.14,
            sums,
        )
        own = grads[0]
        grads = exchange_column(grads)
        if last:
            grads[0] = after(own, output)
        partial, *pieces = run(
            lambda *refs, first=not last: qkv_backward_kernel(first, *refs),
            meta,
            [*grads, turned_a, out_terms, move]
            + ([] if last else [move_t, state, gain_list[0][1], *gain_list[1]])
            + windows(attn, at, at + QKV),
            [wide16] + ([((D, ATTN), BF)] if last else gradient_blocks(ATTN_GAINS)),
            [(TOKENS, QKV), (TOKENS, D)],
            10.0 if last else 3,
        )
        if last:
            attn_above = pieces[0]
            middle_above = ffn_above.two_sums()
            ffn_above.three()
        else:
            attn_sum = Scatter(*pieces)
            attn_sum.one()
        base = (grad, partial, other_core(partial), state, gain_row(layer, 0))
    middle = ffn_sum.two_sums()
    ffn_sum.three()
    attn_sum.one_sums()
    attn_sum.two(middle)
    ffn_sum.three_sums()
    ffn_sum.four()
    middle = attn_sum.two_sums()
    attn_sum.three()
    input_grad = run(last_kernel, meta, list(base), [wide16], [], 4.3, (middle,))[0]
    units_above, down_list[1] = to_owners(
        after(ffn_above.four_sums(), partial), True, None, 0
    )
    last_sums = attn_sum.three_sums()
    attn_sum.four()
    both = after(ffn_sum.four_sums(), last_sums)
    units, down_list[0], attn_above, _ = to_owners(both, True, FFN, 0)
    attn, gain_sums = to_owners(attn_sum.four_sums(), False, 0, LANES)
    in_parts = [[attn, units], [attn_above, units_above]]
    in_list = [jnp.concatenate(parts, axis=1) for parts in in_parts]
    in_grads = jnp.stack(in_list, axis=1)[:, None]
    down_grads = jnp.stack(down_list, axis=1)[:, None]

    gains_grad = gain_sums.reshape(32, 1, LAYERS, 2)
    return (output, frames_to_owner(input_grad), in_grads, down_grads, gains_grad)


def solution(mesh):
    parts = Mesh(mesh.devices.reshape(2, 2, 4, 2, 4), ("yh", "c", "z", "yl", "x"))
    dp = ("z", "yl", "x")
    section = ("yh", "c")
    return jax.shard_map(
        body,
        mesh=parts,
        in_specs=(
            P(dp, section, None),
            P(dp, section, None, None),
            P(dp, section, None, None),
            P(None, section, None, None),
            P(dp, section, None),
            P(dp),
            P(dp),
        ),
        out_specs=(
            P(dp, section, None),
            P(dp, section, None),
            P(dp, section, None, None),
            P(dp, section, None, None),
            P(dp, section, None, None),
        ),
        check_vma=False,
    )
```

```python
import math

import jax
import jax.numpy as jnp
import numpy as np
from jax import lax
from jax.experimental import pallas as pl
from jax.experimental.pallas import tpu as pltpu
from jax.sharding import Mesh, PartitionSpec as P

D = 1024
HEAD = 64
LAYERS = 2
POS = 4
NSEG = 16
EPS = 1e-05
COUNT_BOOST = 4.0

HALF = D // 2
UNITS = 1536
TOKENS = 256
ROWS = TOKENS // POS
LANES = 128
TILE = 256

BF = jnp.bfloat16
F32 = jnp.float32

PLANE = ("c", "z", "x")
COLUMN = ("yh", "yl")
FIRST = ("x", "z")
SECOND = ("z", "x")

QKV = 3 * HALF
ATTN = QKV + HALF
GATE_UP = 2 * UNITS
FFN = GATE_UP + D + HALF
ATTN_GAINS = ATTN + LANES
PAIR = 1408


def unit_picks():
    unit = np.arange(768)
    rest = unit - HALF
    source = np.where(
        unit < HALF,
        704 * (unit // 256) + 88 * (unit % 256 // 64) + unit % 64,
        704 * (rest // 128) + 88 * (rest % 128 // 32) + 64 + rest % 32,
    )
    source = np.where((unit >= HALF) & (rest % 32 >= 24), -PAIR, source)
    row = np.arange(PAIR)[:, None]
    return [jnp.asarray(row == (source + 352 * half)[None, :], BF) for half in range(2)]


def ring_pairs(axis_of_core, step):
    pairs = []
    for c in range(2):
        for z in range(4):
            for x in range(4):
                if axis_of_core[c] == "x":
                    target = (c * 4 + z) * 4 + (x + step) % 4
                else:
                    target = (c * 4 + (z + step) % 4) * 4 + x
                pairs.append(((c * 4 + z) * 4 + x, target))
    return pairs


def shift(value, axis_of_core, step):
    return lax.ppermute(value, PLANE, ring_pairs(axis_of_core, step))


def after(value, *others):
    return lax.optimization_barrier((value, others))[0]


class Gather:
    def __init__(self, piece):
        self.piece = piece

    def near(self, axis_of_core, *deps):
        self.piece = after(self.piece, *deps)
        self.left = shift(self.piece, axis_of_core, 1)
        self.right = shift(self.piece, axis_of_core, -1)
        return self.left, self.right

    def far(self, axis_of_core, *deps):
        half = self.piece.shape[1] // 2
        far_a = shift(after(self.left[:, :half], *deps), axis_of_core, 1)
        far_b = shift(after(self.right[:, half:], *deps), axis_of_core, -1)
        self.blocks = [(self.piece,), (self.left,), (self.right,), (far_a, far_b)]
        return far_a, far_b

    def one(self, *deps):
        return self.near(FIRST, *deps)

    def two(self, *deps):
        done = self.far(FIRST, *deps)
        rows, width = self.piece.shape
        half = width // 2
        whole, part = ((0, rows), (0, width)), ((0, rows), (0, half))
        blocks = [(self.piece, whole, 0, 0), (self.left, whole, rows, 0)]
        blocks += [(self.right, whole, 2 * rows, 0)]
        blocks += [(done[0], part, 3 * rows, 0), (done[1], part, 3 * rows, half)]
        self.piece = place_blocks((blocks, (4 * rows, width)))[0]
        return done

    def three(self, *deps):
        return self.near(SECOND, *deps)

    def four(self, *deps):
        return self.far(SECOND, *deps)


def plus(one, two):
    return one.astype(F32) + two.astype(F32)


def add_halves(left, right, far_a, far_b):
    rows, width = right.shape
    half = far_a.shape[1]
    rest = width - half

    def kernel(left_ref, right_ref, a_ref, b_ref, left_out, right_out, held_a, held_b, a_s, b_s, sems):
        first, last = pl.ds(0, half), pl.ds(half, rest)
        loads = [
            pltpu.make_async_copy(right_ref.at[:, first], held_a, sems.at[0]),
            pltpu.make_async_copy(a_ref, a_s, sems.at[1]),
            pltpu.make_async_copy(left_ref.at[:, last], held_b, sems.at[2]),
            pltpu.make_async_copy(b_ref, b_s, sems.at[3]),
        ]
        for copy in loads:
            copy.start()
        stores = []
        for place, (held, other, target) in enumerate(
            ((held_a, a_s, right_out.at[:, first]), (held_b, b_s, left_out.at[:, last]))
        ):
            loads[2 * place].wait()
            loads[2 * place + 1].wait()

            @pl.loop(0, rows // 16)
            def _(step):
                part = pl.ds(pl.multiple_of(step * 16, 16), 16)
                held[part, :] = (held[part, :].astype(F32) + other[part, :].astype(F32)).astype(BF)

            stores.append(pltpu.make_async_copy(held, target, sems.at[4 + place]))
            stores[-1].start()
        for copy in stores:
            copy.wait()

    scratch = [(rows, half), (rows, rest), (rows, half), (rows, rest)]
    return pl.pallas_call(
        kernel,
        out_shape=[jax.ShapeDtypeStruct(left.shape, BF), jax.ShapeDtypeStruct(right.shape, BF)],
        in_specs=[pl.BlockSpec(memory_space=pl.ANY)] * 4,
        out_specs=[pl.BlockSpec(memory_space=pl.ANY)] * 2,
        scratch_shapes=[pltpu.VMEM(shape, BF) for shape in scratch]
        + [pltpu.SemaphoreType.DMA((6,))],
        input_output_aliases={0: 0, 1: 1},
        compiler_params=pltpu.CompilerParams(vmem_limit_bytes=VMEM_LIMIT),
        cost_estimate=pl.CostEstimate(
            flops=0, bytes_accessed=6 * rows * width, transcendentals=0
        ),
    )(left, right, far_a, far_b)


class Scatter:
    def __init__(self, own, left, right, far_a, far_b):
        self.parts = own, left, right, far_a, far_b
        self.half = far_a.shape[1]

    def far(self, axis_of_core, deps):
        far_a, far_b = self.parts[3:]
        far_a = shift(after(far_a, *deps), axis_of_core, 1)
        far_b = shift(after(far_b, *deps), axis_of_core, -1)
        self.got = far_a, far_b
        return self.got

    def far_sums(self, deps):
        own, left, right = self.parts[:3]
        far_a, far_b = after(self.got, *deps)
        left, right = add_halves(left, right, far_a, far_b)
        self.parts = own, left, right
        return left, right

    def near(self, axis_of_core, deps):
        own, left, right = self.parts
        from_left = shift(after(right, *deps), axis_of_core, 1)
        from_right = shift(after(left, *deps), axis_of_core, -1)
        self.got = from_left, from_right
        return self.got

    def near_sums(self, deps):
        from_left, from_right = after(self.got, *deps)
        self.block = (plus(self.parts[0], from_left) + from_right.astype(F32)).astype(BF)
        return self.block

    def one(self, *deps):
        return self.far(SECOND, deps)

    def one_sums(self, *deps):
        return self.far_sums(deps)

    def two(self, *deps):
        return self.near(SECOND, deps)

    def two_sums(self, *deps):
        block = self.near_sums(deps)
        own, left, right, far = [block[k * 64 : (k + 1) * 64] for k in range(4)]
        self.parts = own, left, right, far[:, : self.half], far[:, self.half :]
        return block

    def three(self, *deps):
        return self.far(FIRST, deps)

    def three_sums(self, *deps):
        return self.far_sums(deps)

    def four(self, *deps):
        return self.near(FIRST, deps)

    def four_sums(self, *deps):
        return self.near_sums(deps)


def to_chip(value, place):
    pairs = [(c * 2 + yl, (yl ^ place) * 2 + c) for c in range(2) for yl in range(2)]
    return lax.ppermute(value, ("c", "yl"), pairs)


def to_owner(value, place):
    pairs = [(c * 2 + yl, yl * 2 + (c ^ place)) for c in range(2) for yl in range(2)]
    return lax.ppermute(value, ("c", "yl"), pairs)


def other_core(value):
    return lax.ppermute(value, "c", [(0, 1), (1, 0)])


def pick(flag, one, two):
    return jnp.where(flag, one, two), jnp.where(flag, two, one)


def exchange_column(blocks):
    got = [blocks[0]]
    for k in range(1, POS):
        got.append(lax.ppermute(blocks[k], COLUMN, [(y, y ^ k) for y in range(POS)]))
    return got


def dot(one, two):
    return jnp.dot(one, two, preferred_element_type=F32)


def dot_nt(one, two):
    return lax.dot_general(one, two, (((1,), (1,)), ((), ())), preferred_element_type=F32)


Y, YL = 16, 17


def identity(size):
    row = lax.broadcasted_iota(jnp.int32, (size, size), 0)
    return (row == lax.broadcasted_iota(jnp.int32, (size, size), 1)).astype(F32).astype(BF)


def row_block(step):
    return pl.ds(pl.multiple_of(step * 32, 32), 32)


def lane_tile(step):
    return pl.ds(pl.multiple_of(step * TILE, TILE), TILE)


def chip_rows(meta, k):
    return pl.ds(pl.multiple_of((meta[Y] ^ k) * ROWS, ROWS), ROWS)


def rsqrt_mean(state):
    return lax.rsqrt(jnp.mean(state * state, axis=-1, keepdims=True) + EPS)


def norm_rows(step, state, gain_ref, out_ref):
    out_ref[row_block(step), :] = (state * rsqrt_mean(state) * gain_ref[...]).astype(BF)


def move_rows(a_s, mv_ref, mvt_ref, moved_s, moved_t_ref):
    for j in range(D // TILE):
        cols = slice(j * TILE, (j + 1) * TILE)
        moved_s[:, cols] = dot(a_s[...], mv_ref[:, cols]).astype(BF)
        moved_t_ref[cols, :] = dot_nt(mvt_ref[cols, :], a_s[...]).astype(BF)


def dot_pieces(left_s, pieces, cols):
    total = None
    for k, piece in enumerate(pieces):
        term = dot(left_s[:, k * TILE : (k + 1) * TILE], piece[:, cols])
        total = term if total is None else total + term
    return total


def qkv_kernel(first, meta, ready, *refs):
    if first:
        x_ref, gain_ref, mv_ref, mvt_ref, *refs = refs
    else:
        x_ref, own_ref, other_ref, gain_ref, mv_ref, mvt_ref, *refs = refs
    pieces, refs = refs[:4], refs[4:]
    h_ref, art_ref, *refs = refs
    outs, (a_s, ar_s, qkv_s) = refs[:4], refs[4:]

    @pl.loop(0, TOKENS // 32)
    def _(step):
        state = x_ref[row_block(step), :].astype(F32)
        if not first:
            state = state + own_ref[row_block(step), :].astype(F32)
            state = state + other_ref[row_block(step), :].astype(F32)
        h_ref[row_block(step), :] = state
        norm_rows(step, state, gain_ref, a_s)

    move_rows(a_s, mv_ref, mvt_ref, ar_s, art_ref)
    ready()

    @pl.loop(0, QKV // TILE)
    def _(step):
        qkv_s[:, lane_tile(step)] = dot_pieces(ar_s, pieces, lane_tile(step)).astype(BF)

    for k in range(POS):
        outs[k][...] = qkv_s[chip_rows(meta, k), :]


PAIRS = [(p, r) for p in range(POS) for r in range(p + 1)]


def head_matrix(shape, feature_dim):
    feature = lax.broadcasted_iota(jnp.int32, shape, feature_dim) // HEAD
    head = lax.broadcasted_iota(jnp.int32, shape, 1 - feature_dim)
    return (feature == head).astype(F32).astype(BF)


def head_sums(products):
    ones = head_matrix((HALF, LANES), 0)
    high = products.astype(BF)
    low = (products - high.astype(F32)).astype(BF)
    return dot(high, ones) + dot(low, ones)


def head_spread(values16):
    return dot(values16, head_matrix((LANES, HALF), 1))


def pair_probs(queries, keys):
    products = jnp.concatenate([queries[p] * keys[r] for p, r in PAIRS], axis=0)
    scores = head_sums(products) * (1.0 / math.sqrt(HEAD))
    probs = {}
    for p in range(POS):
        own = [scores[i * ROWS : (i + 1) * ROWS] for i, pair in enumerate(PAIRS) if pair[0] == p]
        peak = own[0]
        for term in own[1:]:
            peak = jnp.maximum(peak, term)
        terms = [jnp.exp(term - peak) for term in own]
        total = terms[0]
        for term in terms[1:]:
            total = total + term
        for r in range(p + 1):
            probs[p, r] = terms[r] / total
    return probs


def split_qkv(meta, blocks, qkv_s):
    for k in range(POS):
        qkv_s[k] = blocks[k][...]
    return [
        [qkv_s[p ^ meta[Y], :, t * HALF : (t + 1) * HALF].astype(F32) for p in range(POS)]
        for t in range(3)
    ]


def attend_kernel(meta, ready, *refs):
    blocks, outs, (qkv_s, out_s) = refs[:4], refs[4:8], refs[8:]
    queries, keys, values = split_qkv(meta, blocks, qkv_s)
    probs = pair_probs(queries, keys)
    spread = head_spread(jnp.concatenate([probs[pair].astype(BF) for pair in PAIRS], axis=0))
    for p in range(POS):
        total = None
        for i, (pp, r) in enumerate(PAIRS):
            if pp == p:
                term = spread[i * ROWS : (i + 1) * ROWS] * values[r]
                total = term if total is None else total + term
        out_s[p ^ meta[Y]] = total.astype(BF)
    for k in range(POS):
        outs[k][...] = out_s[k]


def attend_backward_kernel(meta, ready, *refs):
    blocks, grad_blocks, outs, (qkv_s, grad_s, out_s) = refs[:4], refs[4:8], refs[8:12], refs[12:]
    queries, keys, values = split_qkv(meta, blocks, qkv_s)
    for k in range(POS):
        grad_s[k] = grad_blocks[k][...]
    grads = [grad_s[p ^ meta[Y]].astype(F32) for p in range(POS)]
    probs = pair_probs(queries, keys)
    products = jnp.concatenate([grads[p] * values[r] for p, r in PAIRS], axis=0)
    grad_probs = head_sums(products)
    grad_probs = {pair: grad_probs[i * ROWS : (i + 1) * ROWS] for i, pair in enumerate(PAIRS)}
    grad_scores = []
    for p, r in PAIRS:
        mean = probs[p, 0] * grad_probs[p, 0]
        for other in range(1, p + 1):
            mean = mean + probs[p, other] * grad_probs[p, other]
        grad_scores.append(probs[p, r] * (grad_probs[p, r] - mean) * (1.0 / math.sqrt(HEAD)))
    stacked = jnp.concatenate(grad_scores, axis=0)
    high = stacked.astype(BF)
    low = (stacked - high.astype(F32)).astype(BF)
    spread_scores = head_spread(high) + head_spread(low)
    spread_probs = head_spread(jnp.concatenate([probs[pair].astype(BF) for pair in PAIRS], axis=0))
    grad_q = [None] * POS
    grad_k = [None] * POS
    grad_v = [None] * POS

    def put(totals, place, term):
        totals[place] = term if totals[place] is None else totals[place] + term

    for i, (p, r) in enumerate(PAIRS):
        score = spread_scores[i * ROWS : (i + 1) * ROWS]
        put(grad_q, p, score * keys[r])
        put(grad_k, r, score * queries[p])
        put(grad_v, r, spread_probs[i * ROWS : (i + 1) * ROWS] * grads[p])
    for p in range(POS):
        for t, totals in enumerate((grad_q, grad_k, grad_v)):
            out_s[p ^ meta[Y], :, t * HALF : (t + 1) * HALF] = totals[p].astype(BF)
    for k in range(POS):
        outs[k][...] = out_s[k]


def unpack_rows(meta, pieces, out_ref, start):
    for k in range(16):
        rows = pl.ds(pl.multiple_of(start + meta[k] * 32, 32), 32)
        piece, row = pieces[k // 4], (k % 4) * 64
        out_ref[rows, :HALF] = piece[row : row + 32, :]
        out_ref[rows, HALF:] = piece[row + 32 : row + 64, :]


def transpose_into(source_s, out_s):
    eye = identity(TILE)
    for j in range(source_s.shape[1] // TILE):
        cols = slice(j * TILE, (j + 1) * TILE)
        out_s[cols, :] = dot_nt(eye, source_s[:, cols]).astype(BF)


def out_kernel(meta, ready, *refs):
    blocks, pieces, refs = refs[:4], refs[4:8], refs[8:]
    ort_ref, wo_ref, partial_ref, o_s, ot_s = refs
    for k in range(POS):
        o_s[chip_rows(meta, k), :] = blocks[k][...]
    transpose_into(o_s, ot_s)
    ready()
    unpack_rows(meta, pieces, wo_ref, 0)
    for k in range(16):
        ort_ref[k * 32 : (k + 1) * 32, :] = ot_s[pl.ds(pl.multiple_of(meta[k] * 32, 32), 32), :]
    for j in range(D // TILE):
        cols = slice(j * TILE, (j + 1) * TILE)
        partial_ref[:, cols] = dot(o_s[...], wo_ref[:, cols]).astype(BF)


def ffn_kernel(counting, meta, ready, *refs):
    h_ref, own_ref, other_ref, gain_ref, mv_ref, mvt_ref, *refs = refs
    pieces, refs = refs[:4], refs[4:]
    m_ref, brt_ref, gate_ref, up_ref, actrt_ref, wd_ref, partial_ref, *refs = refs
    if counting:
        total_ref, *refs = refs
    b_s, br_s, act_s, actt_s = refs

    @pl.loop(0, TOKENS // 32)
    def _(step):
        state = h_ref[row_block(step), :] + own_ref[row_block(step), :].astype(F32)
        state = state + other_ref[row_block(step), :].astype(F32)
        m_ref[row_block(step), :] = state
        norm_rows(step, state, gain_ref, b_s)

    move_rows(b_s, mv_ref, mvt_ref, br_s, brt_ref)
    ready()

    @pl.loop(0, UNITS // TILE)
    def _(step):
        cols = lane_tile(step)
        gate = dot_pieces(br_s, pieces, cols)
        gate_ref[:, cols] = gate
        up = dot_pieces(br_s, pieces, lane_tile(step + UNITS // TILE))
        up_ref[:, cols] = up
        act_s[:, cols] = (gate * jax.nn.sigmoid(gate) * up).astype(BF)

    for k in range(16):
        rows = pl.ds(pl.multiple_of(meta[k] * 64, 64), 64)
        wd_ref[rows, :] = pieces[k // 4][
            (k % 4) * 64 : (k % 4 + 1) * 64, GATE_UP : GATE_UP + D
        ]
    unpack_rows(meta, [piece.at[:, pl.ds(GATE_UP + D, HALF)] for piece in pieces], wd_ref, D)
    if counting:
        total = jnp.zeros((1, LANES), F32)
        for k in range(16):
            rows = slice(D + k * 32, D + (k + 1) * 32)
            total = total + wd_ref[rows, :LANES].astype(F32)[24:25]
        total_ref[...] = total
    transpose_into(act_s, actt_s)
    for k in range(16):
        rows = pl.ds(pl.multiple_of(meta[k] * 64, 64), 64)
        actrt_ref[k * 64 : (k + 1) * 64, :] = actt_s[rows, :]
        rows = pl.ds(pl.multiple_of(D + meta[k] * 32, 32), 32)
        actrt_ref[D + k * 32 : D + (k + 1) * 32, :] = actt_s[rows, :]

    @pl.loop(0, D // TILE)
    def _(step):
        cols = lane_tile(step)
        partial_ref[:, cols] = dot(act_s[...], wd_ref[:, cols]).astype(BF)


def norm_backward(base_ref, own_ref, other_ref, state_ref, gain_ref, put):
    def one_block(step, total):
        rows = row_block(step)
        own = own_ref[rows, :].astype(F32)
        grad = own + other_ref[rows, :].astype(F32)
        state = state_ref[rows, :].astype(F32)
        scale = rsqrt_mean(state)
        normed = state * scale
        grad_norm = grad * gain_ref[...]
        mean = jnp.mean(grad_norm * normed, axis=-1, keepdims=True)
        put(rows, base_ref[rows, :] + scale * (grad_norm - normed * mean))
        return total + jnp.sum((own * normed).reshape(4, 8, D), axis=0)

    total = lax.fori_loop(0, TOKENS // 32, one_block, jnp.zeros((8, D), F32))
    return jnp.sum(total, axis=0, keepdims=True)


def put_piece(refs, k, rows, start, value):
    width = value.shape[1]
    if len(refs) == 1:
        refs[0][slice(k * TILE + rows.start, k * TILE + rows.stop), start : start + width] = value
    elif k < 3:
        refs[k][rows, start : start + width] = value
    else:
        half = refs[3].shape[1]
        if start < half:
            refs[3][rows, start : start + width] = value
        else:
            refs[4][rows, start - half : start - half + width] = value


def put_packed(refs, k, start, step, value):
    for i in range(4):
        row = i * 64 + (step // 2) * 32
        put_piece(
            refs, k, slice(row, row + 32), start + (step % 2) * TILE, value[i * 32 : (i + 1) * 32]
        )


def ffn_backward_kernel(last, meta, ready, *refs):
    if last:
        cot_ref, marks_ref, totals_ref, other_totals_ref, *refs = refs
    else:
        base_ref, own_ref, other_ref, state_ref, gain_ref, *refs = refs
    actrt_ref, brt_ref, gate_ref, up_ref, wd_ref, mv_ref, *refs = refs
    held = 4 if last else 8
    pieces, refs = refs[:held], refs[held:]
    g_ref, *refs = refs
    if not last:
        dgain_ref, *refs = refs
    partial_ref, *refs = refs
    outs, (gf_s, dgu_s, dbr_s) = refs[:-3], refs[-3:]
    pieces, above = pieces[:4], pieces[4:]

    def put(rows, value):
        g_ref[rows, :] = value
        gf_s[rows, :] = value.astype(BF)

    if last:

        @pl.loop(0, TOKENS // 32)
        def _(step):
            rows = row_block(step)
            marks = marks_ref[rows, :].astype(F32)
            totals = totals_ref[...] + other_totals_ref[...]
            place = lax.broadcasted_iota(jnp.int32, (32, LANES), 1).astype(F32)
            count = jnp.sum(jnp.where(place == marks[:, :1], totals, 0.0), axis=1, keepdims=True)
            weight = marks[:, 1:2] * (1.0 + COUNT_BOOST / jnp.maximum(count, 1.0))
            put(rows, cot_ref[rows, :].astype(F32) * weight)

    else:
        dgain_ref[...] = norm_backward(base_ref, own_ref, other_ref, state_ref, gain_ref, put)

    @pl.loop(0, UNITS // TILE)
    def _(step):
        cols = lane_tile(step)
        grad_act = dot_nt(gf_s[...], wd_ref[cols, :])
        gate = gate_ref[:, cols]
        sigma = jax.nn.sigmoid(gate)
        grad_up = grad_act * gate * sigma
        grad_gate = grad_act * up_ref[:, cols] * sigma * (1.0 + gate * (1.0 - sigma))
        dgu_s[:, cols] = grad_gate.astype(BF)
        dgu_s[:, lane_tile(step + UNITS // TILE)] = grad_up.astype(BF)

    everything = slice(0, TILE)
    for k in (3, 1, 2, 0):
        rows = slice(k * TILE, (k + 1) * TILE)
        for j in range(GATE_UP // TILE):
            value = dot(brt_ref[rows, :], dgu_s[:, j * TILE : (j + 1) * TILE]).astype(BF)
            put_piece(outs, k, everything, j * TILE, value)
        for j in range(D // TILE):
            value = dot(actrt_ref[rows, :], gf_s[:, j * TILE : (j + 1) * TILE]).astype(BF)
            put_piece(outs, k, everything, GATE_UP + j * TILE, value)
        tail = slice(D + k * 128, D + (k + 1) * 128)
        for j in range(D // TILE):
            value = dot(actrt_ref[tail, :], gf_s[:, j * TILE : (j + 1) * TILE]).astype(BF)
            put_packed(outs, k, GATE_UP + D, j, value)
    ready()
    for k, sums in enumerate(above):
        for j in range(ATTN // TILE):
            put_piece(outs, k, everything, FFN + j * TILE, sums[:, j * TILE : (j + 1) * TILE])
    for k in range(4):
        dbr_s[:, k * TILE : (k + 1) * TILE] = dot_nt(dgu_s[...], pieces[k][...]).astype(BF)
    for j in range(D // TILE):
        cols = slice(j * TILE, (j + 1) * TILE)
        partial_ref[:, cols] = dot_nt(dbr_s[...], mv_ref[cols, :]).astype(BF)


def out_backward_kernel(meta, ready, *refs):
    base_ref, own_ref, other_ref, state_ref, gain_ref, ort_ref, wo_ref, *refs = refs
    gm_ref, dgain_ref, dwo_ref, *refs = refs
    outs, (ga_s, do_s) = refs[:4], refs[4:]

    def put(rows, value):
        gm_ref[rows, :] = value
        ga_s[rows, :] = value.astype(BF)

    dgain_ref[...] = norm_backward(base_ref, own_ref, other_ref, state_ref, gain_ref, put)
    for j in range(HALF // TILE):
        cols = slice(j * TILE, (j + 1) * TILE)
        do_s[:, cols] = dot_nt(ga_s[...], wo_ref[cols, :]).astype(BF)
    for k in range(POS):
        outs[k][...] = do_s[chip_rows(meta, k), :]
    for k in range(4):
        for j in range(D // TILE):
            cols = slice(j * TILE, (j + 1) * TILE)
            value = dot(ort_ref[k * 128 : (k + 1) * 128, :], ga_s[:, cols]).astype(BF)
            for i in range(4):
                row = k * TILE + i * 64 + (j // 2) * 32
                part = slice((j % 2) * TILE, (j % 2 + 1) * TILE)
                dwo_ref[row : row + 32, part] = value[i * 32 : (i + 1) * 32]


def qkv_backward_kernel(first, meta, ready, *refs):
    blocks, refs = refs[:4], refs[4:]
    art_ref, dwo_ref, mv_ref, *refs = refs
    if first:
        mvt_ref, state_ref, *gain_refs = refs[:5]
        refs = refs[5:]
    pieces, refs = refs[:4], refs[4:]
    partial_ref, *refs = refs
    outs, (dqkv_s, dar_s) = refs[:-2], refs[-2:]
    for k in range(POS):
        dqkv_s[chip_rows(meta, k), :] = blocks[k][...]
    ready()
    for k in range(4):
        dar_s[:, k * TILE : (k + 1) * TILE] = dot_nt(dqkv_s[...], pieces[k][...]).astype(BF)
    for j in range(D // TILE):
        cols = slice(j * TILE, (j + 1) * TILE)
        partial_ref[:, cols] = dot_nt(dar_s[...], mv_ref[cols, :]).astype(BF)
    everything = slice(0, TILE)
    if first:
        def one_block(step, total):
            state = state_ref[row_block(step), :]
            term = partial_ref[row_block(step), :].astype(F32) * state * rsqrt_mean(state)
            return total + jnp.sum(term.reshape(4, 8, D), axis=0)

        total = lax.fori_loop(0, TOKENS // 32, one_block, jnp.zeros((8, D), F32))
        grads = [jnp.sum(total, axis=0, keepdims=True)] + [ref[...] for ref in gain_refs]
        grads = jnp.concatenate(grads + [jnp.zeros((LANES - 4, D), F32)], axis=0).astype(BF)
        for k in range(4):
            value = dot_nt(mvt_ref[k * TILE : (k + 1) * TILE, :], grads).astype(BF)
            put_piece(outs, k, everything, ATTN, value)
    for k in (3, 1, 2, 0):
        rows = slice(k * TILE, (k + 1) * TILE)
        for j in range(QKV // TILE):
            value = dot(art_ref[rows, :], dqkv_s[:, j * TILE : (j + 1) * TILE]).astype(BF)
            put_piece(outs, k, everything, j * TILE, value)
        put_piece(outs, k, everything, QKV, dwo_ref[rows, :])


def last_kernel(meta, ready, *refs):
    base_ref, own_ref, other_ref, state_ref, gain_ref, out_ref = refs

    def put(rows, value):
        out_ref[rows, :] = value.astype(BF)

    norm_backward(base_ref, own_ref, other_ref, state_ref, gain_ref, put)


def pack_attn_kernel(meta, ready, *refs):
    shard, one_ref, two_ref = refs
    low = meta[YL] == 0
    for k in range(QKV // LANES):
        first = shard[:, 2 * k * LANES : (2 * k + 1) * LANES]
        second = shard[:, (2 * k + 1) * LANES : (2 * k + 2) * LANES]
        cols = slice(k * LANES, (k + 1) * LANES)
        one_ref[:, cols] = jnp.where(low, first, second)
        two_ref[:, cols] = jnp.where(low, second, first)
    one_ref[:, QKV:] = shard[:, 3 * D :]


def pack_ffn_kernel(meta, ready, *refs):
    shard, down_ref, *picks = refs[:4]
    one_ref, two_ref = refs[4:]
    low = meta[YL] == 0
    parts = jnp.concatenate([shard[:, k * PAIR : (k + 1) * PAIR] for k in range(4)], axis=0)
    first, second = [dot(parts, pick_ref[...]).astype(BF) for pick_ref in picks]
    for ref, value in (
        (one_ref, jnp.where(low, first, second)),
        (two_ref, jnp.where(low, second, first)),
    ):
        for k in range(4):
            rows = slice(k * 32, (k + 1) * 32)
            start = (k // 2) * UNITS + (k % 2) * HALF
            ref[:, start : start + HALF] = value[rows, :HALF]
            start = (k // 2) * UNITS + D + (k % 2) * TILE
            ref[:, start : start + TILE] = value[rows, HALF:]
    for k in range(3):
        one_ref[:, GATE_UP + k * D : GATE_UP + (k + 1) * D] = down_ref[k * 32 : (k + 1) * 32, :]


def unpack_attn_kernel(meta, one_ref, two_ref, out_ref):
    low = meta[YL] == 0
    for k in range(QKV // LANES):
        cols = slice(k * LANES, (k + 1) * LANES)
        first, second = one_ref[:, cols].astype(F32), two_ref[:, cols].astype(F32)
        out_ref[:, 2 * k * LANES : (2 * k + 1) * LANES] = jnp.where(low, first, second)
        out_ref[:, (2 * k + 1) * LANES : (2 * k + 2) * LANES] = jnp.where(low, second, first)
    out_ref[:, 3 * D :] = one_ref[:, QKV : QKV + D].astype(F32)


def unpack_ffn_kernel(meta, one_ref, two_ref, picks, out_ref, down_ref):
    low = meta[YL] == 0
    halves = []
    for ref in (one_ref, two_ref):
        parts = []
        for k in range(4):
            start = (k // 2) * UNITS + (k % 2) * HALF
            main = ref[:, start : start + HALF]
            start = (k // 2) * UNITS + D + (k % 2) * TILE
            parts.append(jnp.concatenate([main, ref[:, start : start + TILE]], axis=1))
        halves.append(jnp.concatenate(parts, axis=0))
    first = jnp.where(low, halves[0], halves[1])
    second = jnp.where(low, halves[1], halves[0])
    total = dot_nt(first, picks[0][...]) + dot_nt(second, picks[1][...])
    for k in range(4):
        out_ref[:, k * PAIR : (k + 1) * PAIR] = total[k * 32 : (k + 1) * 32]
    for k in range(3):
        part = one_ref[:, GATE_UP + k * D : GATE_UP + (k + 1) * D].astype(F32)
        down_ref[k * 32 : (k + 1) * 32, :] = part


RATE = 3.4e6
VMEM_LIMIT = 56 * 1024 * 1024


def run(kernel, meta, operands, outs, scratch, micros, early=()):
    arrays, specs, places, windows = [], [], [], []
    for operand in operands:
        places.append(len(arrays))
        if not isinstance(operand, tuple):
            arrays.append(operand)
            specs.append(pl.BlockSpec(memory_space=pltpu.VMEM))
            continue
        parts, first, (start, end) = operand
        moves, at = [], 0
        for part in parts:
            low, high = max(start, at), min(end, at + part.shape[1])
            if low < high:
                moves.append((len(arrays), low - at, low - start, high - low))
                arrays.append(part)
                specs.append(pl.BlockSpec(memory_space=pl.ANY))
            at += part.shape[1]
        windows.append((len(places) - 1, first, end - start, moves))
    n_in, n_out, n_early = len(arrays), len(outs), len(early)
    n_windows, n_copies = len(windows), sum(len(window[3]) for window in windows)
    arrays += early
    specs += [pl.BlockSpec(memory_space=pl.ANY)] * n_early
    held = [pltpu.VMEM((TILE, width), BF) for _, _, width, _ in windows]

    def whole(meta_ref, *refs):
        ins, rest = refs[:n_in], refs[n_in + n_early :]
        given = [ins[place] if place < n_in else None for place in places]
        if not windows:
            kernel(meta_ref, lambda: None, *given, *rest)
            return
        sems = rest[-1]
        slots = rest[-1 - n_windows : -1]
        copies = []
        for slot, (place, first, _, moves) in zip(slots, windows):
            for index, source, target, width in moves:
                source = ins[index].at[pl.ds(first, TILE), pl.ds(source, width)]
                target = slot.at[:, pl.ds(target, width)]
                copies.append(pltpu.make_async_copy(source, target, sems.at[len(copies)]))
                copies[-1].start()
            given[place] = slot

        def ready():
            for copy in copies:
                copy.wait()

        kernel(meta_ref, ready, *given, *rest[: -1 - n_windows])

    extra = held + [pltpu.SemaphoreType.DMA((n_copies,))] if windows else []
    return pl.pallas_call(
        whole,
        out_shape=[jax.ShapeDtypeStruct(shape, dtype) for shape, dtype in outs],
        in_specs=[pl.BlockSpec(memory_space=pltpu.SMEM)] + specs,
        out_specs=[pl.BlockSpec(memory_space=pltpu.VMEM)] * n_out,
        scratch_shapes=[pltpu.VMEM(shape, BF) for shape in scratch] + extra,
        compiler_params=pltpu.CompilerParams(vmem_limit_bytes=VMEM_LIMIT),
        cost_estimate=pl.CostEstimate(
            flops=int(micros * 2e9), bytes_accessed=int(micros * RATE), transcendentals=0
        ),
    )(meta, *arrays)


def place_blocks(*targets):
    moves = [(i, *block) for i, (blocks, _) in enumerate(targets) for block in blocks]
    count = len(moves)

    def kernel(*refs):
        out_refs, sems = refs[count:-1], refs[-1]
        copies = []
        for k, (i, _, (rows, columns), row, column) in enumerate(moves):
            source = refs[k].at[pl.ds(rows[0], rows[1]), pl.ds(columns[0], columns[1])]
            target = out_refs[i].at[pl.ds(row, rows[1]), pl.ds(column, columns[1])]
            copies.append(pltpu.make_async_copy(source, target, sems.at[k]))
            copies[-1].start()
        for copy in copies:
            copy.wait()

    size = sum(math.prod(shape) for _, shape in targets)
    return pl.pallas_call(
        kernel,
        out_shape=[jax.ShapeDtypeStruct(shape, BF) for _, shape in targets],
        in_specs=[pl.BlockSpec(memory_space=pl.ANY)] * count,
        out_specs=[pl.BlockSpec(memory_space=pltpu.VMEM)] * len(targets),
        scratch_shapes=[pltpu.SemaphoreType.DMA((count,))],
        compiler_params=pltpu.CompilerParams(vmem_limit_bytes=VMEM_LIMIT),
        cost_estimate=pl.CostEstimate(flops=0, bytes_accessed=4 * size, transcendentals=0),
    )(*[move[1] for move in moves])


def body(frames_in, in_weights, down_weights, gains, cotangent, segment_ids, valid):
    core = lax.axis_index("c")
    yl = lax.axis_index("yl")
    y = 2 * lax.axis_index("yh") + yl
    zi = lax.axis_index("z")
    xi = lax.axis_index("x")
    is_first = core == 0
    is_low = yl == 0

    block = jnp.arange(16, dtype=jnp.int32)

    def offset(k):
        return jnp.where(k == 1, 3, k - k // 2)

    inner, outer = offset(block % 4), offset(block // 4)
    z_of = (zi + jnp.where(is_first, outer, inner)) % 4
    x_of = (xi + jnp.where(is_first, inner, outer)) % 4
    arrived = 4 * z_of + x_of
    chip = jnp.stack([y, yl])

    meta = jnp.concatenate([arrived, chip]).astype(jnp.int32)
    source = 32 * (8 * z_of[:, None] + x_of[:, None])
    source = source + 128 * jnp.stack([core, 1 - core])[None, :]
    source = (source[:, :, None] + jnp.arange(32, dtype=jnp.int32)).reshape(D)
    move = (lax.broadcasted_iota(jnp.int32, (D, D), 0) == source[None, :]).astype(BF)
    move_t = (lax.broadcasted_iota(jnp.int32, (D, D), 1) == source[:, None]).astype(BF)
    picks = unit_picks()

    def frames_to_chip(value):
        one, two = pick(is_first, to_chip(value, 0), to_chip(value, 1))
        return jnp.concatenate([one, two], axis=0)

    def pack_attn(shard):
        return run(
            pack_attn_kernel,
            meta,
            [shard],
            [((32, QKV + D), BF), ((32, QKV), BF)],
            [],
            1.7,
        )

    def attn_blocks(one, two, column):
        one, two = to_chip(one, 0), to_chip(two, 1)
        rows = (0, 32)
        return [
            (one, (rows, (0, ATTN)), 0, column),
            (two, (rows, (0, QKV)), 32, column),
            (one, (rows, (ATTN, HALF)), 32, column + QKV),
        ]

    def pack_ffn(shard, down, marks):
        padding = jnp.zeros((8, D), BF)
        if marks is not None:
            padding = lax.dynamic_update_slice(padding, marks[None], (0, 0))
        down = jnp.concatenate([down, padding], axis=0)
        return run(
            pack_ffn_kernel,
            meta,
            [shard, down, *picks],
            [((32, GATE_UP + 3 * D), BF), ((32, GATE_UP), BF)],
            [],
            4.5,
        )

    def ffn_blocks(one, two):
        one, two = to_chip(one, 0), to_chip(two, 1)
        rows, down, tail = (0, 32), GATE_UP + D, GATE_UP + 2 * D
        return [
            (one, (rows, (0, down)), 0, 0),
            (one, (rows, (tail, HALF)), 0, down),
            (two, (rows, (0, GATE_UP)), 32, 0),
            (one, (rows, (down, D)), 32, GATE_UP),
            (one, (rows, (tail + HALF, HALF)), 32, down),
        ]

    def to_owners(block, has_ffn, attn_at, extra):
        low, high, down = (0, 32), (32, 32), GATE_UP + D
        one, two, outs, kernels = [], [], [], []
        if has_ffn:
            one = [
                (block, (low, (0, down)), 0, 0),
                (block, (high, (GATE_UP, D)), 0, down),
                (block, (low, (down, HALF)), 0, down + D),
                (block, (high, (down, HALF)), 0, down + D + HALF),
            ]
            two = [(block, (high, (0, GATE_UP)), 0, 0)]
            outs += [((32, 4 * PAIR), F32), ((96, D), F32)]
        wide, narrow = (GATE_UP + 3 * D, GATE_UP) if has_ffn else (0, 0)
        first, second = wide, narrow
        if attn_at is not None:
            one += [(block, (low, (attn_at, ATTN)), 0, wide)]
            one += [(block, (high, (attn_at + QKV, HALF)), 0, wide + ATTN)]
            two += [(block, (high, (attn_at, QKV)), 0, narrow)]
            wide, narrow = wide + ATTN + HALF, narrow + QKV
            if extra:
                columns = (attn_at + ATTN, extra)
                one.append((block, (low, columns), 0, wide))
                two.append((block, (high, columns), 0, narrow))
                wide, narrow = wide + extra, narrow + extra
            outs += [((32, 4 * D), F32)]
        cut = place_blocks((one, (32, wide)), (two, (32, narrow)))
        one, two = to_owner(cut[0], 0), to_owner(cut[1], 1)
        sums = plus(one[:, wide - extra :], two[:, narrow - extra :])[:, :4] if extra else None

        def kernel(meta_ref, ready, one_ref, two_ref, *refs):
            if has_ffn:
                pick_refs, refs = refs[:2], refs[2:]
                unpack_ffn_kernel(meta_ref, one_ref, two_ref, pick_refs, refs[0], refs[1])
                refs = refs[2:]
            if attn_at is not None:
                cols = pl.ds(first, ATTN + HALF), pl.ds(second, QKV)
                attn_refs = one_ref.at[:, cols[0]], two_ref.at[:, cols[1]]
                unpack_attn_kernel(meta_ref, *attn_refs, refs[0])

        operands = [one, two, *picks] if has_ffn else [one, two]
        results = list(run(kernel, meta, operands, outs, [], 5.0 if has_ffn else 1.8))
        if has_ffn:
            results[1] = results[1][:88]
        if attn_at is not None:
            results.append(sums)
        return results, cut

    gain_rows = gains[:, 0].transpose(1, 2, 0).reshape(4, D)

    def gain_row(layer, which):
        place = 2 * layer + which
        return gain_all[place : place + 1]

    onehot = segment_ids[:, None] == jnp.arange(LANES, dtype=jnp.int32)[None, :]
    counts = jnp.sum(jnp.where(onehot, valid.astype(F32)[:, None], 0.0), axis=0).astype(BF)
    marks = jnp.stack([segment_ids, valid], axis=1).astype(BF)
    marked = jnp.concatenate([frames_in[:, 0], jnp.pad(marks, ((0, 0), (0, LANES - 2)))], axis=1)

    attn0 = pack_attn(in_weights[:, 0, 0, : 4 * D])
    attn0 = Gather(place_blocks((attn_blocks(*attn0, 0), (64, ATTN)))[0])
    attn0.one()
    later = after(in_weights, attn0.piece)
    ffn0_parts = pack_ffn(later[:, 0, 0, 4 * D :], down_weights[:, 0, 0], None)
    attn0.two(*ffn0_parts)
    attn1_parts = pack_attn(after(later, *ffn0_parts)[:, 0, 1, : 4 * D])
    attn0_three = attn0.three()
    blocks = ffn_blocks(*ffn0_parts)
    blocks += attn_blocks(*after(tuple(attn1_parts), blocks[0][0]), FFN)
    middle0 = Gather(place_blocks((blocks, (64, FFN + ATTN)))[0])
    later = after(in_weights, *attn1_parts)
    ffn1_parts = pack_ffn(later[:, 0, 1, 4 * D :], down_weights[:, 0, 1], counts)
    blocks = ffn_blocks(*after(tuple(ffn1_parts), blocks[-1][0]))
    ffn1 = Gather(place_blocks((blocks, (64, FFN)))[0])
    marked = frames_to_chip(after(marked, blocks[0][0]))
    state = marked[:, :D]
    marks = marked[:, D:]
    gain_all = to_chip(after(gain_rows, blocks[0][0]), 0).astype(F32)
    attn0_four = attn0.four()
    middle0.one()
    middle0.two()
    ffn1.one()
    ffn1_two = ffn1.two()
    ffn1_joined = ffn1.piece
    middle0_three = middle0.three(attn0_four, ffn1_two)
    ffn1.three(middle0_three)
    ffn1.four()

    def windows(gathered, start, end):
        if isinstance(gathered, list):
            return [(parts, 0, (start, end)) for parts in gathered]
        return [((gathered,), k * TILE, (start, end)) for k in range(4)]

    near = [(0, 1), (1, 0), (2, 3), (3, 2)]
    across = [(0, 3), (3, 0), (1, 2), (2, 1)]

    wide = ((TOKENS, D), F32)
    wide16 = ((TOKENS, D), BF)
    turned = ((D, TOKENS), BF)
    row = ((1, D), F32)
    saved = []
    base = None
    for layer in range(LAYERS):
        first = layer == 0
        attn, at = (attn0.blocks, 0) if first else (middle0.blocks, FFN)
        carried = [state] if first else list(base)
        state, turned_a, *blocks = run(
            lambda *refs, first=first: qkv_kernel(first, *refs),
            meta,
            [*carried, gain_row(layer, 0), move, move_t] + windows(attn, at, at + QKV),
            [wide, turned] + [((ROWS, QKV), BF)] * 4,
            [(TOKENS, D), (TOKENS, D), (TOKENS, QKV)],
            7.7,
        )
        blocks = exchange_column(blocks)
        if not first:
            cot = frames_to_chip(after(cotangent[:, 0], blocks[1]))
        mixed = run(
            attend_kernel,
            meta,
            blocks,
            [((ROWS, HALF), BF)] * 4,
            [(POS, ROWS, QKV), (POS, ROWS, HALF)],
            3.0,
        )
        if first:
            middle0.four()
        mixed = exchange_column(mixed)
        turned_o, w_out, partial = run(
            out_kernel,
            meta,
            mixed + windows(attn, at + QKV, at + ATTN),
            [((HALF, TOKENS), BF), ((HALF, D), BF), wide16],
            [(TOKENS, HALF), (HALF, TOKENS)],
            3.6,
        )
        ffn = (middle0 if first else ffn1).blocks
        middle, turned_b, gate, up_part, turned_act, w_down, down_partial, *totals = run(
            lambda *refs, first=first: ffn_kernel(not first, *refs),
            meta,
            [state, partial, other_core(partial), gain_row(layer, 1), move, move_t]
            + windows(ffn, 0, FFN),
            [wide, turned, ((TOKENS, UNITS), F32), ((TOKENS, UNITS), F32)]
            + [((UNITS, TOKENS), BF), ((UNITS, D), BF), wide16]
            + ([] if first else [((1, LANES), F32)]),
            [(TOKENS, D), (TOKENS, D), (TOKENS, UNITS), (UNITS, TOKENS)],
            15.0,
            (ffn1_joined,) if first else (),
        )
        saved.append(
            (state, turned_a, blocks, turned_o, w_out, middle, turned_b, gate, up_part)
            + (turned_act, w_down, attn, at, ffn)
        )
        base = (middle, down_partial, other_core(down_partial))
    totals = totals[0]
    other_totals = other_core(totals)

    def frames_to_owner(value):
        return to_owner(jnp.where(is_first, value[:128], value[128:]), 0)[:, None]

    output = frames_to_owner((base[0] + plus(base[1], base[2])).astype(BF))

    gain_list = [[None, None] for _ in range(LAYERS)]

    down_list = [None] * LAYERS

    def gradient_blocks(width):
        half = width // TILE // 2 * TILE
        return [((TILE, width), BF)] * 3 + [((TILE, half), BF), ((TILE, width - half), BF)]

    for layer in reversed(range(LAYERS)):
        (state, turned_a, blocks, turned_o, w_out, middle, turned_b, gate, up_part) = saved[layer][:9]
        turned_act, w_down, attn, at, ffn = saved[layer][9:]
        last = layer == LAYERS - 1
        carried = [cot, marks, totals, other_totals] if last else list(base)
        results = run(
            lambda *refs, last=last: ffn_backward_kernel(last, *refs),
            meta,
            [*carried, turned_act, turned_b, gate, up_part, w_down, move]
            + windows(ffn, 0, GATE_UP)
            + ([] if last else windows(attn_above, 0, ATTN)),
            [wide]
            + ([] if last else [row])
            + [wide16]
            + gradient_blocks(FFN if last else FFN + ATTN),
            [(TOKENS, D), (TOKENS, GATE_UP), (TOKENS, D)],
            18.0,
            () if last else (middle_above,),
        )
        grad, *results = results
        if not last:
            gain_list[layer + 1][0], *results = results
        partial, *pieces = results
        if last:
            ffn_above = Scatter(*pieces)
            ffn_above.one()
        else:
            ffn_sum = Scatter(*pieces)
            ffn_sum.one()
        other = other_core(partial)
        grad, gain_list[layer][1], out_terms, *mixed = run(
            out_backward_kernel,
            meta,
            [grad, partial, other, middle, gain_row(layer, 1), turned_o, w_out],
            [wide, row, ((D, HALF), BF)] + [((ROWS, HALF), BF)] * 4,
            [(TOKENS, D), (TOKENS, HALF)],
            5.8,
        )
        mixed = exchange_column(mixed)
        sums = (ffn_above if last else ffn_sum).one_sums(*mixed[1:])
        (ffn_above if last else ffn_sum).two()
        grads = run(
            attend_backward_kernel,
            meta,
            [*blocks, *mixed],
            [((ROWS, QKV), BF)] * 4,
            [(POS, ROWS, QKV), (POS, ROWS, HALF), (POS, ROWS, QKV)],
            3.8 if last else 1.14,
            sums,
        )
        own = grads[0]
        grads = exchange_column(grads)
        if not last:
            ffn_above.three(*grads)
        if last:
            grads[0] = after(own, output)
        partial, *pieces = run(
            lambda *refs, first=not last: qkv_backward_kernel(first, *refs),
            meta,
            [*grads, turned_a, out_terms, move]
            + ([] if last else [move_t, state, gain_list[0][1], *gain_list[1]])
            + windows(attn, at, at + QKV),
            [wide16] + ([((D, ATTN), BF)] if last else gradient_blocks(ATTN_GAINS)),
            [(TOKENS, QKV), (TOKENS, D)],
            10.0 if last else 3,
        )
        if last:
            attn_above = pieces[0]
            middle_above = ffn_above.two_sums()
        else:
            attn_sum = Scatter(*pieces)
            attn_sum.one()
            ffn_above.three_sums(partial)
            ffn_above.four()
        base = (grad, partial, other_core(partial), state, gain_row(layer, 0))
    ffn_sum.two_sums()
    attn_sum.one_sums()
    attn_sum.two(*ffn_sum.got)
    ffn_sum.three()
    ffn_sum.three_sums()
    ffn_sum.four()
    attn_sum.two_sums()
    attn_sum.three()
    above = after(ffn_above.four_sums(), partial)
    (units_above, down_list[1]), _ = to_owners(above, True, None, 0)
    last_sums = attn_sum.three_sums()
    attn_sum.four()
    both = after(ffn_sum.four_sums(), last_sums)
    (units, down_list[0], attn_above, _), cut = to_owners(both, True, FFN, 0)
    input_grad = run(last_kernel, meta, list(base), [wide16], [], 4.3, cut)[0]
    (attn, gain_sums), _ = to_owners(attn_sum.four_sums(), False, 0, LANES)
    in_parts = [[attn, units], [attn_above, units_above]]
    in_list = [jnp.concatenate(parts, axis=1) for parts in in_parts]
    in_grads = jnp.stack(in_list, axis=1)[:, None]
    down_grads = jnp.stack(down_list, axis=1)[:, None]

    gains_grad = gain_sums.reshape(32, 1, LAYERS, 2)
    return (output, frames_to_owner(input_grad), in_grads, down_grads, gains_grad)


def solution(mesh):
    parts = Mesh(mesh.devices.reshape(2, 2, 4, 2, 4), ("yh", "c", "z", "yl", "x"))
    dp = ("z", "yl", "x")
    section = ("yh", "c")
    return jax.shard_map(
        body,
        mesh=parts,
        in_specs=(
            P(dp, section, None),
            P(dp, section, None, None),
            P(dp, section, None, None),
            P(None, section, None, None),
            P(dp, section, None),
            P(dp),
            P(dp),
        ),
        out_specs=(
            P(dp, section, None),
            P(dp, section, None),
            P(dp, section, None, None),
            P(dp, section, None, None),
            P(dp, section, None, None),
        ),
        check_vma=False,
    )
```

```python
import math

import jax
import jax.numpy as jnp
import numpy as np
from jax import lax
from jax.experimental import pallas as pl
from jax.experimental.pallas import tpu as pltpu
from jax.sharding import Mesh, PartitionSpec as P

D = 1024
HEAD = 64
LAYERS = 2
POS = 4
NSEG = 16
EPS = 1e-05
COUNT_BOOST = 4.0

HALF = D // 2
UNITS = 1536
TOKENS = 256
ROWS = TOKENS // POS
LANES = 128
TILE = 256

BF = jnp.bfloat16
F32 = jnp.float32

PLANE = ("c", "z", "x")
COLUMN = ("yh", "yl")
FIRST = ("x", "z")
SECOND = ("z", "x")

QKV = 3 * HALF
ATTN = QKV + HALF
GATE_UP = 2 * UNITS
FFN = GATE_UP + D + HALF
ATTN_GAINS = ATTN + LANES
PAIR = 1408


def unit_picks():
    unit = np.arange(768)
    rest = unit - HALF
    source = np.where(
        unit < HALF,
        704 * (unit // 256) + 88 * (unit % 256 // 64) + unit % 64,
        704 * (rest // 128) + 88 * (rest % 128 // 32) + 64 + rest % 32,
    )
    source = np.where((unit >= HALF) & (rest % 32 >= 24), -PAIR, source)
    row = np.arange(PAIR)[:, None]
    return [jnp.asarray(row == (source + 352 * half)[None, :], BF) for half in range(2)]


def ring_pairs(axis_of_core, step):
    pairs = []
    for c in range(2):
        for z in range(4):
            for x in range(4):
                if axis_of_core[c] == "x":
                    target = (c * 4 + z) * 4 + (x + step) % 4
                else:
                    target = (c * 4 + (z + step) % 4) * 4 + x
                pairs.append(((c * 4 + z) * 4 + x, target))
    return pairs


def shift(value, axis_of_core, step):
    return lax.ppermute(value, PLANE, ring_pairs(axis_of_core, step))


def after(value, *others):
    return lax.optimization_barrier((value, others))[0]


class Gather:
    def __init__(self, piece):
        self.piece = piece

    def near(self, axis_of_core, *deps):
        self.piece = after(self.piece, *deps)
        self.left = shift(self.piece, axis_of_core, 1)
        self.right = shift(self.piece, axis_of_core, -1)
        return self.left, self.right

    def far(self, axis_of_core, *deps):
        half = self.piece.shape[1] // 2
        far_a = shift(after(self.left[:, :half], *deps), axis_of_core, 1)
        far_b = shift(after(self.right[:, half:], *deps), axis_of_core, -1)
        self.blocks = [(self.piece,), (self.left,), (self.right,), (far_a, far_b)]
        return far_a, far_b

    def one(self, *deps):
        return self.near(FIRST, *deps)

    def two(self, *deps):
        done = self.far(FIRST, *deps)
        rows, width = self.piece.shape
        half = width // 2
        whole, part = ((0, rows), (0, width)), ((0, rows), (0, half))
        blocks = [(self.piece, whole, 0, 0), (self.left, whole, rows, 0)]
        blocks += [(self.right, whole, 2 * rows, 0)]
        blocks += [(done[0], part, 3 * rows, 0), (done[1], part, 3 * rows, half)]
        self.piece = place_blocks((blocks, (4 * rows, width)))[0]
        return done

    def three(self, *deps):
        return self.near(SECOND, *deps)

    def four(self, *deps):
        return self.far(SECOND, *deps)


def plus(one, two):
    return one.astype(F32) + two.astype(F32)


def add_halves(left, right, far_a, far_b):
    rows, width = right.shape
    half = far_a.shape[1]
    rest = width - half

    def kernel(left_ref, right_ref, a_ref, b_ref, left_out, right_out, held_a, held_b, a_s, b_s, sems):
        first, last = pl.ds(0, half), pl.ds(half, rest)
        loads = [
            pltpu.make_async_copy(right_ref.at[:, first], held_a, sems.at[0]),
            pltpu.make_async_copy(a_ref, a_s, sems.at[1]),
            pltpu.make_async_copy(left_ref.at[:, last], held_b, sems.at[2]),
            pltpu.make_async_copy(b_ref, b_s, sems.at[3]),
        ]
        for copy in loads:
            copy.start()
        stores = []
        for place, (held, other, target) in enumerate(
            ((held_a, a_s, right_out.at[:, first]), (held_b, b_s, left_out.at[:, last]))
        ):
            loads[2 * place].wait()
            loads[2 * place + 1].wait()

            @pl.loop(0, rows // 16)
            def _(step):
                part = pl.ds(pl.multiple_of(step * 16, 16), 16)
                held[part, :] = (held[part, :].astype(F32) + other[part, :].astype(F32)).astype(BF)

            stores.append(pltpu.make_async_copy(held, target, sems.at[4 + place]))
            stores[-1].start()
        for copy in stores:
            copy.wait()

    scratch = [(rows, half), (rows, rest), (rows, half), (rows, rest)]
    return pl.pallas_call(
        kernel,
        out_shape=[jax.ShapeDtypeStruct(left.shape, BF), jax.ShapeDtypeStruct(right.shape, BF)],
        in_specs=[pl.BlockSpec(memory_space=pl.ANY)] * 4,
        out_specs=[pl.BlockSpec(memory_space=pl.ANY)] * 2,
        scratch_shapes=[pltpu.VMEM(shape, BF) for shape in scratch]
        + [pltpu.SemaphoreType.DMA((6,))],
        input_output_aliases={0: 0, 1: 1},
        compiler_params=pltpu.CompilerParams(vmem_limit_bytes=VMEM_LIMIT),
        cost_estimate=pl.CostEstimate(
            flops=0, bytes_accessed=6 * rows * width, transcendentals=0
        ),
    )(left, right, far_a, far_b)


class Scatter:
    def __init__(self, own, left, right, far_a, far_b):
        self.parts = own, left, right, far_a, far_b
        self.half = far_a.shape[1]

    def far(self, axis_of_core, deps):
        far_a, far_b = self.parts[3:]
        far_a = shift(after(far_a, *deps), axis_of_core, 1)
        far_b = shift(after(far_b, *deps), axis_of_core, -1)
        self.got = far_a, far_b
        return self.got

    def far_sums(self, deps):
        own, left, right = self.parts[:3]
        far_a, far_b = after(self.got, *deps)
        left, right = add_halves(left, right, far_a, far_b)
        self.parts = own, left, right
        return left, right

    def near(self, axis_of_core, deps):
        own, left, right = self.parts
        from_left = shift(after(right, *deps), axis_of_core, 1)
        from_right = shift(after(left, *deps), axis_of_core, -1)
        self.got = from_left, from_right
        return self.got

    def near_sums(self, deps):
        from_left, from_right = after(self.got, *deps)
        self.block = (plus(self.parts[0], from_left) + from_right.astype(F32)).astype(BF)
        return self.block

    def one(self, *deps):
        return self.far(SECOND, deps)

    def one_sums(self, *deps):
        return self.far_sums(deps)

    def two(self, *deps):
        return self.near(SECOND, deps)

    def two_sums(self, *deps):
        block = self.near_sums(deps)
        own, left, right, far = [block[k * 64 : (k + 1) * 64] for k in range(4)]
        self.parts = own, left, right, far[:, : self.half], far[:, self.half :]
        return block

    def three(self, *deps):
        return self.far(FIRST, deps)

    def three_sums(self, *deps):
        return self.far_sums(deps)

    def four(self, *deps):
        return self.near(FIRST, deps)

    def four_sums(self, *deps):
        return self.near_sums(deps)


def to_chip(value, place):
    pairs = [(c * 2 + yl, (yl ^ place) * 2 + c) for c in range(2) for yl in range(2)]
    return lax.ppermute(value, ("c", "yl"), pairs)


def to_owner(value, place):
    pairs = [(c * 2 + yl, yl * 2 + (c ^ place)) for c in range(2) for yl in range(2)]
    return lax.ppermute(value, ("c", "yl"), pairs)


def other_core(value):
    return lax.ppermute(value, "c", [(0, 1), (1, 0)])


def pick(flag, one, two):
    return jnp.where(flag, one, two), jnp.where(flag, two, one)


def exchange_column(blocks):
    got = [blocks[0]]
    for k in range(1, POS):
        got.append(lax.ppermute(blocks[k], COLUMN, [(y, y ^ k) for y in range(POS)]))
    return got


def dot(one, two):
    return jnp.dot(one, two, preferred_element_type=F32)


def dot_nt(one, two):
    return lax.dot_general(one, two, (((1,), (1,)), ((), ())), preferred_element_type=F32)


Y, YL = 16, 17


def identity(size):
    row = lax.broadcasted_iota(jnp.int32, (size, size), 0)
    return (row == lax.broadcasted_iota(jnp.int32, (size, size), 1)).astype(F32).astype(BF)


def row_block(step):
    return pl.ds(pl.multiple_of(step * 32, 32), 32)


def lane_tile(step):
    return pl.ds(pl.multiple_of(step * TILE, TILE), TILE)


def chip_rows(meta, k):
    return pl.ds(pl.multiple_of((meta[Y] ^ k) * ROWS, ROWS), ROWS)


def rsqrt_mean(state):
    return lax.rsqrt(jnp.mean(state * state, axis=-1, keepdims=True) + EPS)


def norm_rows(step, state, gain_ref, out_ref):
    out_ref[row_block(step), :] = (state * rsqrt_mean(state) * gain_ref[...]).astype(BF)


def move_rows(a_s, mv_ref, mvt_ref, moved_s, moved_t_ref):
    for j in range(D // TILE):
        cols = slice(j * TILE, (j + 1) * TILE)
        moved_s[:, cols] = dot(a_s[...], mv_ref[:, cols]).astype(BF)
        moved_t_ref[cols, :] = dot_nt(mvt_ref[cols, :], a_s[...]).astype(BF)


def dot_pieces(left_s, pieces, cols):
    total = None
    for k, piece in enumerate(pieces):
        term = dot(left_s[:, k * TILE : (k + 1) * TILE], piece[:, cols])
        total = term if total is None else total + term
    return total


def qkv_kernel(first, meta, ready, *refs):
    if first:
        x_ref, gain_ref, mv_ref, mvt_ref, *refs = refs
    else:
        x_ref, own_ref, other_ref, gain_ref, mv_ref, mvt_ref, *refs = refs
    pieces, refs = refs[:4], refs[4:]
    h_ref, art_ref, *refs = refs
    outs, (a_s, ar_s, qkv_s) = refs[:4], refs[4:]

    @pl.loop(0, TOKENS // 32)
    def _(step):
        state = x_ref[row_block(step), :].astype(F32)
        if not first:
            state = state + own_ref[row_block(step), :].astype(F32)
            state = state + other_ref[row_block(step), :].astype(F32)
        h_ref[row_block(step), :] = state
        norm_rows(step, state, gain_ref, a_s)

    move_rows(a_s, mv_ref, mvt_ref, ar_s, art_ref)
    ready()

    @pl.loop(0, QKV // TILE)
    def _(step):
        qkv_s[:, lane_tile(step)] = dot_pieces(ar_s, pieces, lane_tile(step)).astype(BF)

    for k in range(POS):
        outs[k][...] = qkv_s[chip_rows(meta, k), :]


PAIRS = [(p, r) for p in range(POS) for r in range(p + 1)]


def head_matrix(shape, feature_dim):
    feature = lax.broadcasted_iota(jnp.int32, shape, feature_dim) // HEAD
    head = lax.broadcasted_iota(jnp.int32, shape, 1 - feature_dim)
    return (feature == head).astype(F32).astype(BF)


def head_sums(products):
    ones = head_matrix((HALF, LANES), 0)
    high = products.astype(BF)
    low = (products - high.astype(F32)).astype(BF)
    return dot(high, ones) + dot(low, ones)


def head_spread(values16):
    return dot(values16, head_matrix((LANES, HALF), 1))


def pair_probs(queries, keys):
    products = jnp.concatenate([queries[p] * keys[r] for p, r in PAIRS], axis=0)
    scores = head_sums(products) * (1.0 / math.sqrt(HEAD))
    probs = {}
    for p in range(POS):
        own = [scores[i * ROWS : (i + 1) * ROWS] for i, pair in enumerate(PAIRS) if pair[0] == p]
        peak = own[0]
        for term in own[1:]:
            peak = jnp.maximum(peak, term)
        terms = [jnp.exp(term - peak) for term in own]
        total = terms[0]
        for term in terms[1:]:
            total = total + term
        for r in range(p + 1):
            probs[p, r] = terms[r] / total
    return probs


def split_qkv(meta, blocks, qkv_s):
    for k in range(POS):
        qkv_s[k] = blocks[k][...]
    return [
        [qkv_s[p ^ meta[Y], :, t * HALF : (t + 1) * HALF].astype(F32) for p in range(POS)]
        for t in range(3)
    ]


def attend_kernel(meta, ready, *refs):
    blocks, outs, (qkv_s, out_s) = refs[:4], refs[4:8], refs[8:]
    queries, keys, values = split_qkv(meta, blocks, qkv_s)
    probs = pair_probs(queries, keys)
    spread = head_spread(jnp.concatenate([probs[pair].astype(BF) for pair in PAIRS], axis=0))
    for p in range(POS):
        total = None
        for i, (pp, r) in enumerate(PAIRS):
            if pp == p:
                term = spread[i * ROWS : (i + 1) * ROWS] * values[r]
                total = term if total is None else total + term
        out_s[p ^ meta[Y]] = total.astype(BF)
    for k in range(POS):
        outs[k][...] = out_s[k]


def attend_backward_kernel(meta, ready, *refs):
    blocks, grad_blocks, outs, (qkv_s, grad_s, out_s) = refs[:4], refs[4:8], refs[8:12], refs[12:]
    queries, keys, values = split_qkv(meta, blocks, qkv_s)
    for k in range(POS):
        grad_s[k] = grad_blocks[k][...]
    grads = [grad_s[p ^ meta[Y]].astype(F32) for p in range(POS)]
    probs = pair_probs(queries, keys)
    products = jnp.concatenate([grads[p] * values[r] for p, r in PAIRS], axis=0)
    grad_probs = head_sums(products)
    grad_probs = {pair: grad_probs[i * ROWS : (i + 1) * ROWS] for i, pair in enumerate(PAIRS)}
    grad_scores = []
    for p, r in PAIRS:
        mean = probs[p, 0] * grad_probs[p, 0]
        for other in range(1, p + 1):
            mean = mean + probs[p, other] * grad_probs[p, other]
        grad_scores.append(probs[p, r] * (grad_probs[p, r] - mean) * (1.0 / math.sqrt(HEAD)))
    stacked = jnp.concatenate(grad_scores, axis=0)
    high = stacked.astype(BF)
    low = (stacked - high.astype(F32)).astype(BF)
    spread_scores = head_spread(high) + head_spread(low)
    spread_probs = head_spread(jnp.concatenate([probs[pair].astype(BF) for pair in PAIRS], axis=0))
    grad_q = [None] * POS
    grad_k = [None] * POS
    grad_v = [None] * POS

    def put(totals, place, term):
        totals[place] = term if totals[place] is None else totals[place] + term

    for i, (p, r) in enumerate(PAIRS):
        score = spread_scores[i * ROWS : (i + 1) * ROWS]
        put(grad_q, p, score * keys[r])
        put(grad_k, r, score * queries[p])
        put(grad_v, r, spread_probs[i * ROWS : (i + 1) * ROWS] * grads[p])
    for p in range(POS):
        for t, totals in enumerate((grad_q, grad_k, grad_v)):
            out_s[p ^ meta[Y], :, t * HALF : (t + 1) * HALF] = totals[p].astype(BF)
    for k in range(POS):
        outs[k][...] = out_s[k]


def unpack_rows(meta, pieces, out_ref, start):
    for k in range(16):
        rows = pl.ds(pl.multiple_of(start + meta[k] * 32, 32), 32)
        piece, row = pieces[k // 4], (k % 4) * 64
        out_ref[rows, :HALF] = piece[row : row + 32, :]
        out_ref[rows, HALF:] = piece[row + 32 : row + 64, :]


def transpose_into(source_s, out_s):
    eye = identity(TILE)
    for j in range(source_s.shape[1] // TILE):
        cols = slice(j * TILE, (j + 1) * TILE)
        out_s[cols, :] = dot_nt(eye, source_s[:, cols]).astype(BF)


def out_kernel(meta, ready, *refs):
    blocks, pieces, refs = refs[:4], refs[4:8], refs[8:]
    ort_ref, wo_ref, partial_ref, o_s, ot_s = refs
    for k in range(POS):
        o_s[chip_rows(meta, k), :] = blocks[k][...]
    transpose_into(o_s, ot_s)
    ready()
    unpack_rows(meta, pieces, wo_ref, 0)
    for k in range(16):
        ort_ref[k * 32 : (k + 1) * 32, :] = ot_s[pl.ds(pl.multiple_of(meta[k] * 32, 32), 32), :]
    for j in range(D // TILE):
        cols = slice(j * TILE, (j + 1) * TILE)
        partial_ref[:, cols] = dot(o_s[...], wo_ref[:, cols]).astype(BF)


def ffn_kernel(counting, meta, ready, *refs):
    h_ref, own_ref, other_ref, gain_ref, mv_ref, mvt_ref, *refs = refs
    pieces, refs = refs[:4], refs[4:]
    m_ref, brt_ref, gate_ref, up_ref, actrt_ref, wd_ref, partial_ref, *refs = refs
    if counting:
        total_ref, *refs = refs
    b_s, br_s, act_s, actt_s = refs

    @pl.loop(0, TOKENS // 32)
    def _(step):
        state = h_ref[row_block(step), :] + own_ref[row_block(step), :].astype(F32)
        state = state + other_ref[row_block(step), :].astype(F32)
        m_ref[row_block(step), :] = state
        norm_rows(step, state, gain_ref, b_s)

    move_rows(b_s, mv_ref, mvt_ref, br_s, brt_ref)
    ready()

    @pl.loop(0, UNITS // TILE)
    def _(step):
        cols = lane_tile(step)
        gate = dot_pieces(br_s, pieces, cols)
        gate_ref[:, cols] = gate
        up = dot_pieces(br_s, pieces, lane_tile(step + UNITS // TILE))
        up_ref[:, cols] = up
        act_s[:, cols] = (gate * jax.nn.sigmoid(gate) * up).astype(BF)

    for k in range(16):
        rows = pl.ds(pl.multiple_of(meta[k] * 64, 64), 64)
        wd_ref[rows, :] = pieces[k // 4][
            (k % 4) * 64 : (k % 4 + 1) * 64, GATE_UP : GATE_UP + D
        ]
    unpack_rows(meta, [piece.at[:, pl.ds(GATE_UP + D, HALF)] for piece in pieces], wd_ref, D)
    if counting:
        total = jnp.zeros((1, LANES), F32)
        for k in range(16):
            rows = slice(D + k * 32, D + (k + 1) * 32)
            total = total + wd_ref[rows, :LANES].astype(F32)[24:25]
        total_ref[...] = total
    transpose_into(act_s, actt_s)
    for k in range(16):
        rows = pl.ds(pl.multiple_of(meta[k] * 64, 64), 64)
        actrt_ref[k * 64 : (k + 1) * 64, :] = actt_s[rows, :]
        rows = pl.ds(pl.multiple_of(D + meta[k] * 32, 32), 32)
        actrt_ref[D + k * 32 : D + (k + 1) * 32, :] = actt_s[rows, :]

    @pl.loop(0, D // TILE)
    def _(step):
        cols = lane_tile(step)
        partial_ref[:, cols] = dot(act_s[...], wd_ref[:, cols]).astype(BF)


def norm_backward(base_ref, own_ref, other_ref, state_ref, gain_ref, put):
    def one_block(step, total):
        rows = row_block(step)
        own = own_ref[rows, :].astype(F32)
        grad = own + other_ref[rows, :].astype(F32)
        state = state_ref[rows, :].astype(F32)
        scale = rsqrt_mean(state)
        normed = state * scale
        grad_norm = grad * gain_ref[...]
        mean = jnp.mean(grad_norm * normed, axis=-1, keepdims=True)
        put(rows, base_ref[rows, :] + scale * (grad_norm - normed * mean))
        return total + jnp.sum((own * normed).reshape(4, 8, D), axis=0)

    total = lax.fori_loop(0, TOKENS // 32, one_block, jnp.zeros((8, D), F32))
    return jnp.sum(total, axis=0, keepdims=True)


def put_piece(refs, k, rows, start, value):
    width = value.shape[1]
    if len(refs) == 1:
        refs[0][slice(k * TILE + rows.start, k * TILE + rows.stop), start : start + width] = value
    elif k < 3:
        refs[k][rows, start : start + width] = value
    else:
        half = refs[3].shape[1]
        if start < half:
            refs[3][rows, start : start + width] = value
        else:
            refs[4][rows, start - half : start - half + width] = value


def put_packed(refs, k, start, step, value):
    for i in range(4):
        row = i * 64 + (step // 2) * 32
        put_piece(
            refs, k, slice(row, row + 32), start + (step % 2) * TILE, value[i * 32 : (i + 1) * 32]
        )


def ffn_backward_kernel(last, meta, ready, *refs):
    if last:
        cot_ref, marks_ref, totals_ref, other_totals_ref, *refs = refs
    else:
        base_ref, own_ref, other_ref, state_ref, gain_ref, *refs = refs
    actrt_ref, brt_ref, gate_ref, up_ref, wd_ref, mv_ref, *refs = refs
    held = 4 if last else 8
    pieces, refs = refs[:held], refs[held:]
    g_ref, *refs = refs
    if not last:
        dgain_ref, *refs = refs
    partial_ref, *refs = refs
    outs, (gf_s, dgu_s, dbr_s) = refs[:-3], refs[-3:]
    pieces, above = pieces[:4], pieces[4:]

    def put(rows, value):
        g_ref[rows, :] = value
        gf_s[rows, :] = value.astype(BF)

    if last:

        @pl.loop(0, TOKENS // 32)
        def _(step):
            rows = row_block(step)
            marks = marks_ref[rows, :].astype(F32)
            totals = totals_ref[...] + other_totals_ref[...]
            place = lax.broadcasted_iota(jnp.int32, (32, LANES), 1).astype(F32)
            count = jnp.sum(jnp.where(place == marks[:, :1], totals, 0.0), axis=1, keepdims=True)
            weight = marks[:, 1:2] * (1.0 + COUNT_BOOST / jnp.maximum(count, 1.0))
            put(rows, cot_ref[rows, :].astype(F32) * weight)

    else:
        dgain_ref[...] = norm_backward(base_ref, own_ref, other_ref, state_ref, gain_ref, put)

    @pl.loop(0, UNITS // TILE)
    def _(step):
        cols = lane_tile(step)
        grad_act = dot_nt(gf_s[...], wd_ref[cols, :])
        gate = gate_ref[:, cols]
        sigma = jax.nn.sigmoid(gate)
        grad_up = grad_act * gate * sigma
        grad_gate = grad_act * up_ref[:, cols] * sigma * (1.0 + gate * (1.0 - sigma))
        dgu_s[:, cols] = grad_gate.astype(BF)
        dgu_s[:, lane_tile(step + UNITS // TILE)] = grad_up.astype(BF)

    everything = slice(0, TILE)
    for k in (3, 1, 2, 0):
        rows = slice(k * TILE, (k + 1) * TILE)
        for j in range(GATE_UP // TILE):
            value = dot(brt_ref[rows, :], dgu_s[:, j * TILE : (j + 1) * TILE]).astype(BF)
            put_piece(outs, k, everything, j * TILE, value)
        for j in range(D // TILE):
            value = dot(actrt_ref[rows, :], gf_s[:, j * TILE : (j + 1) * TILE]).astype(BF)
            put_piece(outs, k, everything, GATE_UP + j * TILE, value)
        tail = slice(D + k * 128, D + (k + 1) * 128)
        for j in range(D // TILE):
            value = dot(actrt_ref[tail, :], gf_s[:, j * TILE : (j + 1) * TILE]).astype(BF)
            put_packed(outs, k, GATE_UP + D, j, value)
    ready()
    for k, sums in enumerate(above):
        for j in range(ATTN // TILE):
            put_piece(outs, k, everything, FFN + j * TILE, sums[:, j * TILE : (j + 1) * TILE])
    for k in range(4):
        dbr_s[:, k * TILE : (k + 1) * TILE] = dot_nt(dgu_s[...], pieces[k][...]).astype(BF)
    for j in range(D // TILE):
        cols = slice(j * TILE, (j + 1) * TILE)
        partial_ref[:, cols] = dot_nt(dbr_s[...], mv_ref[cols, :]).astype(BF)


def out_backward_kernel(meta, ready, *refs):
    base_ref, own_ref, other_ref, state_ref, gain_ref, ort_ref, wo_ref, *refs = refs
    gm_ref, dgain_ref, dwo_ref, *refs = refs
    outs, (ga_s, do_s) = refs[:4], refs[4:]

    def put(rows, value):
        gm_ref[rows, :] = value
        ga_s[rows, :] = value.astype(BF)

    dgain_ref[...] = norm_backward(base_ref, own_ref, other_ref, state_ref, gain_ref, put)
    for j in range(HALF // TILE):
        cols = slice(j * TILE, (j + 1) * TILE)
        do_s[:, cols] = dot_nt(ga_s[...], wo_ref[cols, :]).astype(BF)
    for k in range(POS):
        outs[k][...] = do_s[chip_rows(meta, k), :]
    for k in range(4):
        for j in range(D // TILE):
            cols = slice(j * TILE, (j + 1) * TILE)
            value = dot(ort_ref[k * 128 : (k + 1) * 128, :], ga_s[:, cols]).astype(BF)
            for i in range(4):
                row = k * TILE + i * 64 + (j // 2) * 32
                part = slice((j % 2) * TILE, (j % 2 + 1) * TILE)
                dwo_ref[row : row + 32, part] = value[i * 32 : (i + 1) * 32]


def qkv_backward_kernel(first, meta, ready, *refs):
    blocks, refs = refs[:4], refs[4:]
    art_ref, dwo_ref, mv_ref, *refs = refs
    if first:
        mvt_ref, state_ref, *gain_refs = refs[:5]
        refs = refs[5:]
    pieces, refs = refs[:4], refs[4:]
    partial_ref, *refs = refs
    outs, (dqkv_s, dar_s) = refs[:-2], refs[-2:]
    for k in range(POS):
        dqkv_s[chip_rows(meta, k), :] = blocks[k][...]
    ready()
    for k in range(4):
        dar_s[:, k * TILE : (k + 1) * TILE] = dot_nt(dqkv_s[...], pieces[k][...]).astype(BF)
    for j in range(D // TILE):
        cols = slice(j * TILE, (j + 1) * TILE)
        partial_ref[:, cols] = dot_nt(dar_s[...], mv_ref[cols, :]).astype(BF)
    everything = slice(0, TILE)
    if first:
        def one_block(step, total):
            state = state_ref[row_block(step), :]
            term = partial_ref[row_block(step), :].astype(F32) * state * rsqrt_mean(state)
            return total + jnp.sum(term.reshape(4, 8, D), axis=0)

        total = lax.fori_loop(0, TOKENS // 32, one_block, jnp.zeros((8, D), F32))
        grads = [jnp.sum(total, axis=0, keepdims=True)] + [ref[...] for ref in gain_refs]
        grads = jnp.concatenate(grads + [jnp.zeros((LANES - 4, D), F32)], axis=0).astype(BF)
        for k in range(4):
            value = dot_nt(mvt_ref[k * TILE : (k + 1) * TILE, :], grads).astype(BF)
            put_piece(outs, k, everything, ATTN, value)
    for k in (3, 1, 2, 0):
        rows = slice(k * TILE, (k + 1) * TILE)
        for j in range(QKV // TILE):
            value = dot(art_ref[rows, :], dqkv_s[:, j * TILE : (j + 1) * TILE]).astype(BF)
            put_piece(outs, k, everything, j * TILE, value)
        put_piece(outs, k, everything, QKV, dwo_ref[rows, :])


def last_kernel(meta, ready, *refs):
    base_ref, own_ref, other_ref, state_ref, gain_ref, out_ref = refs

    def put(rows, value):
        out_ref[rows, :] = value.astype(BF)

    norm_backward(base_ref, own_ref, other_ref, state_ref, gain_ref, put)


def pack_attn_kernel(meta, ready, *refs):
    shard, one_ref, two_ref = refs
    low = meta[YL] == 0
    for k in range(QKV // LANES):
        first = shard[:, 2 * k * LANES : (2 * k + 1) * LANES]
        second = shard[:, (2 * k + 1) * LANES : (2 * k + 2) * LANES]
        cols = slice(k * LANES, (k + 1) * LANES)
        one_ref[:, cols] = jnp.where(low, first, second)
        two_ref[:, cols] = jnp.where(low, second, first)
    one_ref[:, QKV:] = shard[:, 3 * D :]


def pack_ffn_kernel(meta, ready, *refs):
    shard, down_ref, *picks = refs[:4]
    one_ref, two_ref = refs[4:]
    low = meta[YL] == 0
    parts = jnp.concatenate([shard[:, k * PAIR : (k + 1) * PAIR] for k in range(4)], axis=0)
    first, second = [dot(parts, pick_ref[...]).astype(BF) for pick_ref in picks]
    for ref, value in (
        (one_ref, jnp.where(low, first, second)),
        (two_ref, jnp.where(low, second, first)),
    ):
        for k in range(4):
            rows = slice(k * 32, (k + 1) * 32)
            start = (k // 2) * UNITS + (k % 2) * HALF
            ref[:, start : start + HALF] = value[rows, :HALF]
            start = (k // 2) * UNITS + D + (k % 2) * TILE
            ref[:, start : start + TILE] = value[rows, HALF:]
    for k in range(3):
        one_ref[:, GATE_UP + k * D : GATE_UP + (k + 1) * D] = down_ref[k * 32 : (k + 1) * 32, :]


def unpack_attn_kernel(meta, one_ref, two_ref, out_ref):
    low = meta[YL] == 0
    for k in range(QKV // LANES):
        cols = slice(k * LANES, (k + 1) * LANES)
        first, second = one_ref[:, cols].astype(F32), two_ref[:, cols].astype(F32)
        out_ref[:, 2 * k * LANES : (2 * k + 1) * LANES] = jnp.where(low, first, second)
        out_ref[:, (2 * k + 1) * LANES : (2 * k + 2) * LANES] = jnp.where(low, second, first)
    out_ref[:, 3 * D :] = one_ref[:, QKV : QKV + D].astype(F32)


def unpack_ffn_kernel(meta, one_ref, two_ref, picks, out_ref, down_ref):
    low = meta[YL] == 0
    halves = []
    for ref in (one_ref, two_ref):
        parts = []
        for k in range(4):
            start = (k // 2) * UNITS + (k % 2) * HALF
            main = ref[:, start : start + HALF]
            start = (k // 2) * UNITS + D + (k % 2) * TILE
            parts.append(jnp.concatenate([main, ref[:, start : start + TILE]], axis=1))
        halves.append(jnp.concatenate(parts, axis=0))
    first = jnp.where(low, halves[0], halves[1])
    second = jnp.where(low, halves[1], halves[0])
    total = dot_nt(first, picks[0][...]) + dot_nt(second, picks[1][...])
    for k in range(4):
        out_ref[:, k * PAIR : (k + 1) * PAIR] = total[k * 32 : (k + 1) * 32]
    for k in range(3):
        part = one_ref[:, GATE_UP + k * D : GATE_UP + (k + 1) * D].astype(F32)
        down_ref[k * 32 : (k + 1) * 32, :] = part


RATE = 3.4e6
VMEM_LIMIT = 56 * 1024 * 1024


def run(kernel, meta, operands, outs, scratch, micros, early=()):
    arrays, specs, places, windows = [], [], [], []
    for operand in operands:
        places.append(len(arrays))
        if not isinstance(operand, tuple):
            arrays.append(operand)
            specs.append(pl.BlockSpec(memory_space=pltpu.VMEM))
            continue
        parts, first, (start, end) = operand
        moves, at = [], 0
        for part in parts:
            low, high = max(start, at), min(end, at + part.shape[1])
            if low < high:
                moves.append((len(arrays), low - at, low - start, high - low))
                arrays.append(part)
                specs.append(pl.BlockSpec(memory_space=pl.ANY))
            at += part.shape[1]
        windows.append((len(places) - 1, first, end - start, moves))
    n_in, n_out, n_early = len(arrays), len(outs), len(early)
    n_windows, n_copies = len(windows), sum(len(window[3]) for window in windows)
    arrays += early
    specs += [pl.BlockSpec(memory_space=pl.ANY)] * n_early
    held = [pltpu.VMEM((TILE, width), BF) for _, _, width, _ in windows]

    def whole(meta_ref, *refs):
        ins, rest = refs[:n_in], refs[n_in + n_early :]
        given = [ins[place] if place < n_in else None for place in places]
        if not windows:
            kernel(meta_ref, lambda: None, *given, *rest)
            return
        sems = rest[-1]
        slots = rest[-1 - n_windows : -1]
        copies = []
        for slot, (place, first, _, moves) in zip(slots, windows):
            for index, source, target, width in moves:
                source = ins[index].at[pl.ds(first, TILE), pl.ds(source, width)]
                target = slot.at[:, pl.ds(target, width)]
                copies.append(pltpu.make_async_copy(source, target, sems.at[len(copies)]))
                copies[-1].start()
            given[place] = slot

        def ready():
            for copy in copies:
                copy.wait()

        kernel(meta_ref, ready, *given, *rest[: -1 - n_windows])

    extra = held + [pltpu.SemaphoreType.DMA((n_copies,))] if windows else []
    return pl.pallas_call(
        whole,
        out_shape=[jax.ShapeDtypeStruct(shape, dtype) for shape, dtype in outs],
        in_specs=[pl.BlockSpec(memory_space=pltpu.SMEM)] + specs,
        out_specs=[pl.BlockSpec(memory_space=pltpu.VMEM)] * n_out,
        scratch_shapes=[pltpu.VMEM(shape, BF) for shape in scratch] + extra,
        compiler_params=pltpu.CompilerParams(vmem_limit_bytes=VMEM_LIMIT),
        cost_estimate=pl.CostEstimate(
            flops=int(micros * 2e9), bytes_accessed=int(micros * RATE), transcendentals=0
        ),
    )(meta, *arrays)


def place_blocks(*targets):
    moves = [(i, *block) for i, (blocks, _) in enumerate(targets) for block in blocks]
    count = len(moves)

    def kernel(*refs):
        out_refs, sems = refs[count:-1], refs[-1]
        copies = []
        for k, (i, _, (rows, columns), row, column) in enumerate(moves):
            source = refs[k].at[pl.ds(rows[0], rows[1]), pl.ds(columns[0], columns[1])]
            target = out_refs[i].at[pl.ds(row, rows[1]), pl.ds(column, columns[1])]
            copies.append(pltpu.make_async_copy(source, target, sems.at[k]))
            copies[-1].start()
        for copy in copies:
            copy.wait()

    size = sum(math.prod(shape) for _, shape in targets)
    return pl.pallas_call(
        kernel,
        out_shape=[jax.ShapeDtypeStruct(shape, BF) for _, shape in targets],
        in_specs=[pl.BlockSpec(memory_space=pl.ANY)] * count,
        out_specs=[pl.BlockSpec(memory_space=pltpu.VMEM)] * len(targets),
        scratch_shapes=[pltpu.SemaphoreType.DMA((count,))],
        compiler_params=pltpu.CompilerParams(vmem_limit_bytes=VMEM_LIMIT),
        cost_estimate=pl.CostEstimate(flops=0, bytes_accessed=4 * size, transcendentals=0),
    )(*[move[1] for move in moves])


def body(frames_in, in_weights, down_weights, gains, cotangent, segment_ids, valid):
    core = lax.axis_index("c")
    yl = lax.axis_index("yl")
    y = 2 * lax.axis_index("yh") + yl
    zi = lax.axis_index("z")
    xi = lax.axis_index("x")
    is_first = core == 0
    is_low = yl == 0

    block = jnp.arange(16, dtype=jnp.int32)

    def offset(k):
        return jnp.where(k == 1, 3, k - k // 2)

    inner, outer = offset(block % 4), offset(block // 4)
    z_of = (zi + jnp.where(is_first, outer, inner)) % 4
    x_of = (xi + jnp.where(is_first, inner, outer)) % 4
    arrived = 4 * z_of + x_of
    chip = jnp.stack([y, yl])

    meta = jnp.concatenate([arrived, chip]).astype(jnp.int32)
    source = 32 * (8 * z_of[:, None] + x_of[:, None])
    source = source + 128 * jnp.stack([core, 1 - core])[None, :]
    source = (source[:, :, None] + jnp.arange(32, dtype=jnp.int32)).reshape(D)
    move = (lax.broadcasted_iota(jnp.int32, (D, D), 0) == source[None, :]).astype(BF)
    move_t = (lax.broadcasted_iota(jnp.int32, (D, D), 1) == source[:, None]).astype(BF)
    picks = unit_picks()

    def frames_to_chip(value):
        one, two = pick(is_first, to_chip(value, 0), to_chip(value, 1))
        return jnp.concatenate([one, two], axis=0)

    def pack_attn(shard):
        return run(
            pack_attn_kernel,
            meta,
            [shard],
            [((32, QKV + D), BF), ((32, QKV), BF)],
            [],
            1.7,
        )

    def attn_blocks(one, two, column):
        one, two = to_chip(one, 0), to_chip(two, 1)
        rows = (0, 32)
        return [
            (one, (rows, (0, ATTN)), 0, column),
            (two, (rows, (0, QKV)), 32, column),
            (one, (rows, (ATTN, HALF)), 32, column + QKV),
        ]

    def pack_ffn(shard, down, marks):
        padding = jnp.zeros((8, D), BF)
        if marks is not None:
            padding = lax.dynamic_update_slice(padding, marks[None], (0, 0))
        down = jnp.concatenate([down, padding], axis=0)
        return run(
            pack_ffn_kernel,
            meta,
            [shard, down, *picks],
            [((32, GATE_UP + 3 * D), BF), ((32, GATE_UP), BF)],
            [],
            4.5,
        )

    def ffn_blocks(one, two):
        one, two = to_chip(one, 0), to_chip(two, 1)
        rows, down, tail = (0, 32), GATE_UP + D, GATE_UP + 2 * D
        return [
            (one, (rows, (0, down)), 0, 0),
            (one, (rows, (tail, HALF)), 0, down),
            (two, (rows, (0, GATE_UP)), 32, 0),
            (one, (rows, (down, D)), 32, GATE_UP),
            (one, (rows, (tail + HALF, HALF)), 32, down),
        ]

    def to_owners(block, has_ffn, attn_at, extra):
        low, high, down = (0, 32), (32, 32), GATE_UP + D
        one, two, outs, kernels = [], [], [], []
        if has_ffn:
            one = [
                (block, (low, (0, down)), 0, 0),
                (block, (high, (GATE_UP, D)), 0, down),
                (block, (low, (down, HALF)), 0, down + D),
                (block, (high, (down, HALF)), 0, down + D + HALF),
            ]
            two = [(block, (high, (0, GATE_UP)), 0, 0)]
            outs += [((32, 4 * PAIR), F32), ((96, D), F32)]
        wide, narrow = (GATE_UP + 3 * D, GATE_UP) if has_ffn else (0, 0)
        first, second = wide, narrow
        if attn_at is not None:
            one += [(block, (low, (attn_at, ATTN)), 0, wide)]
            one += [(block, (high, (attn_at + QKV, HALF)), 0, wide + ATTN)]
            two += [(block, (high, (attn_at, QKV)), 0, narrow)]
            wide, narrow = wide + ATTN + HALF, narrow + QKV
            if extra:
                columns = (attn_at + ATTN, extra)
                one.append((block, (low, columns), 0, wide))
                two.append((block, (high, columns), 0, narrow))
                wide, narrow = wide + extra, narrow + extra
            outs += [((32, 4 * D), F32)]
        cut = place_blocks((one, (32, wide)), (two, (32, narrow)))
        one, two = to_owner(cut[0], 0), to_owner(cut[1], 1)
        sums = plus(one[:, wide - extra :], two[:, narrow - extra :])[:, :4] if extra else None

        def kernel(meta_ref, ready, one_ref, two_ref, *refs):
            if has_ffn:
                pick_refs, refs = refs[:2], refs[2:]
                unpack_ffn_kernel(meta_ref, one_ref, two_ref, pick_refs, refs[0], refs[1])
                refs = refs[2:]
            if attn_at is not None:
                cols = pl.ds(first, ATTN + HALF), pl.ds(second, QKV)
                attn_refs = one_ref.at[:, cols[0]], two_ref.at[:, cols[1]]
                unpack_attn_kernel(meta_ref, *attn_refs, refs[0])

        operands = [one, two, *picks] if has_ffn else [one, two]
        results = list(run(kernel, meta, operands, outs, [], 5.0 if has_ffn else 1.8))
        if has_ffn:
            results[1] = results[1][:88]
        if attn_at is not None:
            results.append(sums)
        return results, cut

    gain_rows = gains[:, 0].transpose(1, 2, 0).reshape(4, D)

    def gain_row(layer, which):
        place = 2 * layer + which
        return gain_all[place : place + 1]

    onehot = segment_ids[:, None] == jnp.arange(LANES, dtype=jnp.int32)[None, :]
    counts = jnp.sum(jnp.where(onehot, valid.astype(F32)[:, None], 0.0), axis=0).astype(BF)
    marks = jnp.stack([segment_ids, valid], axis=1).astype(BF)
    marked = jnp.concatenate([frames_in[:, 0], jnp.pad(marks, ((0, 0), (0, LANES - 2)))], axis=1)

    attn0 = pack_attn(in_weights[:, 0, 0, : 4 * D])
    attn0 = Gather(place_blocks((attn_blocks(*attn0, 0), (64, ATTN)))[0])
    attn0.one()
    later = after(in_weights, attn0.piece)
    ffn0_parts = pack_ffn(later[:, 0, 0, 4 * D :], down_weights[:, 0, 0], None)
    attn0.two(*ffn0_parts)
    attn1_parts = pack_attn(after(later, *ffn0_parts)[:, 0, 1, : 4 * D])
    attn0_three = attn0.three()
    blocks = ffn_blocks(*ffn0_parts)
    blocks += attn_blocks(*after(tuple(attn1_parts), blocks[0][0]), FFN)
    middle0 = Gather(place_blocks((blocks, (64, FFN + ATTN)))[0])
    later = after(in_weights, *attn1_parts)
    ffn1_parts = pack_ffn(later[:, 0, 1, 4 * D :], down_weights[:, 0, 1], counts)
    blocks = ffn_blocks(*after(tuple(ffn1_parts), blocks[-1][0]))
    ffn1 = Gather(place_blocks((blocks, (64, FFN)))[0])
    marked = frames_to_chip(after(marked, blocks[0][0]))
    state = marked[:, :D]
    marks = marked[:, D:]
    gain_all = to_chip(after(gain_rows, blocks[0][0]), 0).astype(F32)
    attn0_four = attn0.four()
    middle0.one()
    middle0.two()
    ffn1.one()
    ffn1_two = ffn1.two()
    ffn1_joined = ffn1.piece
    middle0_three = middle0.three(attn0_four, ffn1_two)
    ffn1.three(middle0_three)
    ffn1.four()

    def windows(gathered, start, end):
        if isinstance(gathered, list):
            return [(parts, 0, (start, end)) for parts in gathered]
        return [((gathered,), k * TILE, (start, end)) for k in range(4)]

    near = [(0, 1), (1, 0), (2, 3), (3, 2)]
    across = [(0, 3), (3, 0), (1, 2), (2, 1)]

    wide = ((TOKENS, D), F32)
    wide16 = ((TOKENS, D), BF)
    turned = ((D, TOKENS), BF)
    row = ((1, D), F32)
    saved = []
    base = None
    for layer in range(LAYERS):
        first = layer == 0
        attn, at = (attn0.blocks, 0) if first else (middle0.blocks, FFN)
        carried = [state] if first else list(base)
        state, turned_a, *blocks = run(
            lambda *refs, first=first: qkv_kernel(first, *refs),
            meta,
            [*carried, gain_row(layer, 0), move, move_t] + windows(attn, at, at + QKV),
            [wide, turned] + [((ROWS, QKV), BF)] * 4,
            [(TOKENS, D), (TOKENS, D), (TOKENS, QKV)],
            7.7,
        )
        blocks = exchange_column(blocks)
        if not first:
            cot = frames_to_chip(after(cotangent[:, 0], blocks[1]))
        mixed = run(
            attend_kernel,
            meta,
            blocks,
            [((ROWS, HALF), BF)] * 4,
            [(POS, ROWS, QKV), (POS, ROWS, HALF)],
            3.0,
        )
        if first:
            middle0.four()
        mixed = exchange_column(mixed)
        turned_o, w_out, partial = run(
            out_kernel,
            meta,
            mixed + windows(attn, at + QKV, at + ATTN),
            [((HALF, TOKENS), BF), ((HALF, D), BF), wide16],
            [(TOKENS, HALF), (HALF, TOKENS)],
            3.6,
        )
        ffn = (middle0 if first else ffn1).blocks
        middle, turned_b, gate, up_part, turned_act, w_down, down_partial, *totals = run(
            lambda *refs, first=first: ffn_kernel(not first, *refs),
            meta,
            [state, partial, other_core(partial), gain_row(layer, 1), move, move_t]
            + windows(ffn, 0, FFN),
            [wide, turned, ((TOKENS, UNITS), F32), ((TOKENS, UNITS), F32)]
            + [((UNITS, TOKENS), BF), ((UNITS, D), BF), wide16]
            + ([] if first else [((1, LANES), F32)]),
            [(TOKENS, D), (TOKENS, D), (TOKENS, UNITS), (UNITS, TOKENS)],
            15.0,
            (ffn1_joined,) if first else (),
        )
        saved.append(
            (state, turned_a, blocks, turned_o, w_out, middle, turned_b, gate, up_part)
            + (turned_act, w_down, attn, at, ffn)
        )
        base = (middle, down_partial, other_core(down_partial))
    totals = totals[0]
    other_totals = other_core(totals)

    def frames_to_owner(value):
        return to_owner(jnp.where(is_first, value[:128], value[128:]), 0)[:, None]

    output = frames_to_owner((base[0] + plus(base[1], base[2])).astype(BF))

    gain_list = [[None, None] for _ in range(LAYERS)]

    down_list = [None] * LAYERS

    def gradient_blocks(width):
        half = width // TILE // 2 * TILE
        return [((TILE, width), BF)] * 3 + [((TILE, half), BF), ((TILE, width - half), BF)]

    for layer in reversed(range(LAYERS)):
        (state, turned_a, blocks, turned_o, w_out, middle, turned_b, gate, up_part) = saved[layer][:9]
        turned_act, w_down, attn, at, ffn = saved[layer][9:]
        last = layer == LAYERS - 1
        carried = [cot, marks, totals, other_totals] if last else list(base)
        results = run(
            lambda *refs, last=last: ffn_backward_kernel(last, *refs),
            meta,
            [*carried, turned_act, turned_b, gate, up_part, w_down, move]
            + windows(ffn, 0, GATE_UP)
            + ([] if last else windows(attn_above, 0, ATTN)),
            [wide]
            + ([] if last else [row])
            + [wide16]
            + gradient_blocks(FFN if last else FFN + ATTN),
            [(TOKENS, D), (TOKENS, GATE_UP), (TOKENS, D)],
            18.0,
            () if last else (middle_above,),
        )
        grad, *results = results
        if not last:
            gain_list[layer + 1][0], *results = results
        partial, *pieces = results
        if last:
            ffn_above = Scatter(*pieces)
            ffn_above.one()
        else:
            ffn_sum = Scatter(*pieces)
            ffn_sum.one()
        other = other_core(partial)
        grad, gain_list[layer][1], out_terms, *mixed = run(
            out_backward_kernel,
            meta,
            [grad, partial, other, middle, gain_row(layer, 1), turned_o, w_out],
            [wide, row, ((D, HALF), BF)] + [((ROWS, HALF), BF)] * 4,
            [(TOKENS, D), (TOKENS, HALF)],
            5.8,
        )
        mixed = exchange_column(mixed)
        sums = (ffn_above if last else ffn_sum).one_sums(*mixed[1:])
        (ffn_above if last else ffn_sum).two()
        grads = run(
            attend_backward_kernel,
            meta,
            [*blocks, *mixed],
            [((ROWS, QKV), BF)] * 4,
            [(POS, ROWS, QKV), (POS, ROWS, HALF), (POS, ROWS, QKV)],
            3.8 if last else 1.14,
            sums,
        )
        own = grads[0]
        grads = exchange_column(grads)
        if not last:
            ffn_above.three(*grads)
        if last:
            grads[0] = after(own, output)
        partial, *pieces = run(
            lambda *refs, first=not last: qkv_backward_kernel(first, *refs),
            meta,
            [*grads, turned_a, out_terms, move]
            + ([] if last else [move_t, state, gain_list[0][1], *gain_list[1]])
            + windows(attn, at, at + QKV),
            [wide16] + ([((D, ATTN), BF)] if last else gradient_blocks(ATTN_GAINS)),
            [(TOKENS, QKV), (TOKENS, D)],
            10.0 if last else 3,
        )
        if last:
            attn_above = pieces[0]
            middle_above = ffn_above.two_sums()
        else:
            attn_sum = Scatter(*pieces)
            attn_sum.one()
            ffn_above.three_sums(partial)
            ffn_above.four()
        base = (grad, partial, other_core(partial), state, gain_row(layer, 0))
    ffn_sum.two_sums()
    attn_sum.one_sums()
    attn_sum.two(*ffn_sum.got)
    sums = ffn_sum.three()
    ffn_sum.three_sums()
    ffn_sum.four()
    attn_sum.two_sums()
    attn_sum.three()
    above = after(ffn_above.four_sums(), *sums)
    (units_above, down_list[1]), _ = to_owners(above, True, None, 0)
    last_sums = attn_sum.three_sums()
    attn_sum.four()
    both = after(ffn_sum.four_sums(), last_sums)
    (units, down_list[0], attn_above, _), cut = to_owners(both, True, FFN, 0)
    input_grad = run(last_kernel, meta, list(base), [wide16], [], 4.3, cut)[0]
    (attn, gain_sums), _ = to_owners(attn_sum.four_sums(), False, 0, LANES)
    in_parts = [[attn, units], [attn_above, units_above]]
    in_list = [jnp.concatenate(parts, axis=1) for parts in in_parts]
    in_grads = jnp.stack(in_list, axis=1)[:, None]
    down_grads = jnp.stack(down_list, axis=1)[:, None]

    gains_grad = gain_sums.reshape(32, 1, LAYERS, 2)
    return (output, frames_to_owner(input_grad), in_grads, down_grads, gains_grad)


def solution(mesh):
    parts = Mesh(mesh.devices.reshape(2, 2, 4, 2, 4), ("yh", "c", "z", "yl", "x"))
    dp = ("z", "yl", "x")
    section = ("yh", "c")
    return jax.shard_map(
        body,
        mesh=parts,
        in_specs=(
            P(dp, section, None),
            P(dp, section, None, None),
            P(dp, section, None, None),
            P(None, section, None, None),
            P(dp, section, None),
            P(dp),
            P(dp),
        ),
        out_specs=(
            P(dp, section, None),
            P(dp, section, None),
            P(dp, section, None, None),
            P(dp, section, None, None),
            P(dp, section, None, None),
        ),
        check_vma=False,
    )
```
